32 devices in a mesh: sys: 4 (over y, x), edge: 8 (over z, core).
Axes of the slice: x: 2, y: 2, z: 4, core: 2. Of those that a mesh axis runs over, the one named last changes fastest.
Arguments:
- atoms: bfloat16 [4, 512, 896], P('sys', 'edge'), may hold values from -6 to 6
- cotangent: bfloat16 [4, 512, 896], P('sys', 'edge'), may hold values from -6 to 6
- experts: bfloat16 [16, 1792, 896], P('sys', 'edge'), may hold values from -0.125 to 0.125
- radial: bfloat16 [4, 16384, 896], P('sys', 'edge'), may hold values from -6 to 6
- coef: float32 [4, 16], replicated, may hold values from 0.02 to 0.5
- source: int32 [4, 16384], P('sys', 'edge'), may hold values from 0 to 511
- target: int32 [4, 16384], P('sys', 'edge'), may hold values from 0 to 511
Outputs:
- node_out: bfloat16 [4, 512, 896], P('sys', 'edge')
- atom_grad: float32 [4, 512, 896], P('sys', 'edge')
- expert_grad: float32 [16, 1792, 896], P('sys', 'edge')
The draws below stay inside these ranges and needn't reach their ends.
All inputs are finite; a program needn't handle non-finite values.
Results may differ from the reference program's by a relative error of at most 0.018.
Values may be sent and summed in bfloat16 or wider, within the bound.
No kernel may reach another device: no remote copies, remote signals or barrier semaphores. Data moves between devices by JAX's collectives and lax.ppermute only.
A program may use at most 128 MiB of HBM per device.

```python
import math
import jax
import jax.numpy as jnp
from jax import lax

D = 896
DIN = 1792
EXPERTS = 16
EDGES = 16384
ATOMS = 512
SYSTEMS = 4


def place_ends(entries, own_key, low, high):
    longest = entries.shape.index(max(entries.shape))
    spots = []
    for shift in (0, 1):
        where = [jax.random.randint(jax.random.fold_in(own_key, axis), (), 0, length) for axis, length in enumerate(entries.shape)]
        where[longest] = (where[longest] + shift) % entries.shape[longest]
        spots.append(tuple(where))
    return entries.at[spots[0]].set(low).at[spots[1]].set(high)


def shard_levels(key, shape, pieces, low, largest):
    loudness = 1.0
    for position, blocks in pieces:
        heights = jax.random.uniform(jax.random.fold_in(jax.random.fold_in(key, 6), position), (blocks,), jnp.float32, low / len(pieces), largest / len(pieces))
        loudness = loudness * jnp.repeat(jnp.exp(heights), shape[position] // blocks).reshape((-1,) + (1,) * (len(shape) - 1 - position))
    return loudness


def gaussian(stream_key, extent, width, reach, split=(), held_as=jnp.bfloat16):
    entries = jax.random.normal(stream_key, extent, jnp.float32) * width
    if len(split) > 0:
        entries = shard_levels(stream_key, extent, split, -0.22, 0.18) * entries
    return jnp.clip(entries, min=-reach, max=reach).astype(held_as)


def setup_inputs(seed: int = 0) -> dict:
    seeds = jax.random.split(jax.random.key(seed), 8)
    return {
        "atoms": gaussian(seeds[0], (SYSTEMS, ATOMS, D), 1.0, 6.0, ((0, 4), (1, 8))),
        "cotangent": gaussian(seeds[1], (SYSTEMS, ATOMS, D), 1.0, 6.0, ((0, 4), (1, 8))),
        "experts": gaussian(seeds[2], (EXPERTS, DIN, D), DIN ** -0.5, 0.125, ((0, 4), (1, 8))),
        "radial": gaussian(seeds[3], (SYSTEMS, EDGES, D), 1.0, 6.0, ((0, 4), (1, 8))),
        "coef": jnp.clip(jnp.exp(jax.random.uniform(seeds[4], (SYSTEMS, EXPERTS), jnp.float32, math.log(0.02), math.log(0.5))), 0.02, 0.5),
        "source": place_ends(jax.random.randint(seeds[5], (SYSTEMS, EDGES), 0, ATOMS), jax.random.fold_in(seeds[5], 1), 0, ATOMS - 1).astype(jnp.int32),
        "target": place_ends(jax.random.randint(seeds[6], (SYSTEMS, EDGES), 0, ATOMS), jax.random.fold_in(seeds[6], 1), 0, ATOMS - 1).astype(jnp.int32),
    }


def reference(atoms, cotangent, experts, radial, coef, source, target):
    merged_all = jnp.einsum("se,erd->srd", coef.astype(jnp.float32), experts.astype(jnp.float32), precision=lax.Precision.HIGHEST).astype(jnp.bfloat16)
    node_list = []
    grad_list = []
    merged_grads = []
    for sysnum in range(SYSTEMS):
        merged = merged_all[sysnum]
        feats = atoms[sysnum]
        edge_in = jnp.concatenate([jnp.take(feats, source[sysnum], axis=0), jnp.take(feats, target[sysnum], axis=0)], axis=1)
        pre = jnp.dot(edge_in, merged, preferred_element_type=jnp.float32)
        radial_f = radial[sysnum].astype(jnp.float32)
        message = (jax.nn.silu(pre) * radial_f).astype(jnp.bfloat16)
        node_sum = jax.ops.segment_sum(message.astype(jnp.float32), target[sysnum], num_segments=ATOMS)
        node_list.append(node_sum.astype(jnp.bfloat16))
        edge_cot = jnp.take(cotangent[sysnum], target[sysnum], axis=0).astype(jnp.float32)
        sigma = jax.nn.sigmoid(pre)
        slope = sigma * (1.0 + pre * (1.0 - sigma))
        pre_grad = (edge_cot * radial_f * slope).astype(jnp.bfloat16)
        input_grad = lax.dot_general(pre_grad, merged, (((1,), (1,)), ((), ())), preferred_element_type=jnp.float32).astype(jnp.bfloat16)
        first = jax.ops.segment_sum(input_grad[:, :D].astype(jnp.float32), source[sysnum], num_segments=ATOMS)
        second = jax.ops.segment_sum(input_grad[:, D:].astype(jnp.float32), target[sysnum], num_segments=ATOMS)
        grad_list.append(first + second)
        merged_grads.append(lax.dot_general(edge_in, pre_grad, (((0,), (0,)), ((), ())), preferred_element_type=jnp.float32))
    stacked = jnp.stack(merged_grads)
    expert_grad = jnp.einsum("se,srd->erd", coef.astype(jnp.float32), stacked, precision=lax.Precision.HIGHEST)
    return jnp.stack(node_list), jnp.stack(grad_list), expert_grad
```

```python
import functools

import jax
import jax.numpy as jnp
from jax import lax
from jax.experimental import pallas as pl
from jax.experimental.pallas import tpu as pltpu
from jax.sharding import PartitionSpec as P

F32 = jnp.float32
BF16 = jnp.bfloat16
VMEM_LIMIT = 48 << 20
LANES = 128


def whole_vmem():
    return pl.BlockSpec(memory_space=pltpu.VMEM)


def whole_smem():
    return pl.BlockSpec(memory_space=pltpu.SMEM)


def params():
    return pltpu.CompilerParams(vmem_limit_bytes=VMEM_LIMIT)


def merge_kernel(place_ref, coef_ref, experts_ref, *part_refs):
    me = place_ref[0]
    count, rows, _ = experts_ref.shape
    step = 16
    for k, part_ref in enumerate(part_refs):
        scales = [coef_ref[me ^ k, me * count + e] for e in range(count)]

        @pl.loop(0, rows // step)
        def _(i):
            at = pl.ds(pl.multiple_of(i * step, step), step)
            total = scales[0] * experts_ref[0, at, :].astype(F32)
            for e in range(1, count):
                total = total + scales[e] * experts_ref[e, at, :].astype(F32)
            part_ref[at, :] = total.astype(part_ref.dtype)


def merge_parts(place, coef, experts, systems):
    _, rows, width = experts.shape
    return pl.pallas_call(
        merge_kernel,
        out_shape=[
            jax.ShapeDtypeStruct((rows, width), BF16 if k else F32) for k in range(systems)
        ],
        in_specs=[whole_smem(), whole_smem(), whole_vmem()],
        out_specs=[whole_vmem()] * systems,
        compiler_params=params(),
        name="merge_parts",
    )(place, coef, experts)


def expert_kernel(place_ref, coef_ref, *refs):
    me = place_ref[0]
    grad_refs, out_ref = refs[:-1], refs[-1]
    count, rows, _ = out_ref.shape
    step = 16
    scales = [
        [coef_ref[me ^ k, me * count + e] for e in range(count)] for k in range(len(grad_refs))
    ]

    @pl.loop(0, rows // step)
    def _(i):
        at = pl.ds(pl.multiple_of(i * step, step), step)
        grads = [ref[at, :].astype(F32) for ref in grad_refs]
        for e in range(count):
            total = scales[0][e] * grads[0]
            for k in range(1, len(grads)):
                total = total + scales[k][e] * grads[k]
            out_ref[e, at, :] = total


def expert_grads(place, coef, grads, count):
    rows, width = grads[0].shape
    return pl.pallas_call(
        expert_kernel,
        out_shape=jax.ShapeDtypeStruct((count, rows, width), F32),
        in_specs=[whole_smem(), whole_smem()] + [whole_vmem()] * len(grads),
        out_specs=whole_vmem(),
        compiler_params=params(),
        name="expert_grads",
    )(place, coef, *grads)


def edge_kernel(chips, place_ref, cols_ref, rows_ref, radial_ref, atoms_ref, cot_ref, *refs):
    block_refs = refs[: 2 * chips]
    kept_ref, sent_ref, weight_ref, proj_ref, acc_ref = refs[2 * chips :]
    step = pl.program_id(0)
    atoms, width_in = atoms_ref.shape
    tile = radial_ref.shape[0]

    @pl.when(step == 0)
    def _():
        chip, core = place_ref[1], place_ref[2]
        depth = block_refs[0].shape[0]
        for k in range(chips):
            source = lax.rem(chip - k + chips, chips)
            for other in range(2):
                device = 2 * source + (core if other == 0 else 1 - core)
                at = pl.ds(pl.multiple_of(device * depth, depth), depth)
                weight_ref[at, :] = block_refs[2 * k + other][...]
        for half in range(2):
            proj_ref[half * atoms : (half + 1) * atoms, :] = jnp.dot(
                atoms_ref[...],
                weight_ref[half * width_in : (half + 1) * width_in, :],
                preferred_element_type=F32,
            ).astype(BF16)
        acc_ref[...] = jnp.zeros_like(acc_ref)

    def hot(index, shape, axis):
        return jnp.where(index == lax.broadcasted_iota(jnp.int32, shape, axis), 1.0, 0.0).astype(BF16)

    hot_src = hot(cols_ref[:, 0:1], (tile, atoms), 1)
    hot_tgt = hot(cols_ref[:, 1:2], (tile, atoms), 1)
    pre = jnp.dot(hot_src, proj_ref[:atoms, :], preferred_element_type=F32)
    pre = pre + jnp.dot(hot_tgt, proj_ref[atoms:, :], preferred_element_type=F32)
    cot = jnp.dot(hot_tgt, cot_ref[...], preferred_element_type=F32)
    radial = radial_ref[...].astype(F32)
    sigma = 0.5 + 0.5 * jnp.tanh(0.5 * pre)
    silu = pre * sigma
    message = (silu * radial).astype(BF16)
    pre_grad = (cot * radial * (sigma + silu * (1.0 - sigma))).astype(BF16)
    sum_src = hot(rows_ref[0:1, :], (atoms, tile), 0)
    sum_tgt = hot(rows_ref[1:2, :], (atoms, tile), 0)
    acc_ref[0] += jnp.dot(sum_src, pre_grad, preferred_element_type=F32)
    acc_ref[1] += jnp.dot(sum_tgt, pre_grad, preferred_element_type=F32)
    acc_ref[2] += jnp.dot(sum_tgt, message, preferred_element_type=F32)

    @pl.when(step == pl.num_programs(0) - 1)
    def _():
        half = atoms // 2
        kept_ref[...] = acc_ref[:, :half, :]
        sent_ref[...] = acc_ref[:, half:, :].astype(BF16)


def edge_sums(chips, place, cols, rows, radial, atoms, cot, blocks, tile):
    edges = radial.shape[0]
    count, width_in = atoms.shape
    width = blocks[0].shape[1]
    flops = 2 * count * width * (2 * width_in + 6 * edges)
    fixed = lambda *shape: pl.BlockSpec(shape, lambda i: (0,) * len(shape))
    return pl.pallas_call(
        functools.partial(edge_kernel, chips),
        grid=(edges // tile,),
        out_shape=[
            jax.ShapeDtypeStruct((3, count // 2, width), F32),
            jax.ShapeDtypeStruct((3, count // 2, width), BF16),
            jax.ShapeDtypeStruct((2 * width_in, width), BF16),
        ],
        in_specs=[
            whole_smem(),
            pl.BlockSpec((tile, 2), lambda i: (i, 0)),
            pl.BlockSpec((2, tile), lambda i: (0, i)),
            pl.BlockSpec((tile, width), lambda i: (i, 0)),
            fixed(count, width_in),
            fixed(count, width),
        ]
        + [whole_vmem()] * len(blocks),
        out_specs=[
            fixed(3, count // 2, width),
            fixed(3, count // 2, width),
            fixed(2 * width_in, width),
        ],
        scratch_shapes=[
            pltpu.VMEM((2 * count, width), BF16),
            pltpu.VMEM((3, count, width), F32),
        ],
        compiler_params=params(),
        cost_estimate=pl.CostEstimate(
            flops=flops, bytes_accessed=4 * edges * width, transcendentals=edges * width
        ),
        name="edge_sums",
    )(place, cols, rows, radial, atoms, cot, *blocks)


def shards(systems, ways, atoms, cotangent, experts, radial, coef, source, target):
    chips = ways // 2
    me_sys = lax.axis_index("sys")
    me_edge = lax.axis_index("edge")
    chip, core = me_edge // 2, me_edge % 2
    place = jnp.stack([me_sys, chip, core]).astype(jnp.int32)
    count = experts.shape[0]
    width = experts.shape[2]
    own_atoms = atoms.shape[1]

    def across(x, k):
        return lax.ppermute(x, "sys", [(s, s ^ k) for s in range(systems)])

    def swap(x):
        return lax.ppermute(x, "edge", [(e, e ^ 1) for e in range(ways)])

    def shift(x, k):
        return lax.ppermute(x, "edge", [(e, (e + 2 * k) % ways) for e in range(ways)])

    def gather(x):
        got = [x]
        for _ in range(chips - 1):
            got.append(shift(got[-1], 1))
        return got

    parts = merge_parts(place, coef, experts, systems)
    got = [across(parts[k], k) for k in range(1, systems)]

    features = gather(jnp.concatenate([atoms, cotangent], axis=0))
    features = jnp.concatenate(features, axis=1)
    features = jnp.concatenate([features, swap(features)], axis=1)
    all_atoms, all_cot = features[0], features[1]

    def slot(index):
        owner, offset = index // own_atoms, index % own_atoms
        back = (chip - owner // 2 + chips) % chips
        return ((owner % 2) ^ core) * (chips * own_atoms) + back * own_atoms + offset

    ends = jnp.stack([slot(source[0]), slot(target[0])])
    ends_t = ends.T

    total = parts[0]
    for part in got:
        total = total + part.astype(F32)
    blocks = []
    for block in gather(total.astype(BF16)):
        blocks += [block, swap(block)]

    edges = radial.shape[1]
    kept, sent, weight = edge_sums(
        chips, place, ends_t, ends, radial[0], all_atoms, all_cot, blocks, min(512, edges)
    )
    other = swap(sent)

    def part_of(lo, hi, k):
        at = slice(k * own_atoms, (k + 1) * own_atoms)
        return kept[lo:hi, at] + other[lo:hi, at].astype(F32)

    def scatter(lo, hi):
        total = part_of(lo, hi, 1 % chips)
        for t in range(1, chips):
            total = shift(total.astype(BF16), 1).astype(F32) + part_of(lo, hi, (t + 1) % chips)
        return total

    sums = scatter(0, 2).astype(BF16)
    node = scatter(2, 3).astype(BF16)

    def half_for(k):
        return jnp.where((chip + k) % chips < chips // 2, sums[0], sums[1])

    picked = [half_for(0)] + [shift(half_for(k), k) for k in range(1, chips)]
    picked = jnp.concatenate(picked, axis=0)
    picked_other = swap(picked)
    depth = experts.shape[1]
    own_cols = lax.dynamic_slice_in_dim(all_atoms, (me_edge % chips) * depth, depth, 1).T
    half = chips * own_atoms
    merged_grad = jnp.dot(own_cols[:, :half], picked, preferred_element_type=F32)
    merged_grad = merged_grad + jnp.dot(own_cols[:, half:], picked_other, preferred_element_type=F32)
    send = merged_grad.astype(BF16)
    grads = [merged_grad] + [across(send, k) for k in range(1, systems)]
    expert_grad = expert_grads(place, coef, grads, count)

    over = (((1,), (1,)), ((), ()))
    atom_grad = lax.dot_general(sums[0], weight[:width], over, preferred_element_type=F32)
    atom_grad = atom_grad + lax.dot_general(
        sums[1], weight[width:], over, preferred_element_type=F32
    )
    return node, atom_grad[None], expert_grad


def solution(mesh):
    placed = P("sys", "edge", None)
    return jax.shard_map(
        functools.partial(shards, mesh.shape["sys"], mesh.shape["edge"]),
        mesh=mesh,
        in_specs=(placed, placed, placed, placed, P(), P("sys", "edge"), P("sys", "edge")),
        out_specs=(placed, placed, placed),
        check_vma=False,
    )
```

```python
import functools

import jax
import jax.numpy as jnp
from jax import lax
from jax.experimental import pallas as pl
from jax.experimental.pallas import tpu as pltpu
from jax.sharding import PartitionSpec as P

F32 = jnp.float32
BF16 = jnp.bfloat16
VMEM_LIMIT = 48 << 20
LANES = 128
PIECES = 2


def whole_vmem():
    return pl.BlockSpec(memory_space=pltpu.VMEM)


def whole_smem():
    return pl.BlockSpec(memory_space=pltpu.SMEM)


def params():
    return pltpu.CompilerParams(vmem_limit_bytes=VMEM_LIMIT)


def column_chunks(width, pieces):
    tiles = width // LANES
    pieces = max(1, min(pieces, tiles))
    ends = [(tiles * (i + 1) + pieces - 1) // pieces for i in range(pieces)]
    starts = [0] + ends[:-1]
    if tiles * LANES != width:
        return [(0, width)]
    return [(lo * LANES, (hi - lo) * LANES) for lo, hi in zip(starts, ends)]


def merge_kernel(chunks, place_ref, coef_ref, experts_ref, *part_refs):
    me = place_ref[0]
    count, rows, _ = experts_ref.shape
    systems = len(part_refs) // len(chunks)
    step = 16
    scales = [[coef_ref[me ^ k, me * count + e] for e in range(count)] for k in range(systems)]

    @pl.loop(0, rows // step)
    def _(i):
        at = pl.ds(pl.multiple_of(i * step, step), step)
        for j, (lo, size) in enumerate(chunks):
            for col in range(0, size, LANES):
                wide = min(LANES, size - col)
                loaded = [
                    experts_ref[e, at, lo + col : lo + col + wide].astype(F32)
                    for e in range(count)
                ]
                for k in range(systems):
                    total = scales[k][0] * loaded[0]
                    for e in range(1, count):
                        total = total + scales[k][e] * loaded[e]
                    ref = part_refs[j * systems + k]
                    ref[at, col : col + wide] = total.astype(ref.dtype)


def merge_parts(place, coef, experts, systems, chunks):
    count, rows, width = experts.shape
    block = rows // 2 if rows % 32 == 0 else rows
    kinds = [BF16 if k else F32 for _ in chunks for k in range(systems)]
    sizes = [size for _, size in chunks for _ in range(systems)]
    return pl.pallas_call(
        functools.partial(merge_kernel, chunks),
        grid=(rows // block,),
        out_shape=[jax.ShapeDtypeStruct((rows, n), kind) for n, kind in zip(sizes, kinds)],
        in_specs=[
            whole_smem(),
            whole_smem(),
            pl.BlockSpec((count, block, width), lambda i: (0, i, 0)),
        ],
        out_specs=[pl.BlockSpec((block, n), lambda i: (i, 0)) for n in sizes],
        compiler_params=params(),
        name="merge_parts",
    )(place, coef, experts)


def expert_kernel(place_ref, coef_ref, *refs):
    me = place_ref[0]
    out_ref = refs[-1]
    count, rows, _ = out_ref.shape
    systems = coef_ref.shape[0]
    grad_refs = refs[:systems]
    step = 16
    scales = [[coef_ref[me ^ k, me * count + e] for e in range(count)] for k in range(systems)]

    @pl.loop(0, rows // step)
    def _(i):
        at = pl.ds(pl.multiple_of(i * step, step), step)
        grads = [ref[at, :].astype(F32) for ref in grad_refs]
        for e in range(count):
            total = scales[0][e] * grads[0]
            for k in range(1, systems):
                total = total + scales[k][e] * grads[k]
            out_ref[e, at, :] = total


def expert_grads(place, coef, grads, count, width, lo, earlier):
    rows, size = grads[0].shape
    tile = LANES if size % LANES == 0 else size
    extra = [] if earlier is None else [earlier]
    return pl.pallas_call(
        expert_kernel,
        grid=(size // tile,),
        out_shape=jax.ShapeDtypeStruct((count, rows, width), F32),
        in_specs=[whole_smem(), whole_smem()]
        + [pl.BlockSpec((rows, tile), lambda i: (0, i))] * len(grads)
        + [pl.BlockSpec(memory_space=pl.ANY)] * len(extra),
        out_specs=pl.BlockSpec((count, rows, tile), lambda i: (0, 0, lo // tile + i)),
        input_output_aliases={2 + len(grads): 0} if extra else {},
        compiler_params=params(),
        name="expert_grads",
    )(place, coef, *grads, *extra)


def prepare_kernel(chunks, cols_ref, rows_ref, radial_ref, near_ref, far_ref, *refs):
    pieces = len(chunks)
    atoms_ref, gather_ref, sum_ref = refs[:3]
    radial_refs, scaled_refs, cot_ref = refs[3 : 3 + pieces], refs[3 + pieces : -1], refs[-1]
    slots, _, block, _ = near_ref.shape
    atoms = atoms_ref.shape[0]
    tile = radial_ref.shape[0]

    @pl.when(pl.program_id(0) == 0)
    def _():
        for side, ref in enumerate((near_ref, far_ref)):
            for k in range(slots):
                at = slice((side * slots + k) * block, (side * slots + k + 1) * block)
                atoms_ref[at, :] = ref[k, 0]
                cot_ref[at, :] = ref[k, 1]

    def hot(index, shape, axis):
        return jnp.where(index == lax.broadcasted_iota(jnp.int32, shape, axis), 1.0, 0.0).astype(BF16)

    gather_ref[:, :atoms] = hot(cols_ref[:, 0:1], (tile, atoms), 1)
    hot_tgt = hot(cols_ref[:, 1:2], (tile, atoms), 1)
    gather_ref[:, atoms:] = hot_tgt
    sum_ref[:atoms, :] = hot(rows_ref[0:1, :], (atoms, tile), 0)
    sum_ref[atoms:, :] = hot(rows_ref[1:2, :], (atoms, tile), 0)
    for j, (lo, size) in enumerate(chunks):
        at = slice(lo, lo + size)
        cot = jnp.dot(hot_tgt, cot_ref[:, at], preferred_element_type=F32)
        radial_refs[j][...] = radial_ref[:, at]
        scaled_refs[j][...] = (cot * radial_ref[:, at].astype(F32)).astype(BF16)


def prepare(chunks, cols, rows, radial, near, far, tile):
    edges, width = radial.shape
    slots, _, block, _ = near.shape
    atoms = 2 * slots * block
    by_edge = lambda n: pl.BlockSpec((tile, n), lambda i: (i, 0))
    by_column = lambda n: pl.BlockSpec((n, tile), lambda i: (0, i))
    per_chunk = [by_edge(size) for _, size in chunks]
    return pl.pallas_call(
        functools.partial(prepare_kernel, chunks),
        grid=(edges // tile,),
        out_shape=[
            jax.ShapeDtypeStruct((atoms, width), BF16),
            jax.ShapeDtypeStruct((edges, 2 * atoms), BF16),
            jax.ShapeDtypeStruct((2 * atoms, edges), BF16),
        ]
        + [jax.ShapeDtypeStruct((edges, size), BF16) for _ in range(2) for _, size in chunks],
        in_specs=[by_edge(2), by_column(2), by_edge(width), whole_vmem(), whole_vmem()],
        out_specs=[
            pl.BlockSpec((atoms, width), lambda i: (0, 0)),
            by_edge(2 * atoms),
            by_column(2 * atoms),
        ]
        + per_chunk * 2,
        scratch_shapes=[pltpu.VMEM((atoms, width), BF16)],
        compiler_params=params(),
        cost_estimate=pl.CostEstimate(
            flops=2 * atoms * width * edges, bytes_accessed=14 * edges * width, transcendentals=0
        ),
        name="prepare",
    )(cols, rows, radial, near, far)


def edge_kernel(
    place_ref, gather_ref, sum_ref, radial_ref, scaled_ref, atoms_ref, near_ref, far_ref, *refs
):
    kept_ref, sent_ref, node_kept_ref, node_sent_ref, weight_ref, proj_ref, acc_ref = refs
    step = pl.program_id(0)
    atoms, width_in = atoms_ref.shape

    @pl.when(step == 0)
    def _():
        core = place_ref[2]
        chips, depth, _ = near_ref.shape
        for chip in range(chips):
            for ref, parity in ((near_ref, core), (far_ref, 1 - core)):
                at = pl.ds(pl.multiple_of((2 * chip + parity) * depth, depth), depth)
                weight_ref[at, :] = ref[chip]
        for half in range(2):
            proj_ref[half * atoms : (half + 1) * atoms, :] = jnp.dot(
                atoms_ref[...],
                weight_ref[half * width_in : (half + 1) * width_in, :],
                preferred_element_type=F32,
            ).astype(BF16)
        acc_ref[...] = jnp.zeros_like(acc_ref)

    pre = jnp.dot(gather_ref[...], proj_ref[...], preferred_element_type=F32)
    sigma = 0.5 + 0.5 * jnp.tanh(0.5 * pre)
    silu = pre * sigma
    message = (silu * radial_ref[...].astype(F32)).astype(BF16)
    slope = sigma + silu * (1.0 - sigma)
    pre_grad = (scaled_ref[...].astype(F32) * slope).astype(BF16)
    acc_ref[0] += jnp.dot(sum_ref[:atoms, :], pre_grad, preferred_element_type=F32)
    acc_ref[1] += jnp.dot(sum_ref[atoms:, :], pre_grad, preferred_element_type=F32)
    acc_ref[2] += jnp.dot(sum_ref[atoms:, :], message, preferred_element_type=F32)

    @pl.when(step == pl.num_programs(0) - 1)
    def _():
        half = atoms // 2
        kept_ref[...] = acc_ref[:2, :half, :]
        sent_ref[...] = acc_ref[:2, half:, :].astype(BF16)
        node_kept_ref[...] = acc_ref[2, :half, :]
        node_sent_ref[...] = acc_ref[2, half:, :].astype(BF16)


def edge_sums(place, gather, sums, radial, scaled, atoms, near, far, tile):
    edges, width = radial.shape
    count, width_in = atoms.shape
    flops = 2 * count * width * (2 * width_in + 5 * edges)
    fixed = lambda *shape: pl.BlockSpec(shape, lambda i: (0,) * len(shape))
    outs = [
        ((2, count // 2, width), F32),
        ((2, count // 2, width), BF16),
        ((count // 2, width), F32),
        ((count // 2, width), BF16),
        ((2 * width_in, width), BF16),
    ]
    return pl.pallas_call(
        edge_kernel,
        grid=(edges // tile,),
        out_shape=[jax.ShapeDtypeStruct(shape, kind) for shape, kind in outs],
        in_specs=[
            whole_smem(),
            pl.BlockSpec((tile, 2 * count), lambda i: (i, 0)),
            pl.BlockSpec((2 * count, tile), lambda i: (0, i)),
            pl.BlockSpec((tile, width), lambda i: (i, 0)),
            pl.BlockSpec((tile, width), lambda i: (i, 0)),
            fixed(count, width_in),
            whole_vmem(),
            whole_vmem(),
        ],
        out_specs=[fixed(*shape) for shape, _ in outs],
        scratch_shapes=[
            pltpu.VMEM((2 * count, width), BF16),
            pltpu.VMEM((3, count, width), F32),
        ],
        compiler_params=params(),
        cost_estimate=pl.CostEstimate(
            flops=flops,
            bytes_accessed=4 * edges * width + 8 * edges * count,
            transcendentals=edges * width,
        ),
        name="edge_sums",
    )(place, gather, sums, radial, scaled, atoms, near, far)


def after(x, *others):
    return lax.optimization_barrier((x, *others))[0]


def shards(systems, ways, pieces, atoms, cotangent, experts, radial, coef, source, target):
    chips = ways // 2
    me_sys = lax.axis_index("sys")
    me_edge = lax.axis_index("edge")
    chip, core = me_edge // 2, me_edge % 2
    place = jnp.stack([me_sys, chip, core]).astype(jnp.int32)
    count, depth, width = experts.shape
    own = atoms.shape[1]
    edges = radial.shape[1]
    tile = min(512, edges)
    chunks = column_chunks(width, pieces)
    lines = [[2 * z + c for z in range(chips)] for c in range(2)]

    def across(x, k):
        return lax.ppermute(x, "sys", [(s, s ^ k) for s in range(systems)])

    def swap(x):
        return lax.ppermute(x, "edge", [(e, e ^ 1) for e in range(ways)])

    def shift(x, k):
        return lax.ppermute(x, "edge", [(e, (e + 2 * k) % ways) for e in range(ways)])

    features = jnp.concatenate([atoms, cotangent], axis=0)
    near = jnp.stack([features] + [shift(features, k) for k in range(1, chips)])
    far = swap(near)

    def slot(index):
        owner, offset = index // own, index % own
        back = (chip - owner // 2 + chips) % chips
        return ((owner % 2) ^ core) * (chips * own) + back * own + offset

    ends = jnp.stack([slot(source[0]), slot(target[0])])
    prepared = prepare(chunks, ends.T, ends, radial[0], near, far, tile)
    all_atoms, hot_gather, hot_sum = prepared[:3]
    radials, scaled = prepared[3 : 3 + len(chunks)], prepared[3 + len(chunks) :]
    own_cols = lax.dynamic_slice_in_dim(all_atoms, (me_edge % chips) * depth, depth, 1).T

    parts = merge_parts(place, coef, experts, systems, chunks)
    weights = []
    for j in range(len(chunks)):
        total = parts[j * systems]
        got = [across(parts[j * systems + k], k) for k in range(1, systems)]
        for part in got:
            total = total + part.astype(F32)
        block = lax.all_gather(total.astype(BF16), "edge", axis_index_groups=lines)
        weights.append((block, swap(block)))

    def slots(kept, other):
        return [
            kept[..., k * own : (k + 1) * own, :]
            + other[..., k * own : (k + 1) * own, :].astype(F32)
            for k in range(chips)
        ]

    def scatter(blocks):
        total = blocks[0]
        for k in range(1, chips):
            total = total + shift(blocks[k].astype(BF16), chips - k).astype(F32)
        return total

    atom_grad, expert_grad, nodes = None, None, []
    over = (((1,), (1,)), ((), ()))
    half = chips * own
    for j, (lo, size) in enumerate(chunks):
        kept, sent, node_kept, node_sent, weight = edge_sums(
            place, hot_gather, hot_sum, radials[j], scaled[j], all_atoms, *weights[j], tile
        )
        sums = scatter(slots(kept, swap(sent))).astype(BF16)
        nodes.append(slots(node_kept, swap(node_sent)))

        def half_for(k):
            return jnp.where((chip + k) % chips < chips // 2, sums[0], sums[1])

        picked = [half_for(0)] + [shift(half_for(k), k) for k in range(1, chips)]
        picked = jnp.concatenate(picked, axis=0)
        picked_other = swap(picked)
        grad = jnp.dot(own_cols[:, :half], picked, preferred_element_type=F32)
        grad = grad + jnp.dot(own_cols[:, half:], picked_other, preferred_element_type=F32)
        send = grad.astype(BF16)
        grads = [grad] + [across(send, k) for k in range(1, systems)]
        expert_grad = expert_grads(place, coef, grads, count, width, lo, expert_grad)
        for i in range(2):
            part = lax.dot_general(
                sums[i], weight[i * width : (i + 1) * width], over, preferred_element_type=F32
            )
            atom_grad = part if atom_grad is None else atom_grad + part

    blocks = [jnp.concatenate(list(x), axis=1) for x in zip(*nodes)]
    blocks = [blocks[0]] + [after(x.astype(BF16), picked) for x in blocks[1:]]
    node = scatter(blocks).astype(BF16)
    return node[None], atom_grad[None], expert_grad


def solution(mesh):
    placed = P("sys", "edge", None)
    return jax.shard_map(
        functools.partial(shards, mesh.shape["sys"], mesh.shape["edge"], PIECES),
        mesh=mesh,
        in_specs=(placed, placed, placed, placed, P(), P("sys", "edge"), P("sys", "edge")),
        out_specs=(placed, placed, placed),
        check_vma=False,
    )
```

```python
import functools

import jax
import jax.numpy as jnp
from jax import lax
from jax.experimental import pallas as pl
from jax.experimental.pallas import tpu as pltpu
from jax.sharding import PartitionSpec as P

F32 = jnp.float32
BF16 = jnp.bfloat16
VMEM_LIMIT = 48 << 20
LANES = 128
PIECES = 1


def whole_vmem():
    return pl.BlockSpec(memory_space=pltpu.VMEM)


def whole_smem():
    return pl.BlockSpec(memory_space=pltpu.SMEM)


def params():
    return pltpu.CompilerParams(vmem_limit_bytes=VMEM_LIMIT)


def column_chunks(width, pieces):
    tiles = width // LANES
    pieces = max(1, min(pieces, tiles))
    ends = [(tiles * (i + 1) + pieces - 1) // pieces for i in range(pieces)]
    starts = [0] + ends[:-1]
    if tiles * LANES != width:
        return [(0, width)]
    return [(lo * LANES, (hi - lo) * LANES) for lo, hi in zip(starts, ends)]


def merge_kernel(chunks, place_ref, coef_ref, experts_ref, *part_refs):
    me = place_ref[0]
    count, rows, _ = experts_ref.shape
    systems = len(part_refs) // len(chunks)
    step = 16
    scales = [[coef_ref[me ^ k, me * count + e] for e in range(count)] for k in range(systems)]

    @pl.loop(0, rows // step)
    def _(i):
        at = pl.ds(pl.multiple_of(i * step, step), step)
        for j, (lo, size) in enumerate(chunks):
            for col in range(0, size, LANES):
                wide = min(LANES, size - col)
                loaded = [
                    experts_ref[e, at, lo + col : lo + col + wide].astype(F32)
                    for e in range(count)
                ]
                for k in range(systems):
                    total = scales[k][0] * loaded[0]
                    for e in range(1, count):
                        total = total + scales[k][e] * loaded[e]
                    ref = part_refs[j * systems + k]
                    ref[at, col : col + wide] = total.astype(ref.dtype)


def merge_parts(place, coef, experts, systems, chunks):
    count, rows, width = experts.shape
    block = rows // 2 if rows % 32 == 0 else rows
    kinds = [BF16 if k else F32 for _ in chunks for k in range(systems)]
    sizes = [size for _, size in chunks for _ in range(systems)]
    return pl.pallas_call(
        functools.partial(merge_kernel, chunks),
        grid=(rows // block,),
        out_shape=[jax.ShapeDtypeStruct((rows, n), kind) for n, kind in zip(sizes, kinds)],
        in_specs=[
            whole_smem(),
            whole_smem(),
            pl.BlockSpec((count, block, width), lambda i: (0, i, 0)),
        ],
        out_specs=[pl.BlockSpec((block, n), lambda i: (i, 0)) for n in sizes],
        compiler_params=params(),
        name="merge_parts",
    )(place, coef, experts)


def expert_kernel(place_ref, coef_ref, *refs):
    me = place_ref[0]
    out_ref = refs[-1]
    count, rows, _ = out_ref.shape
    systems = coef_ref.shape[0]
    grad_refs = refs[:systems]
    step = 16
    scales = [[coef_ref[me ^ k, me * count + e] for e in range(count)] for k in range(systems)]

    @pl.loop(0, rows // step)
    def _(i):
        at = pl.ds(pl.multiple_of(i * step, step), step)
        grads = [ref[at, :].astype(F32) for ref in grad_refs]
        for e in range(count):
            total = scales[0][e] * grads[0]
            for k in range(1, systems):
                total = total + scales[k][e] * grads[k]
            out_ref[e, at, :] = total


def expert_grads(place, coef, grads, count, width, lo, earlier):
    rows, size = grads[0].shape
    tile = LANES if size % LANES == 0 else size
    extra = [] if earlier is None else [earlier]
    return pl.pallas_call(
        expert_kernel,
        grid=(size // tile,),
        out_shape=jax.ShapeDtypeStruct((count, rows, width), F32),
        in_specs=[whole_smem(), whole_smem()]
        + [pl.BlockSpec((rows, tile), lambda i: (0, i))] * len(grads)
        + [pl.BlockSpec(memory_space=pl.ANY)] * len(extra),
        out_specs=pl.BlockSpec((count, rows, tile), lambda i: (0, 0, lo // tile + i)),
        input_output_aliases={2 + len(grads): 0} if extra else {},
        compiler_params=params(),
        name="expert_grads",
    )(place, coef, *grads, *extra)


def prepare_kernel(chunks, cols_ref, rows_ref, radial_ref, near_ref, far_ref, *refs):
    pieces = len(chunks)
    atoms_ref, gather_ref, sum_ref = refs[:3]
    radial_refs, scaled_refs, cot_ref = refs[3 : 3 + pieces], refs[3 + pieces : -1], refs[-1]
    slots, _, block, _ = near_ref.shape
    atoms = atoms_ref.shape[0]
    tile = radial_ref.shape[0]

    @pl.when(pl.program_id(0) == 0)
    def _():
        for side, ref in enumerate((near_ref, far_ref)):
            for k in range(slots):
                at = slice((side * slots + k) * block, (side * slots + k + 1) * block)
                atoms_ref[at, :] = ref[k, 0]
                cot_ref[at, :] = ref[k, 1]

    def hot(index, shape, axis):
        return jnp.where(index == lax.broadcasted_iota(jnp.int32, shape, axis), 1.0, 0.0).astype(BF16)

    gather_ref[:, :atoms] = hot(cols_ref[:, 0:1], (tile, atoms), 1)
    hot_tgt = hot(cols_ref[:, 1:2], (tile, atoms), 1)
    gather_ref[:, atoms:] = hot_tgt
    sum_ref[:atoms, :] = hot(rows_ref[0:1, :], (atoms, tile), 0)
    sum_ref[atoms:, :] = hot(rows_ref[1:2, :], (atoms, tile), 0)
    for j, (lo, size) in enumerate(chunks):
        at = slice(lo, lo + size)
        cot = jnp.dot(hot_tgt, cot_ref[:, at], preferred_element_type=F32)
        radial_refs[j][...] = radial_ref[:, at]
        scaled_refs[j][...] = (cot * radial_ref[:, at].astype(F32)).astype(BF16)


def prepare(chunks, cols, rows, radial, near, far, tile):
    edges, width = radial.shape
    slots, _, block, _ = near.shape
    atoms = 2 * slots * block
    by_edge = lambda n: pl.BlockSpec((tile, n), lambda i: (i, 0))
    by_column = lambda n: pl.BlockSpec((n, tile), lambda i: (0, i))
    per_chunk = [by_edge(size) for _, size in chunks]
    return pl.pallas_call(
        functools.partial(prepare_kernel, chunks),
        grid=(edges // tile,),
        out_shape=[
            jax.ShapeDtypeStruct((atoms, width), BF16),
            jax.ShapeDtypeStruct((edges, 2 * atoms), BF16),
            jax.ShapeDtypeStruct((2 * atoms, edges), BF16),
        ]
        + [jax.ShapeDtypeStruct((edges, size), BF16) for _ in range(2) for _, size in chunks],
        in_specs=[by_edge(2), by_column(2), by_edge(width), whole_vmem(), whole_vmem()],
        out_specs=[
            pl.BlockSpec((atoms, width), lambda i: (0, 0)),
            by_edge(2 * atoms),
            by_column(2 * atoms),
        ]
        + per_chunk * 2,
        scratch_shapes=[pltpu.VMEM((atoms, width), BF16)],
        compiler_params=params(),
        cost_estimate=pl.CostEstimate(
            flops=2 * atoms * width * edges, bytes_accessed=14 * edges * width, transcendentals=0
        ),
        name="prepare",
    )(cols, rows, radial, near, far)


def edge_kernel(
    place_ref, gather_ref, sum_ref, radial_ref, scaled_ref, atoms_ref, near_ref, far_ref, *refs
):
    kept_ref, sent_ref, node_kept_ref, node_sent_ref, weight_ref, proj_ref, acc_ref = refs
    step = pl.program_id(0)
    atoms, width_in = atoms_ref.shape

    @pl.when(step == 0)
    def _():
        core = place_ref[2]
        chips, depth, _ = near_ref.shape
        for chip in range(chips):
            for ref, parity in ((near_ref, core), (far_ref, 1 - core)):
                at = pl.ds(pl.multiple_of((2 * chip + parity) * depth, depth), depth)
                weight_ref[at, :] = ref[chip]
        for half in range(2):
            proj_ref[half * atoms : (half + 1) * atoms, :] = jnp.dot(
                atoms_ref[...],
                weight_ref[half * width_in : (half + 1) * width_in, :],
                preferred_element_type=F32,
            ).astype(BF16)
        acc_ref[...] = jnp.zeros_like(acc_ref)

    pre = jnp.dot(gather_ref[...], proj_ref[...], preferred_element_type=F32)
    sigma = 0.5 + 0.5 * jnp.tanh(0.5 * pre)
    silu = pre * sigma
    message = (silu * radial_ref[...].astype(F32)).astype(BF16)
    slope = sigma + silu * (1.0 - sigma)
    pre_grad = (scaled_ref[...].astype(F32) * slope).astype(BF16)
    acc_ref[0] += jnp.dot(sum_ref[:atoms, :], pre_grad, preferred_element_type=F32)
    acc_ref[1] += jnp.dot(sum_ref[atoms:, :], pre_grad, preferred_element_type=F32)
    acc_ref[2] += jnp.dot(sum_ref[atoms:, :], message, preferred_element_type=F32)

    @pl.when(step == pl.num_programs(0) - 1)
    def _():
        half = atoms // 2
        kept_ref[...] = acc_ref[:2, :half, :]
        sent_ref[...] = acc_ref[:2, half:, :].astype(BF16)
        node_kept_ref[...] = acc_ref[2, :half, :]
        node_sent_ref[...] = acc_ref[2, half:, :].astype(BF16)


def edge_sums(place, gather, sums, radial, scaled, atoms, near, far, tile):
    edges, width = radial.shape
    count, width_in = atoms.shape
    flops = 2 * count * width * (2 * width_in + 5 * edges)
    fixed = lambda *shape: pl.BlockSpec(shape, lambda i: (0,) * len(shape))
    outs = [
        ((2, count // 2, width), F32),
        ((2, count // 2, width), BF16),
        ((count // 2, width), F32),
        ((count // 2, width), BF16),
        ((2 * width_in, width), BF16),
    ]
    return pl.pallas_call(
        edge_kernel,
        grid=(edges // tile,),
        out_shape=[jax.ShapeDtypeStruct(shape, kind) for shape, kind in outs],
        in_specs=[
            whole_smem(),
            pl.BlockSpec((tile, 2 * count), lambda i: (i, 0)),
            pl.BlockSpec((2 * count, tile), lambda i: (0, i)),
            pl.BlockSpec((tile, width), lambda i: (i, 0)),
            pl.BlockSpec((tile, width), lambda i: (i, 0)),
            fixed(count, width_in),
            whole_vmem(),
            whole_vmem(),
        ],
        out_specs=[fixed(*shape) for shape, _ in outs],
        scratch_shapes=[
            pltpu.VMEM((2 * count, width), BF16),
            pltpu.VMEM((3, count, width), F32),
        ],
        compiler_params=params(),
        cost_estimate=pl.CostEstimate(
            flops=flops,
            bytes_accessed=4 * edges * width + 8 * edges * count,
            transcendentals=edges * width,
        ),
        name="edge_sums",
    )(place, gather, sums, radial, scaled, atoms, near, far)


def after(x, *others):
    return lax.optimization_barrier((x, *others))[0]


def shards(systems, ways, pieces, atoms, cotangent, experts, radial, coef, source, target):
    chips = ways // 2
    me_sys = lax.axis_index("sys")
    me_edge = lax.axis_index("edge")
    chip, core = me_edge // 2, me_edge % 2
    place = jnp.stack([me_sys, chip, core]).astype(jnp.int32)
    count, depth, width = experts.shape
    own = atoms.shape[1]
    edges = radial.shape[1]
    tile = min(512, edges)
    chunks = column_chunks(width, pieces)
    lines = [[2 * z + c for z in range(chips)] for c in range(2)]

    def across(x, k):
        return lax.ppermute(x, "sys", [(s, s ^ k) for s in range(systems)])

    def swap(x):
        return lax.ppermute(x, "edge", [(e, e ^ 1) for e in range(ways)])

    def shift(x, k):
        return lax.ppermute(x, "edge", [(e, (e + 2 * k) % ways) for e in range(ways)])

    features = jnp.concatenate([atoms, cotangent], axis=0)
    near = jnp.stack([features] + [shift(features, k) for k in range(1, chips)])
    far = swap(near)

    def slot(index):
        owner, offset = index // own, index % own
        back = (chip - owner // 2 + chips) % chips
        return ((owner % 2) ^ core) * (chips * own) + back * own + offset

    ends = jnp.stack([slot(source[0]), slot(target[0])])
    prepared = prepare(chunks, ends.T, ends, radial[0], near, far, tile)
    all_atoms, hot_gather, hot_sum = prepared[:3]
    radials, scaled = prepared[3 : 3 + len(chunks)], prepared[3 + len(chunks) :]
    own_cols = lax.dynamic_slice_in_dim(all_atoms, (me_edge % chips) * depth, depth, 1).T

    parts = merge_parts(place, coef, experts, systems, chunks)
    weights = []
    for j in range(len(chunks)):
        total = parts[j * systems]
        got = [across(parts[j * systems + k], k) for k in range(1, systems)]
        for part in got:
            total = total + part.astype(F32)
        block = lax.all_gather(total.astype(BF16), "edge", axis_index_groups=lines)
        weights.append((block, swap(block)))

    def slots(kept, other):
        return [
            kept[..., k * own : (k + 1) * own, :]
            + other[..., k * own : (k + 1) * own, :].astype(F32)
            for k in range(chips)
        ]

    def scatter(blocks):
        total = blocks[0]
        for k in range(1, chips):
            total = total + shift(blocks[k].astype(BF16), chips - k).astype(F32)
        return total

    atom_grad, expert_grad, nodes = None, None, []
    over = (((1,), (1,)), ((), ()))
    half = chips * own
    for j, (lo, size) in enumerate(chunks):
        kept, sent, node_kept, node_sent, weight = edge_sums(
            place, hot_gather, hot_sum, radials[j], scaled[j], all_atoms, *weights[j], tile
        )
        sums = scatter(slots(kept, swap(sent))).astype(BF16)
        nodes.append(slots(node_kept, swap(node_sent)))

        def half_for(k):
            return jnp.where((chip + k) % chips < chips // 2, sums[0], sums[1])

        picked = [half_for(0)] + [shift(half_for(k), k) for k in range(1, chips)]
        picked = jnp.concatenate(picked, axis=0)
        picked_other = swap(picked)
        grad = jnp.dot(own_cols[:, :half], picked, preferred_element_type=F32)
        grad = grad + jnp.dot(own_cols[:, half:], picked_other, preferred_element_type=F32)
        send = grad.astype(BF16)
        grads = [grad] + [across(send, k) for k in range(1, systems)]
        expert_grad = expert_grads(place, coef, grads, count, width, lo, expert_grad)
        for i in range(2):
            part = lax.dot_general(
                sums[i], weight[i * width : (i + 1) * width], over, preferred_element_type=F32
            )
            atom_grad = part if atom_grad is None else atom_grad + part

    blocks = [jnp.concatenate(list(x), axis=1) for x in zip(*nodes)]
    blocks = [blocks[0]] + [after(x.astype(BF16), picked) for x in blocks[1:]]
    node = scatter(blocks).astype(BF16)
    return node[None], atom_grad[None], expert_grad


def solution(mesh):
    placed = P("sys", "edge", None)
    return jax.shard_map(
        functools.partial(shards, mesh.shape["sys"], mesh.shape["edge"], PIECES),
        mesh=mesh,
        in_specs=(placed, placed, placed, placed, P(), P("sys", "edge"), P("sys", "edge")),
        out_specs=(placed, placed, placed),
        check_vma=False,
    )
```

```python
import functools

import jax
import jax.numpy as jnp
from jax import lax
from jax.experimental import pallas as pl
from jax.experimental.pallas import tpu as pltpu
from jax.sharding import PartitionSpec as P

F32 = jnp.float32
BF16 = jnp.bfloat16
VMEM_LIMIT = 48 << 20
STEP = 16


def whole_vmem():
    return pl.BlockSpec(memory_space=pltpu.VMEM)


def in_hbm():
    return pl.BlockSpec(memory_space=pltpu.HBM)


def whole_smem():
    return pl.BlockSpec(memory_space=pltpu.SMEM)


def params():
    return pltpu.CompilerParams(vmem_limit_bytes=VMEM_LIMIT)


def row_parts(depth):
    first = -(-depth // (2 * STEP)) * STEP
    return [(0, first), (first, depth - first)]


def merge_kernel(parts, place_ref, coef_ref, experts_ref, *refs):
    part_refs, held_ref, sems = refs[:-2], refs[-2], refs[-1]
    me = place_ref[0]
    count, _, width = experts_ref.shape
    systems = len(part_refs) // len(parts)
    copies = []
    for h, (lo, size) in enumerate(parts):
        at = pl.ds(lo, size)
        copies.append(
            pltpu.make_async_copy(experts_ref.at[:, at, :], held_ref.at[:, at, :], sems.at[h])
        )
        copies[-1].start()
    scales = [[coef_ref[me ^ k, me * count + e] for e in range(count)] for k in range(systems)]
    for h, (lo, size) in enumerate(parts):
        copies[h].wait()

        @pl.loop(0, size // STEP)
        def _(i):
            at = pl.ds(pl.multiple_of(i * STEP, STEP), STEP)
            source = pl.ds(pl.multiple_of(lo + i * STEP, STEP), STEP)
            for col in range(0, width, 128):
                cols = slice(col, min(col + 128, width))
                loaded = [held_ref[e, source, cols].astype(F32) for e in range(count)]
                for k in range(systems):
                    total = scales[k][0] * loaded[0]
                    for e in range(1, count):
                        total = total + scales[k][e] * loaded[e]
                    ref = part_refs[h * systems + k]
                    ref[at, cols] = total.astype(ref.dtype)


def merge_parts(place, coef, experts, systems, parts):
    _, _, width = experts.shape
    outs = [((size, width), BF16 if k else F32) for _, size in parts for k in range(systems)]
    return pl.pallas_call(
        functools.partial(merge_kernel, parts),
        out_shape=[jax.ShapeDtypeStruct(*out) for out in outs],
        in_specs=[whole_smem(), whole_smem(), in_hbm()],
        out_specs=[whole_vmem()] * len(outs),
        scratch_shapes=[
            pltpu.VMEM(experts.shape, BF16),
            pltpu.SemaphoreType.DMA((len(parts),)),
        ],
        compiler_params=params(),
        name="merge_parts",
    )(place, coef, experts)


def merged_grad_kernel(parts, cols_ref, *refs):
    block_refs, out_refs, sums_ref = refs[: -2 * len(parts) - 1], refs[-2 * len(parts) - 1 : -1], refs[-1]
    own = block_refs[0].shape[0]
    for i, ref in enumerate(block_refs):
        sums_ref[i * own : (i + 1) * own, :] = ref[...]
    for h, (lo, size) in enumerate(parts):
        grad = jnp.dot(cols_ref[lo : lo + size, :], sums_ref[...], preferred_element_type=F32)
        out_refs[2 * h][...] = grad
        out_refs[2 * h + 1][...] = grad.astype(BF16)


def merged_grads(cols, blocks, parts):
    own, width = blocks[0].shape
    outs = [((size, width), kind) for _, size in parts for kind in (F32, BF16)]
    return pl.pallas_call(
        functools.partial(merged_grad_kernel, parts),
        out_shape=[jax.ShapeDtypeStruct(*out) for out in outs],
        in_specs=[whole_vmem()] * (1 + len(blocks)),
        out_specs=[whole_vmem()] * len(outs),
        scratch_shapes=[pltpu.VMEM((own * len(blocks), width), BF16)],
        compiler_params=params(),
        name="merged_grads",
    )(cols, *blocks)


def expert_kernel(parts, masks, place_ref, coef_ref, *refs):
    grad_refs, out_ref, held_ref, sems = refs[:-3], refs[-3], refs[-2], refs[-1]
    me = place_ref[0]
    count, _, width = out_ref.shape
    systems = coef_ref.shape[0]
    copies = []
    for h, (lo, size) in enumerate(parts):
        scales = [
            [coef_ref[me ^ mask, me * count + e] for e in range(count)] for mask in masks[h]
        ]

        @pl.loop(0, size // STEP)
        def _(i):
            at = pl.ds(pl.multiple_of(i * STEP, STEP), STEP)
            to = pl.ds(pl.multiple_of(lo + i * STEP, STEP), STEP)
            for col in range(0, width, 128):
                cols = slice(col, min(col + 128, width))
                grads = [ref[at, cols].astype(F32) for ref in grad_refs[h * systems : (h + 1) * systems]]
                for e in range(count):
                    total = scales[0][e] * grads[0]
                    for k in range(1, systems):
                        total = total + scales[k][e] * grads[k]
                    held_ref[e, to, cols] = total

        at = pl.ds(lo, size)
        copies.append(pltpu.make_async_copy(held_ref.at[:, at, :], out_ref.at[:, at, :], sems.at[h]))
        copies[-1].start()
    for copy in copies:
        copy.wait()


def expert_grads(place, coef, grads, masks, shape, parts):
    return pl.pallas_call(
        functools.partial(expert_kernel, parts, masks),
        out_shape=jax.ShapeDtypeStruct(shape, F32),
        in_specs=[whole_smem(), whole_smem()] + [whole_vmem()] * len(grads),
        out_specs=in_hbm(),
        scratch_shapes=[pltpu.VMEM(shape, F32), pltpu.SemaphoreType.DMA((len(parts),))],
        compiler_params=params(),
        name="expert_grads",
    )(place, coef, *grads)


def prepare_kernel(slots, cols_ref, rows_ref, radial_ref, *refs):
    atom_refs, cot_refs = refs[:slots], refs[slots : 2 * slots]
    atoms_ref, gather_ref, sum_ref, scaled_ref, cot_ref = refs[2 * slots :]
    atoms = atoms_ref.shape[0]
    tile = radial_ref.shape[0]

    @pl.when(pl.program_id(0) == 0)
    def _():
        own = atoms // slots
        for k in range(slots):
            at = slice(k * own, (k + 1) * own)
            atoms_ref[at, :] = atom_refs[k][0]
            cot_ref[at, :] = cot_refs[k][0]

    def hot(index, shape, axis):
        return jnp.where(index == lax.broadcasted_iota(jnp.int32, shape, axis), 1.0, 0.0).astype(BF16)

    gather_ref[:, :atoms] = hot(cols_ref[:, 0:1], (tile, atoms), 1)
    hot_tgt = hot(cols_ref[:, 1:2], (tile, atoms), 1)
    gather_ref[:, atoms:] = hot_tgt
    sum_ref[:atoms, :] = hot(rows_ref[0:1, :], (atoms, tile), 0)
    sum_ref[atoms:, :] = hot(rows_ref[1:2, :], (atoms, tile), 0)
    cot = jnp.dot(hot_tgt, cot_ref[...], preferred_element_type=F32)
    scaled_ref[...] = (cot * radial_ref[...].astype(F32)).astype(BF16)


def prepare(cols, rows, radial, atom_blocks, cot_blocks, tile):
    edges, width = radial.shape
    slots = len(atom_blocks)
    atoms = slots * atom_blocks[0].shape[1]
    by_edge = lambda n: pl.BlockSpec((tile, n), lambda i: (i, 0))
    by_column = lambda n: pl.BlockSpec((n, tile), lambda i: (0, i))
    return pl.pallas_call(
        functools.partial(prepare_kernel, slots),
        grid=(edges // tile,),
        out_shape=[
            jax.ShapeDtypeStruct((atoms, width), BF16),
            jax.ShapeDtypeStruct((edges, 2 * atoms), BF16),
            jax.ShapeDtypeStruct((2 * atoms, edges), BF16),
            jax.ShapeDtypeStruct((edges, width), BF16),
        ],
        in_specs=[by_edge(2), by_column(2), by_edge(width)] + [whole_vmem()] * (2 * slots),
        out_specs=[
            pl.BlockSpec((atoms, width), lambda i: (0, 0)),
            by_edge(2 * atoms),
            by_column(2 * atoms),
            by_edge(width),
        ],
        scratch_shapes=[pltpu.VMEM((atoms, width), BF16)],
        compiler_params=params(),
        cost_estimate=pl.CostEstimate(
            flops=2 * atoms * width * edges, bytes_accessed=14 * edges * width, transcendentals=0
        ),
        name="prepare",
    )(cols, rows, radial, *atom_blocks, *cot_blocks)


def edge_kernel(
    chips, parts, place_ref, gather_ref, sum_ref, radial_ref, scaled_ref, atoms_ref, *refs
):
    blocks = 2 * chips * len(parts)
    block_refs = refs[:blocks]
    kept_refs, sent_refs, weight_out = refs[blocks : blocks + 3], refs[blocks + 3 : blocks + 6], refs[blocks + 6]
    weight_ref, proj_ref, acc_ref, sem = refs[blocks + 7 :]
    step = pl.program_id(0)
    atoms, width_in = atoms_ref.shape
    store = pltpu.make_async_copy(weight_ref, weight_out, sem)

    @pl.when(step == 0)
    def _():
        chip, core = place_ref[1], place_ref[2]
        depth = sum(size for _, size in parts)
        for h, (lo, size) in enumerate(parts):
            for k in range(chips):
                source = lax.rem(chip - k + chips, chips)
                for other in range(2):
                    device = 2 * source + (core if other == 0 else 1 - core)
                    at = pl.ds(pl.multiple_of(device * depth + lo, STEP), size)
                    weight_ref[at, :] = block_refs[(h * chips + k) * 2 + other][...]
        store.start()
        for half in range(2):
            proj_ref[half * atoms : (half + 1) * atoms, :] = jnp.dot(
                atoms_ref[...],
                weight_ref[half * width_in : (half + 1) * width_in, :],
                preferred_element_type=F32,
            ).astype(BF16)
        acc_ref[...] = jnp.zeros_like(acc_ref)

    pre = jnp.dot(gather_ref[...], proj_ref[...], preferred_element_type=F32)
    sigma = 0.5 + 0.5 * jnp.tanh(0.5 * pre)
    silu = pre * sigma
    message = (silu * radial_ref[...].astype(F32)).astype(BF16)
    slope = sigma + silu * (1.0 - sigma)
    pre_grad = (scaled_ref[...].astype(F32) * slope).astype(BF16)
    acc_ref[0] += jnp.dot(sum_ref[:atoms, :], pre_grad, preferred_element_type=F32)
    acc_ref[1] += jnp.dot(sum_ref[atoms:, :], pre_grad, preferred_element_type=F32)
    acc_ref[2] += jnp.dot(sum_ref[atoms:, :], message, preferred_element_type=F32)

    @pl.when(step == pl.num_programs(0) - 1)
    def _():
        half = atoms // 2
        for i in range(3):
            kept_refs[i][...] = acc_ref[i, :half, :]
            sent_refs[i][...] = acc_ref[i, half:, :].astype(BF16)
        store.wait()


def edge_sums(chips, parts, place, gather, sums, radial, scaled, atoms, blocks, tile):
    edges, width = radial.shape
    count, width_in = atoms.shape
    flops = 2 * count * width * (2 * width_in + 5 * edges)
    fixed = lambda *shape: pl.BlockSpec(shape, lambda i: (0,) * len(shape))
    halves = [((count // 2, width), F32)] * 3 + [((count // 2, width), BF16)] * 3
    outs = halves + [((2 * width_in, width), BF16)]
    return pl.pallas_call(
        functools.partial(edge_kernel, chips, parts),
        grid=(edges // tile,),
        out_shape=[jax.ShapeDtypeStruct(shape, kind) for shape, kind in outs],
        in_specs=[
            whole_smem(),
            pl.BlockSpec((tile, 2 * count), lambda i: (i, 0)),
            pl.BlockSpec((2 * count, tile), lambda i: (0, i)),
            pl.BlockSpec((tile, width), lambda i: (i, 0)),
            pl.BlockSpec((tile, width), lambda i: (i, 0)),
            fixed(count, width_in),
        ]
        + [whole_vmem()] * len(blocks),
        out_specs=[fixed(*shape) for shape, _ in halves] + [in_hbm()],
        scratch_shapes=[
            pltpu.VMEM((2 * width_in, width), BF16),
            pltpu.VMEM((2 * count, width), BF16),
            pltpu.VMEM((3, count, width), F32),
            pltpu.SemaphoreType.DMA,
        ],
        compiler_params=params(),
        cost_estimate=pl.CostEstimate(
            flops=flops,
            bytes_accessed=4 * edges * width + 8 * edges * count,
            transcendentals=edges * width,
        ),
        name="edge_sums",
    )(place, gather, sums, radial, scaled, atoms, *blocks)


def after(x, *others):
    return lax.optimization_barrier((x, *others))[0]


def shards(systems, ways, atoms, cotangent, experts, radial, coef, source, target):
    chips = ways // 2
    me_sys = lax.axis_index("sys")
    me_edge = lax.axis_index("edge")
    chip, core = me_edge // 2, me_edge % 2
    place = jnp.stack([me_sys, chip, core]).astype(jnp.int32)
    _, depth, width = experts.shape
    own = atoms.shape[1]
    tile = min(512, radial.shape[1])
    parts = row_parts(depth)

    def across(x, k):
        return lax.ppermute(x, "sys", [(s, s ^ k) for s in range(systems)])

    def swap(x):
        return lax.ppermute(x, "edge", [(e, e ^ 1) for e in range(ways)])

    def shift(x, k):
        return lax.ppermute(x, "edge", [(e, (e + 2 * k) % ways) for e in range(ways)])

    def gather(x):
        got = [x]
        for _ in range(chips - 1):
            got.append(shift(got[-1], 1))
        return got

    def both_cores(blocks):
        return blocks + [swap(block) for block in blocks]

    def slot(index):
        owner, offset = index // own, index % own
        back = (chip - owner // 2 + chips) % chips
        return ((owner % 2) ^ core) * (chips * own) + back * own + offset

    atom_blocks, cot_blocks = both_cores(gather(atoms)), both_cores(gather(cotangent))
    ends = jnp.stack([slot(source[0]), slot(target[0])])
    all_atoms, hot_gather, hot_sum, scaled = prepare(
        ends.T, ends, radial[0], atom_blocks, cot_blocks, tile
    )
    own_cols = lax.dynamic_slice_in_dim(all_atoms, (me_edge % chips) * depth, depth, 1).T

    merged = merge_parts(place, coef, experts, systems, parts)
    blocks = []
    for h in range(len(parts)):
        total = merged[h * systems]
        for k in range(1, systems):
            total = total + across(merged[h * systems + k], k).astype(F32)
        for block in gather(total.astype(BF16)):
            blocks += [block, swap(block)]

    *halves, weight = edge_sums(
        chips, parts, place, hot_gather, hot_sum, radial[0], scaled, all_atoms, blocks, tile
    )

    def slots(i):
        kept, other = halves[i], swap(halves[3 + i])
        cut = lambda x, k: x[k * own : (k + 1) * own]
        return [cut(kept, k) + cut(other, k).astype(F32) for k in range(chips)]

    def ring_sum(terms):
        total = terms[1 % chips]
        for t in range(1, chips):
            total = shift(total.astype(BF16), 1).astype(F32) + terms[(t + 1) % chips]
        return total

    sums = [ring_sum(slots(i)).astype(BF16) for i in range(2)]

    def half_for(k):
        return jnp.where((chip + k) % chips < chips // 2, sums[0], sums[1])

    picked = both_cores([half_for(0)] + [shift(half_for(k), k) for k in range(1, chips)])
    grads = merged_grads(own_cols, picked, parts)

    bits = [1 << b for b in range((systems - 1).bit_length())]
    all_grads, all_masks = [], []
    for h, order in enumerate((bits, bits[::-1])):
        held, masks = [grads[2 * h + 1]], [0]
        for bit in order:
            held += [across(x, bit) for x in held]
            masks += [mask ^ bit for mask in masks]
        all_grads += [grads[2 * h]] + held[1:]
        all_masks.append(masks)
    expert_grad = expert_grads(place, coef, all_grads, all_masks, experts.shape, parts)

    node = slots(2)
    total = node[0]
    for k in range(1, chips):
        total = total + shift(after(node[k].astype(BF16), *picked), chips - k).astype(F32)

    over = (((1,), (1,)), ((), ()))
    atom_grad = lax.dot_general(sums[0], weight[:width], over, preferred_element_type=F32)
    atom_grad = atom_grad + lax.dot_general(
        sums[1], weight[width:], over, preferred_element_type=F32
    )
    return total.astype(BF16)[None], atom_grad[None], expert_grad


def solution(mesh):
    placed = P("sys", "edge", None)
    return jax.shard_map(
        functools.partial(shards, mesh.shape["sys"], mesh.shape["edge"]),
        mesh=mesh,
        in_specs=(placed, placed, placed, placed, P(), P("sys", "edge"), P("sys", "edge")),
        out_specs=(placed, placed, placed),
        check_vma=False,
    )
```

```python
import functools

import jax
import jax.numpy as jnp
from jax import lax
from jax.experimental import pallas as pl
from jax.experimental.pallas import tpu as pltpu
from jax.sharding import PartitionSpec as P

F32 = jnp.float32
BF16 = jnp.bfloat16
VMEM_LIMIT = 48 << 20
STEP = 16


def whole_vmem():
    return pl.BlockSpec(memory_space=pltpu.VMEM)


def in_hbm():
    return pl.BlockSpec(memory_space=pltpu.HBM)


def whole_smem():
    return pl.BlockSpec(memory_space=pltpu.SMEM)


def params():
    return pltpu.CompilerParams(vmem_limit_bytes=VMEM_LIMIT)


def row_parts(depth):
    first = -(-depth // (2 * STEP)) * STEP
    return [(0, first), (first, depth - first)]


def merge_kernel(parts, place_ref, coef_ref, experts_ref, atoms_ref, cot_ref, both_ref, *refs):
    part_refs, held_ref, sems, both_sem = refs[:-3], refs[-3], refs[-2], refs[-1]
    me = place_ref[0]
    count, _, width = experts_ref.shape
    systems = len(part_refs) // len(parts)
    joins = [
        pltpu.make_async_copy(ref.at[0], both_ref.at[i], both_sem.at[i])
        for i, ref in enumerate((atoms_ref, cot_ref))
    ]
    copies = []
    for h, (lo, size) in enumerate(parts):
        at = pl.ds(lo, size)
        copies.append(
            pltpu.make_async_copy(experts_ref.at[:, at, :], held_ref.at[:, at, :], sems.at[h])
        )
        copies[-1].start()
    for join in joins:
        join.start()
    scales = [[coef_ref[me ^ k, me * count + e] for e in range(count)] for k in range(systems)]
    for h, (lo, size) in enumerate(parts):
        copies[h].wait()

        @pl.loop(0, size // STEP)
        def _(i):
            at = pl.ds(pl.multiple_of(i * STEP, STEP), STEP)
            source = pl.ds(pl.multiple_of(lo + i * STEP, STEP), STEP)
            for col in range(0, width, 128):
                cols = slice(col, min(col + 128, width))
                loaded = [held_ref[e, source, cols].astype(F32) for e in range(count)]
                for k in range(systems):
                    total = scales[k][0] * loaded[0]
                    for e in range(1, count):
                        total = total + scales[k][e] * loaded[e]
                    ref = part_refs[h * systems + k]
                    ref[at, cols] = total.astype(ref.dtype)
    for join in joins:
        join.wait()


def merge_parts(place, coef, experts, atoms, cotangent, systems, parts):
    _, _, width = experts.shape
    outs = [((2, *atoms.shape[1:]), BF16)]
    outs += [((size, width), BF16 if k else F32) for _, size in parts for k in range(systems)]
    return pl.pallas_call(
        functools.partial(merge_kernel, parts),
        out_shape=[jax.ShapeDtypeStruct(*out) for out in outs],
        in_specs=[whole_smem(), whole_smem()] + [in_hbm()] * 3,
        out_specs=[in_hbm()] + [whole_vmem()] * (len(outs) - 1),
        scratch_shapes=[
            pltpu.VMEM(experts.shape, BF16),
            pltpu.SemaphoreType.DMA((len(parts),)),
            pltpu.SemaphoreType.DMA((2,)),
        ],
        compiler_params=params(),
        name="merge_parts",
    )(place, coef, experts, atoms, cotangent)


def merged_grad_kernel(parts, cols_ref, *refs):
    block_refs, out_refs, sums_ref = refs[: -2 * len(parts) - 1], refs[-2 * len(parts) - 1 : -1], refs[-1]
    own = block_refs[0].shape[0]
    for i, ref in enumerate(block_refs):
        sums_ref[i * own : (i + 1) * own, :] = ref[...]
    for h, (lo, size) in enumerate(parts):
        grad = jnp.dot(cols_ref[lo : lo + size, :], sums_ref[...], preferred_element_type=F32)
        out_refs[2 * h][...] = grad
        out_refs[2 * h + 1][...] = grad.astype(BF16)


def merged_grads(cols, blocks, parts):
    own, width = blocks[0].shape
    outs = [((size, width), kind) for _, size in parts for kind in (F32, BF16)]
    return pl.pallas_call(
        functools.partial(merged_grad_kernel, parts),
        out_shape=[jax.ShapeDtypeStruct(*out) for out in outs],
        in_specs=[whole_vmem()] * (1 + len(blocks)),
        out_specs=[whole_vmem()] * len(outs),
        scratch_shapes=[pltpu.VMEM((own * len(blocks), width), BF16)],
        compiler_params=params(),
        name="merged_grads",
    )(cols, *blocks)


def expert_kernel(parts, place_ref, coef_ref, *refs):
    grad_refs, out_ref, held_ref, sems = refs[:-3], refs[-3], refs[-2], refs[-1]
    me = place_ref[0]
    count, _, width = out_ref.shape
    systems = coef_ref.shape[0]
    copies = []
    for h, (lo, size) in enumerate(parts):
        scales = [
            [coef_ref[me ^ k, me * count + e] for e in range(count)] for k in range(systems)
        ]

        @pl.loop(0, size // STEP)
        def _(i):
            at = pl.ds(pl.multiple_of(i * STEP, STEP), STEP)
            to = pl.ds(pl.multiple_of(lo + i * STEP, STEP), STEP)
            for col in range(0, width, 128):
                cols = slice(col, min(col + 128, width))
                grads = [ref[at, cols].astype(F32) for ref in grad_refs[h * systems : (h + 1) * systems]]
                for e in range(count):
                    total = scales[0][e] * grads[0]
                    for k in range(1, systems):
                        total = total + scales[k][e] * grads[k]
                    held_ref[e, to, cols] = total

        at = pl.ds(lo, size)
        copies.append(pltpu.make_async_copy(held_ref.at[:, at, :], out_ref.at[:, at, :], sems.at[h]))
        copies[-1].start()
    for copy in copies:
        copy.wait()


def expert_grads(place, coef, grads, shape, parts):
    return pl.pallas_call(
        functools.partial(expert_kernel, parts),
        out_shape=jax.ShapeDtypeStruct(shape, F32),
        in_specs=[whole_smem(), whole_smem()] + [whole_vmem()] * len(grads),
        out_specs=in_hbm(),
        scratch_shapes=[pltpu.VMEM(shape, F32), pltpu.SemaphoreType.DMA((len(parts),))],
        compiler_params=params(),
        name="expert_grads",
    )(place, coef, *grads)


def hot_kernel(cols_ref, rows_ref, across_ref, down_ref, gather_ref, sum_ref, token_ref):
    atoms = down_ref.shape[0]

    def hot(same):
        return jnp.where(same, 1.0, 0.0).astype(BF16)

    for i in range(2):
        at = slice(i * atoms, (i + 1) * atoms)
        gather_ref[:, at] = hot(cols_ref[:, i : i + 1] == across_ref[...])
        sum_ref[at, :] = hot(down_ref[...] == rows_ref[i : i + 1, :])
    token_ref[...] = jnp.zeros_like(token_ref)


def hot_ends(cols, rows, order, tile):
    edges, atoms = cols.shape[0], order.shape[0]
    fixed = lambda *shape: pl.BlockSpec(shape, lambda i: (0, 0))
    return pl.pallas_call(
        hot_kernel,
        grid=(edges // tile,),
        out_shape=[
            jax.ShapeDtypeStruct((edges, 2 * atoms), BF16),
            jax.ShapeDtypeStruct((2 * atoms, edges), BF16),
            jax.ShapeDtypeStruct((8, 128), F32),
        ],
        in_specs=[
            pl.BlockSpec((tile, 2), lambda i: (i, 0)),
            pl.BlockSpec((2, tile), lambda i: (0, i)),
            fixed(1, atoms),
            fixed(atoms, 1),
        ],
        out_specs=[
            pl.BlockSpec((tile, 2 * atoms), lambda i: (i, 0)),
            pl.BlockSpec((2 * atoms, tile), lambda i: (0, i)),
            fixed(8, 128),
        ],
        compiler_params=params(),
        cost_estimate=pl.CostEstimate(
            flops=16 * edges * atoms, bytes_accessed=8 * edges * atoms, transcendentals=0
        ),
        name="hot_ends",
    )(cols, rows, order[None, :], order[:, None])


def scale_kernel(slots, gather_ref, radial_ref, *refs):
    block_refs = refs[:slots]
    atoms_out, scaled_ref, atoms_ref, cot_ref, sems = refs[slots:]
    step = pl.program_id(0)
    own = block_refs[0].shape[1]
    store = pltpu.make_async_copy(atoms_ref, atoms_out, sems.at[2 * slots])

    @pl.when(step == 0)
    def _():
        loads = []
        for k, ref in enumerate(block_refs):
            at = pl.ds(k * own, own)
            for i, to in enumerate((atoms_ref, cot_ref)):
                loads.append(pltpu.make_async_copy(ref.at[i], to.at[at], sems.at[2 * k + i]))
                loads[-1].start()
        for load in loads:
            load.wait()
        store.start()

    cot = jnp.dot(gather_ref[...], cot_ref[...], preferred_element_type=F32)
    scaled_ref[...] = (cot * radial_ref[...].astype(F32)).astype(BF16)

    @pl.when(step == pl.num_programs(0) - 1)
    def _():
        store.wait()


def scaled_edges(hot_gather, radial, blocks, tile):
    edges, width = radial.shape
    atoms = hot_gather.shape[1] // 2
    slots = len(blocks)
    return pl.pallas_call(
        functools.partial(scale_kernel, slots),
        grid=(edges // tile,),
        out_shape=[
            jax.ShapeDtypeStruct((atoms, width), BF16),
            jax.ShapeDtypeStruct((edges, width), BF16),
        ],
        in_specs=[
            pl.BlockSpec((tile, atoms), lambda i: (i, 1)),
            pl.BlockSpec((tile, width), lambda i: (i, 0)),
        ]
        + [in_hbm()] * slots,
        out_specs=[
            in_hbm(),
            pl.BlockSpec((tile, width), lambda i: (i, 0)),
        ],
        scratch_shapes=[
            pltpu.VMEM((atoms, width), BF16),
            pltpu.VMEM((atoms, width), BF16),
            pltpu.SemaphoreType.DMA((2 * slots + 1,)),
        ],
        compiler_params=params(),
        cost_estimate=pl.CostEstimate(
            flops=2 * atoms * width * edges, bytes_accessed=6 * edges * width, transcendentals=0
        ),
        name="scaled_edges",
    )(hot_gather, radial, *blocks)


def edge_kernel(
    chips, parts, place_ref, gather_ref, sum_ref, radial_ref, scaled_ref, atoms_ref, *refs
):
    blocks = 2 * chips * len(parts)
    block_refs = refs[:blocks]
    kept_refs, sent_refs, weight_out = refs[blocks : blocks + 3], refs[blocks + 3 : blocks + 6], refs[blocks + 6]
    weight_ref, proj_ref, acc_ref, sem, sems = refs[blocks + 7 :]
    step = pl.program_id(0)
    atoms, width_in = atoms_ref.shape
    store = pltpu.make_async_copy(weight_ref, weight_out, sem)

    @pl.when(step == 0)
    def _():
        chip, core = place_ref[1], place_ref[2]
        depth = sum(size for _, size in parts)
        loads = []
        for h, (lo, size) in enumerate(parts):
            for k in range(chips):
                source = lax.rem(chip - k + chips, chips)
                for other in range(2):
                    device = 2 * source + (core if other == 0 else 1 - core)
                    at = pl.ds(pl.multiple_of(device * depth + lo, STEP), size)
                    i = (h * chips + k) * 2 + other
                    loads.append(
                        pltpu.make_async_copy(block_refs[i], weight_ref.at[at], sems.at[i])
                    )
                    loads[-1].start()
        for load in loads:
            load.wait()
        store.start()
        for half in range(2):
            proj_ref[half * atoms : (half + 1) * atoms, :] = jnp.dot(
                atoms_ref[...],
                weight_ref[half * width_in : (half + 1) * width_in, :],
                preferred_element_type=F32,
            ).astype(BF16)
        acc_ref[...] = jnp.zeros_like(acc_ref)

    pre = jnp.dot(gather_ref[...], proj_ref[...], preferred_element_type=F32)
    sigma = 0.5 + 0.5 * jnp.tanh(0.5 * pre)
    silu = pre * sigma
    message = (silu * radial_ref[...].astype(F32)).astype(BF16)
    slope = sigma + silu * (1.0 - sigma)
    pre_grad = (scaled_ref[...].astype(F32) * slope).astype(BF16)
    acc_ref[0] += jnp.dot(sum_ref[:atoms, :], pre_grad, preferred_element_type=F32)
    acc_ref[1] += jnp.dot(sum_ref[atoms:, :], pre_grad, preferred_element_type=F32)
    acc_ref[2] += jnp.dot(sum_ref[atoms:, :], message, preferred_element_type=F32)

    @pl.when(step == pl.num_programs(0) - 1)
    def _():
        half = atoms // 2
        for i in range(3):
            kept_refs[i][...] = acc_ref[i, :half, :]
            sent_refs[i][...] = acc_ref[i, half:, :].astype(BF16)
        store.wait()


def edge_sums(chips, parts, place, gather, sums, radial, scaled, atoms, blocks, tile):
    edges, width = radial.shape
    count, width_in = atoms.shape
    flops = 2 * count * width * (2 * width_in + 5 * edges)
    fixed = lambda *shape: pl.BlockSpec(shape, lambda i: (0,) * len(shape))
    halves = [((count // 2, width), F32)] * 3 + [((count // 2, width), BF16)] * 3
    outs = halves + [((2 * width_in, width), BF16)]
    return pl.pallas_call(
        functools.partial(edge_kernel, chips, parts),
        grid=(edges // tile,),
        out_shape=[jax.ShapeDtypeStruct(shape, kind) for shape, kind in outs],
        in_specs=[
            whole_smem(),
            pl.BlockSpec((tile, 2 * count), lambda i: (i, 0)),
            pl.BlockSpec((2 * count, tile), lambda i: (0, i)),
            pl.BlockSpec((tile, width), lambda i: (i, 0)),
            pl.BlockSpec((tile, width), lambda i: (i, 0)),
            fixed(count, width_in),
        ]
        + [in_hbm()] * len(blocks),
        out_specs=[fixed(*shape) for shape, _ in halves] + [in_hbm()],
        scratch_shapes=[
            pltpu.VMEM((2 * width_in, width), BF16),
            pltpu.VMEM((2 * count, width), BF16),
            pltpu.VMEM((3, count, width), F32),
            pltpu.SemaphoreType.DMA,
            pltpu.SemaphoreType.DMA((len(blocks),)),
        ],
        compiler_params=params(),
        cost_estimate=pl.CostEstimate(
            flops=flops,
            bytes_accessed=4 * edges * width + 8 * edges * count,
            transcendentals=edges * width,
        ),
        name="edge_sums",
    )(place, gather, sums, radial, scaled, atoms, *blocks)


def after(x, *others):
    return lax.optimization_barrier((x, *others))[0]


def shards(systems, ways, atoms, cotangent, experts, radial, coef, source, target):
    chips = ways // 2
    me_sys = lax.axis_index("sys")
    me_edge = lax.axis_index("edge")
    chip, core = me_edge // 2, me_edge % 2
    place = jnp.stack([me_sys, chip, core]).astype(jnp.int32)
    _, depth, width = experts.shape
    own = atoms.shape[1]
    tile = min(512, radial.shape[1])
    parts = row_parts(depth)

    def across(x, k):
        return lax.ppermute(x, "sys", [(s, s ^ k) for s in range(systems)])

    def swap(x):
        return lax.ppermute(x, "edge", [(e, e ^ 1) for e in range(ways)])

    def shift(x, k):
        return lax.ppermute(x, "edge", [(e, (e + 2 * k) % ways) for e in range(ways)])

    def both_cores(blocks):
        return blocks + [swap(block) for block in blocks]

    merged = merge_parts(place, coef, experts, atoms, cotangent, systems, parts)
    features, *merged = merged
    features = both_cores([features] + [shift(features, k) for k in range(1, chips)])

    at = jnp.arange(ways * own, dtype=jnp.int32)
    side, back, offset = at // (chips * own), at // own % chips, at % own
    order = (2 * ((chip - back + chips) % chips) + (core ^ side)) * own + offset
    ends = jnp.concatenate([source, target])
    hot_gather, hot_sum, hot_token = hot_ends(ends.T, ends, order, tile)
    all_atoms, scaled = scaled_edges(hot_gather, radial[0], features, tile)
    own_cols = lax.dynamic_slice_in_dim(all_atoms, (me_edge % chips) * depth, depth, 1).T

    blocks = []
    for h in range(len(parts)):
        total = merged[h * systems] + (hot_token[0, 0] if h == 0 else 0.0)
        for k in range(1, systems):
            total = total + across(merged[h * systems + k], k).astype(F32)
        held = total.astype(BF16)
        for k in range(chips):
            if k:
                held = shift(held, 1)
            blocks += [held, swap(held)]

    *halves, weight = edge_sums(
        chips, parts, place, hot_gather, hot_sum, radial[0], scaled, all_atoms, blocks, tile
    )

    def slots(i):
        kept, other = halves[i], swap(halves[3 + i])
        cut = lambda x, k: x[k * own : (k + 1) * own]
        return [cut(kept, k) + cut(other, k).astype(F32) for k in range(chips)]

    def ring_sum(terms):
        total = terms[1 % chips]
        for t in range(1, chips):
            total = shift(total.astype(BF16), 1).astype(F32) + terms[(t + 1) % chips]
        return total

    sums = [ring_sum(slots(i)).astype(BF16) for i in range(2)]

    def half_for(k):
        return jnp.where((chip + k) % chips < chips // 2, sums[0], sums[1])

    picked = both_cores([half_for(0)] + [shift(half_for(k), k) for k in range(1, chips)])
    grads = merged_grads(own_cols, picked, parts)

    all_grads = []
    for h in range(len(parts)):
        send = grads[2 * h + 1]
        all_grads += [grads[2 * h]] + [across(send, k) for k in range(1, systems)]
    expert_grad = expert_grads(place, coef, all_grads, experts.shape, parts)

    node = slots(2)
    total = node[0]
    for k in range(1, chips):
        total = total + shift(after(node[k].astype(BF16), *picked), chips - k).astype(F32)

    over = (((1,), (1,)), ((), ()))
    atom_grad = lax.dot_general(sums[0], weight[:width], over, preferred_element_type=F32)
    atom_grad = atom_grad + lax.dot_general(
        sums[1], weight[width:], over, preferred_element_type=F32
    )
    return total.astype(BF16)[None], atom_grad[None], expert_grad


def solution(mesh):
    placed = P("sys", "edge", None)
    return jax.shard_map(
        functools.partial(shards, mesh.shape["sys"], mesh.shape["edge"]),
        mesh=mesh,
        in_specs=(placed, placed, placed, placed, P(), P("sys", "edge"), P("sys", "edge")),
        out_specs=(placed, placed, placed),
        check_vma=False,
    )
```

```python
import functools

import jax
import jax.numpy as jnp
from jax import lax
from jax.experimental import pallas as pl
from jax.experimental.pallas import tpu as pltpu
from jax.sharding import PartitionSpec as P

F32 = jnp.float32
BF16 = jnp.bfloat16
LARGE = 60 << 20
SMALL = 24 << 20
STEP = 16


def whole_vmem():
    return pl.BlockSpec(memory_space=pltpu.VMEM)


def in_hbm():
    return pl.BlockSpec(memory_space=pltpu.HBM)


def whole_smem():
    return pl.BlockSpec(memory_space=pltpu.SMEM)


def params(limit=LARGE):
    return pltpu.CompilerParams(vmem_limit_bytes=limit)


def row_parts(depth):
    first = -(-depth // (2 * STEP)) * STEP
    return [(0, first), (first, depth - first)]


def merge_kernel(lo, pairs, place_ref, coef_ref, experts_ref, *refs):
    systems, count = coef_ref.shape[0], experts_ref.shape[0]
    pair_refs, part_refs = refs[:pairs], refs[-systems - 3 : -3]
    held_ref, sem, pair_sems = refs[-3:]
    me = place_ref[0]
    size, width = part_refs[0].shape
    load = pltpu.make_async_copy(experts_ref.at[:, pl.ds(lo, size), :], held_ref, sem)
    load.start()
    joins = []
    if pairs:
        both_ref = refs[-systems - 4]
        for i, ref in enumerate(pair_refs[:2]):
            joins.append(pltpu.make_async_copy(ref.at[0], both_ref.at[i], pair_sems.at[i]))
            joins[-1].start()
    scales = [[coef_ref[me ^ k, me * count + e] for e in range(count)] for k in range(systems)]
    load.wait()

    @pl.loop(0, size // STEP)
    def _(i):
        at = pl.ds(pl.multiple_of(i * STEP, STEP), STEP)
        for col in range(0, width, 128):
            cols = slice(col, min(col + 128, width))
            loaded = [held_ref[e, at, cols].astype(F32) for e in range(count)]
            for k in range(systems):
                total = scales[k][0] * loaded[0]
                for e in range(1, count):
                    total = total + scales[k][e] * loaded[e]
                part_refs[k][at, cols] = total.astype(part_refs[k].dtype)

    for join in joins:
        join.wait()


def merge_part(place, coef, experts, systems, part, joined=()):
    count, _, width = experts.shape
    lo, size = part
    outs = [((2, *joined[0].shape[1:]), BF16)] if joined else []
    outs += [((size, width), BF16 if k else F32) for k in range(systems)]
    return pl.pallas_call(
        functools.partial(merge_kernel, lo, len(joined)),
        out_shape=[jax.ShapeDtypeStruct(*out) for out in outs],
        in_specs=[whole_smem(), whole_smem()] + [in_hbm()] * (1 + len(joined)),
        out_specs=([in_hbm()] if joined else []) + [whole_vmem()] * systems,
        scratch_shapes=[
            pltpu.VMEM((count, size, width), BF16),
            pltpu.SemaphoreType.DMA,
            pltpu.SemaphoreType.DMA((2,)),
        ],
        compiler_params=params(),
        name="merge_part",
    )(place, coef, experts, *joined)


def merged_grad_kernel(cols_ref, *refs):
    block_refs, grad_ref, sent_ref, sums_ref = refs[:-3], refs[-3], refs[-2], refs[-1]
    own = block_refs[0].shape[0]
    for i, ref in enumerate(block_refs):
        sums_ref[i * own : (i + 1) * own, :] = ref[...]
    grad = jnp.dot(cols_ref[...], sums_ref[...], preferred_element_type=F32)
    grad_ref[...] = grad
    sent_ref[...] = grad.astype(BF16)


def merged_grads(cols, blocks):
    own, width = blocks[0].shape
    return pl.pallas_call(
        merged_grad_kernel,
        out_shape=[jax.ShapeDtypeStruct((cols.shape[0], width), kind) for kind in (F32, BF16)],
        in_specs=[whole_vmem()] * (1 + len(blocks)),
        out_specs=[whole_vmem()] * 2,
        scratch_shapes=[pltpu.VMEM((own * len(blocks), width), BF16)],
        compiler_params=params(SMALL),
        name="merged_grads",
    )(cols, *blocks)


def expert_kernel(parts, place_ref, coef_ref, *refs):
    grad_refs, out_ref, held_ref, sems = refs[:-3], refs[-3], refs[-2], refs[-1]
    me = place_ref[0]
    count, _, width = out_ref.shape
    systems = coef_ref.shape[0]
    copies = []
    scales = [[coef_ref[me ^ k, me * count + e] for e in range(count)] for k in range(systems)]
    for h, (lo, size) in enumerate(parts):

        @pl.loop(0, size // STEP)
        def _(i):
            at = pl.ds(pl.multiple_of(lo + i * STEP, STEP), STEP)
            for col in range(0, width, 128):
                cols = slice(col, min(col + 128, width))
                grads = [ref[at, cols].astype(F32) for ref in grad_refs]
                for e in range(count):
                    total = scales[0][e] * grads[0]
                    for k in range(1, systems):
                        total = total + scales[k][e] * grads[k]
                    held_ref[e, at, cols] = total

        at = pl.ds(lo, size)
        copies.append(pltpu.make_async_copy(held_ref.at[:, at, :], out_ref.at[:, at, :], sems.at[h]))
        copies[-1].start()
    for copy in copies:
        copy.wait()


def expert_grads(place, coef, grads, shape, parts):
    return pl.pallas_call(
        functools.partial(expert_kernel, parts),
        out_shape=jax.ShapeDtypeStruct(shape, F32),
        in_specs=[whole_smem(), whole_smem()] + [whole_vmem()] * len(grads),
        out_specs=in_hbm(),
        scratch_shapes=[pltpu.VMEM(shape, F32), pltpu.SemaphoreType.DMA((len(parts),))],
        compiler_params=params(SMALL),
        name="expert_grads",
    )(place, coef, *grads)


def hot_kernel(cols_ref, rows_ref, across_ref, down_ref, _, gather_ref, sum_ref, token_ref):
    atoms = down_ref.shape[0]

    def hot(same):
        return jnp.where(same, 1.0, 0.0).astype(BF16)

    for i in range(2):
        at = slice(i * atoms, (i + 1) * atoms)
        gather_ref[:, at] = hot(cols_ref[:, i : i + 1] == across_ref[...])
        sum_ref[at, :] = hot(down_ref[...] == rows_ref[i : i + 1, :])
    token_ref[...] = jnp.zeros_like(token_ref)


def hot_ends(cols, rows, order, earlier, tile):
    edges, atoms = cols.shape[0], order.shape[0]
    fixed = lambda *shape: pl.BlockSpec(shape, lambda i: (0, 0))
    return pl.pallas_call(
        hot_kernel,
        grid=(edges // tile,),
        out_shape=[
            jax.ShapeDtypeStruct((edges, 2 * atoms), BF16),
            jax.ShapeDtypeStruct((2 * atoms, edges), BF16),
            jax.ShapeDtypeStruct((8, 128), F32),
        ],
        in_specs=[
            pl.BlockSpec((tile, 2), lambda i: (i, 0)),
            pl.BlockSpec((2, tile), lambda i: (0, i)),
            fixed(1, atoms),
            fixed(atoms, 1),
            in_hbm(),
        ],
        out_specs=[
            pl.BlockSpec((tile, 2 * atoms), lambda i: (i, 0)),
            pl.BlockSpec((2 * atoms, tile), lambda i: (0, i)),
            fixed(8, 128),
        ],
        compiler_params=params(),
        cost_estimate=pl.CostEstimate(
            flops=16 * edges * atoms, bytes_accessed=8 * edges * atoms, transcendentals=0
        ),
        name="hot_ends",
    )(cols, rows, order[None, :], order[:, None], earlier)


def scale_kernel(slots, gather_ref, radial_ref, *refs):
    block_refs = refs[:slots]
    atoms_out, scaled_ref, token_ref, atoms_ref, cot_ref, sems = refs[slots:]
    step = pl.program_id(0)
    own = block_refs[0].shape[1]
    store = pltpu.make_async_copy(atoms_ref, atoms_out, sems.at[2 * slots])

    @pl.when(step == 0)
    def _():
        loads = []
        for k, ref in enumerate(block_refs):
            at = pl.ds(k * own, own)
            for i, to in enumerate((atoms_ref, cot_ref)):
                loads.append(pltpu.make_async_copy(ref.at[i], to.at[at], sems.at[2 * k + i]))
                loads[-1].start()
        for load in loads:
            load.wait()
        store.start()

    cot = jnp.dot(gather_ref[...], cot_ref[...], preferred_element_type=F32)
    scaled_ref[...] = (cot * radial_ref[...].astype(F32)).astype(BF16)
    token_ref[...] = jnp.zeros_like(token_ref)

    @pl.when(step == pl.num_programs(0) - 1)
    def _():
        store.wait()


def scaled_edges(hot_gather, radial, blocks, tile):
    edges, width = radial.shape
    atoms = hot_gather.shape[1] // 2
    slots = len(blocks)
    return pl.pallas_call(
        functools.partial(scale_kernel, slots),
        grid=(edges // tile,),
        out_shape=[
            jax.ShapeDtypeStruct((atoms, width), BF16),
            jax.ShapeDtypeStruct((edges, width), BF16),
            jax.ShapeDtypeStruct((8, 128), F32),
        ],
        in_specs=[
            pl.BlockSpec((tile, atoms), lambda i: (i, 1)),
            pl.BlockSpec((tile, width), lambda i: (i, 0)),
        ]
        + [in_hbm()] * slots,
        out_specs=[
            in_hbm(),
            pl.BlockSpec((tile, width), lambda i: (i, 0)),
            pl.BlockSpec((8, 128), lambda i: (0, 0)),
        ],
        scratch_shapes=[
            pltpu.VMEM((atoms, width), BF16),
            pltpu.VMEM((atoms, width), BF16),
            pltpu.SemaphoreType.DMA((2 * slots + 1,)),
        ],
        compiler_params=params(),
        cost_estimate=pl.CostEstimate(
            flops=2 * atoms * width * edges, bytes_accessed=6 * edges * width, transcendentals=0
        ),
        name="scaled_edges",
    )(hot_gather, radial, *blocks)


def edge_kernel(
    chips, parts, place_ref, gather_ref, sum_ref, radial_ref, scaled_ref, atoms_hbm, _, *refs
):
    blocks = 2 * chips * len(parts)
    block_refs, kept_refs, sent_refs = refs[:blocks], refs[blocks : blocks + 3], refs[blocks + 3 : blocks + 6]
    weight_out, atoms_ref, weight_ref, proj_ref, value_ref, acc_ref, sem, sems = refs[blocks + 6 :]
    step, last = pl.program_id(0), pl.num_programs(0) - 1
    atoms, width_in = atoms_ref.shape
    width = radial_ref.shape[1]
    store = pltpu.make_async_copy(weight_ref, weight_out, sem)

    def messages():
        pre = jnp.dot(gather_ref[...], proj_ref[...], preferred_element_type=F32)
        sigma = 0.5 + 0.5 * jnp.tanh(0.5 * pre)
        silu = pre * sigma
        slope = sigma + silu * (1.0 - sigma)
        to = lax.rem(step, 2)
        value_ref[to, :, :width] = (scaled_ref[...].astype(F32) * slope).astype(BF16)
        value_ref[to, :, width:] = (silu * radial_ref[...].astype(F32)).astype(BF16)

    def add_up():
        at = lax.rem(step + 1, 2)
        acc_ref[:, :width] += jnp.dot(
            sum_ref[:atoms, :], value_ref[at, :, :width], preferred_element_type=F32
        )
        acc_ref[:, width:] += jnp.dot(
            sum_ref[atoms:, :], value_ref[at], preferred_element_type=F32
        )

    @pl.when(step == 0)
    def _():
        chip, core = place_ref[1], place_ref[2]
        depth = sum(size for _, size in parts)
        loads = [pltpu.make_async_copy(atoms_hbm, atoms_ref, sems.at[blocks])]
        for h, (lo, size) in enumerate(parts):
            for k in range(chips):
                source = lax.rem(chip - k + chips, chips)
                for other in range(2):
                    device = 2 * source + (core if other == 0 else 1 - core)
                    at = pl.ds(pl.multiple_of(device * depth + lo, STEP), size)
                    i = (h * chips + k) * 2 + other
                    loads.append(
                        pltpu.make_async_copy(block_refs[i], weight_ref.at[at], sems.at[i])
                    )
        for load in loads:
            load.start()
        acc_ref[...] = jnp.zeros_like(acc_ref)
        for load in loads:
            load.wait()
        store.start()
        for half in range(2):
            proj_ref[half * atoms : (half + 1) * atoms, :] = jnp.dot(
                atoms_ref[...],
                weight_ref[half * width_in : (half + 1) * width_in, :],
                preferred_element_type=F32,
            ).astype(BF16)
        messages()

    @pl.when(jnp.logical_and(step > 0, step < last))
    def _():
        add_up()
        messages()

    @pl.when(step == last)
    def _():
        add_up()
        half = atoms // 2
        for i in range(3):
            cols = slice(i * width, (i + 1) * width)
            kept_refs[i][...] = acc_ref[:half, cols]
            sent_refs[i][...] = acc_ref[half:, cols].astype(BF16)
        store.wait()


def edge_sums(chips, parts, place, gather, sums, radial, scaled, atoms, earlier, blocks, tile):
    edges, width = radial.shape
    count, width_in = atoms.shape
    flops = 2 * count * width * (2 * width_in + 5 * edges)
    fixed = lambda *shape: pl.BlockSpec(shape, lambda i: (0,) * len(shape))
    halves = [((count // 2, width), F32)] * 3 + [((count // 2, width), BF16)] * 3
    outs = halves + [((2 * width_in, width), BF16)]
    steps = edges // tile
    return pl.pallas_call(
        functools.partial(edge_kernel, chips, parts),
        grid=(steps + 1,),
        out_shape=[jax.ShapeDtypeStruct(shape, kind) for shape, kind in outs],
        in_specs=[
            whole_smem(),
            pl.BlockSpec((tile, 2 * count), lambda i: (jnp.minimum(i, steps - 1), 0)),
            pl.BlockSpec((2 * count, tile), lambda i: (0, jnp.maximum(i - 1, 0))),
            pl.BlockSpec((tile, width), lambda i: (jnp.minimum(i, steps - 1), 0)),
            pl.BlockSpec((tile, width), lambda i: (jnp.minimum(i, steps - 1), 0)),
        ]
        + [in_hbm()] * (2 + len(blocks)),
        out_specs=[fixed(*shape) for shape, _ in halves] + [in_hbm()],
        scratch_shapes=[
            pltpu.VMEM((count, width_in), BF16),
            pltpu.VMEM((2 * width_in, width), BF16),
            pltpu.VMEM((2 * count, width), BF16),
            pltpu.VMEM((2, tile, 2 * width), BF16),
            pltpu.VMEM((count, 3 * width), F32),
            pltpu.SemaphoreType.DMA,
            pltpu.SemaphoreType.DMA((len(blocks) + 1,)),
        ],
        compiler_params=params(),
        cost_estimate=pl.CostEstimate(
            flops=flops,
            bytes_accessed=4 * edges * width + 8 * edges * count,
            transcendentals=edges * width,
        ),
        name="edge_sums",
    )(place, gather, sums, radial, scaled, atoms, earlier, *blocks)


def after(x, *others):
    return lax.optimization_barrier((x, *others))[0]


def shards(systems, ways, atoms, cotangent, experts, radial, coef, source, target):
    chips = ways // 2
    me_sys = lax.axis_index("sys")
    me_edge = lax.axis_index("edge")
    chip, core = me_edge // 2, me_edge % 2
    place = jnp.stack([me_sys, chip, core]).astype(jnp.int32)
    _, depth, width = experts.shape
    own = atoms.shape[1]
    tile = min(512, radial.shape[1])
    parts = row_parts(depth)

    def across(x, k):
        return lax.ppermute(x, "sys", [(s, s ^ k) for s in range(systems)])

    def swap(x):
        return lax.ppermute(x, "edge", [(e, e ^ 1) for e in range(ways)])

    def shift(x, k):
        return lax.ppermute(x, "edge", [(e, (e + 2 * k) % ways) for e in range(ways)])

    def both_cores(blocks):
        return blocks + [swap(block) for block in blocks]

    merged = [merge_part(place, coef, experts, systems, parts[0])]
    joined = (atoms, cotangent, merged[0][0])
    features, *second = merge_part(place, coef, experts, systems, parts[1], joined)
    merged.append(second)
    features = both_cores([features] + [shift(features, k) for k in range(1, chips)])

    at = jnp.arange(ways * own, dtype=jnp.int32)
    side, back, offset = at // (chips * own), at // own % chips, at % own
    order = (2 * ((chip - back + chips) % chips) + (core ^ side)) * own + offset
    ends = jnp.concatenate([source, target])
    hot_gather, hot_sum, hot_token = hot_ends(ends.T, ends, order, second[0], tile)
    all_atoms, scaled, scaled_token = scaled_edges(hot_gather, radial[0], features, tile)
    own_cols = lax.dynamic_slice_in_dim(all_atoms, (me_edge % chips) * depth, depth, 1).T

    blocks = []
    for h in range(len(parts)):
        total = merged[h][0] + (hot_token[0, 0] if h == 0 else 0.0)
        for k in range(1, systems):
            total = total + across(merged[h][k], k).astype(F32)
        held = total.astype(BF16)
        for k in range(chips):
            if h and k == chips - 1:
                held = held + scaled_token[0, 0].astype(BF16)
            if k:
                held = shift(held, 1)
            blocks += [held, swap(held)]

    *halves, weight = edge_sums(
        chips, parts, place, hot_gather, hot_sum, radial[0], scaled, all_atoms, own_cols, blocks, tile
    )

    def slots(i):
        kept, other = halves[i], swap(halves[3 + i])
        cut = lambda x, k: x[k * own : (k + 1) * own]
        return [cut(kept, k) + cut(other, k).astype(F32) for k in range(chips)]

    def ring_sum(terms):
        total = terms[1 % chips]
        for t in range(1, chips):
            total = shift(total.astype(BF16), 1).astype(F32) + terms[(t + 1) % chips]
        return total

    sums = [ring_sum(slots(i)).astype(BF16) for i in range(2)]

    def half_for(k):
        return jnp.where((chip + k) % chips < chips // 2, sums[0], sums[1])

    picked = both_cores([half_for(0)] + [shift(half_for(k), k) for k in range(1, chips)])
    grad, send = merged_grads(own_cols, picked)

    grads = [grad] + [across(send, k) for k in range(1, systems)]
    expert_grad = expert_grads(place, coef, grads, experts.shape, parts)

    node = slots(2)
    total = node[0]
    for k in range(1, chips):
        total = total + shift(after(node[k].astype(BF16), *picked), chips - k).astype(F32)

    over = (((1,), (1,)), ((), ()))
    atom_grad = lax.dot_general(sums[0], weight[:width], over, preferred_element_type=F32)
    atom_grad = atom_grad + lax.dot_general(
        sums[1], weight[width:], over, preferred_element_type=F32
    )
    return total.astype(BF16)[None], atom_grad[None], expert_grad


def solution(mesh):
    placed = P("sys", "edge", None)
    return jax.shard_map(
        functools.partial(shards, mesh.shape["sys"], mesh.shape["edge"]),
        mesh=mesh,
        in_specs=(placed, placed, placed, placed, P(), P("sys", "edge"), P("sys", "edge")),
        out_specs=(placed, placed, placed),
        check_vma=False,
    )
```

```python
import functools

import jax
import jax.numpy as jnp
from jax import lax
from jax.experimental import pallas as pl
from jax.experimental.pallas import tpu as pltpu
from jax.sharding import PartitionSpec as P

F32 = jnp.float32
BF16 = jnp.bfloat16
LARGE = 60 << 20
SMALL = 24 << 20
STEP = 16


def whole_vmem():
    return pl.BlockSpec(memory_space=pltpu.VMEM)


def in_hbm():
    return pl.BlockSpec(memory_space=pltpu.HBM)


def whole_smem():
    return pl.BlockSpec(memory_space=pltpu.SMEM)


def params(limit=LARGE):
    return pltpu.CompilerParams(vmem_limit_bytes=limit)


def row_parts(depth):
    first = -(-depth // (2 * STEP)) * STEP
    return [(0, first), (first, depth - first)]


def merge_kernel(parts, place_ref, coef_ref, experts_ref, *refs):
    part_refs, held_ref, sems = refs[:-2], refs[-2], refs[-1]
    systems, count = coef_ref.shape[0], experts_ref.shape[0]
    width = experts_ref.shape[2]
    me = place_ref[0]
    loads = []
    for h, (lo, size) in enumerate(parts):
        at = pl.ds(lo, size)
        loads.append(
            pltpu.make_async_copy(experts_ref.at[:, at, :], held_ref.at[:, at, :], sems.at[h])
        )
        loads[-1].start()
    scales = [[coef_ref[me ^ k, me * count + e] for e in range(count)] for k in range(systems)]
    for h, (lo, size) in enumerate(parts):
        loads[h].wait()

        @pl.loop(0, size // STEP)
        def _(i):
            at = pl.ds(pl.multiple_of(lo + i * STEP, STEP), STEP)
            for col in range(0, width, 128):
                cols = slice(col, min(col + 128, width))
                loaded = [held_ref[e, at, cols].astype(F32) for e in range(count)]
                for k in range(systems):
                    total = scales[k][0] * loaded[0]
                    for e in range(1, count):
                        total = total + scales[k][e] * loaded[e]
                    part_refs[k][at, cols] = total.astype(part_refs[k].dtype)


def merge_parts(place, coef, experts, parts):
    _, depth, width = experts.shape
    systems = coef.shape[0]
    return pl.pallas_call(
        functools.partial(merge_kernel, parts),
        out_shape=[
            jax.ShapeDtypeStruct((depth, width), BF16 if k else F32) for k in range(systems)
        ],
        in_specs=[whole_smem(), whole_smem(), in_hbm()],
        out_specs=[whole_vmem()] * systems,
        scratch_shapes=[
            pltpu.VMEM(experts.shape, BF16),
            pltpu.SemaphoreType.DMA((len(parts),)),
        ],
        compiler_params=params(),
        name="merge_parts",
    )(place, coef, experts)


def merged_grad_kernel(place_ref, cols_ref, *refs):
    block_refs, grad_ref, sent_ref, token_ref, sums_ref = refs[:-4], *refs[-4:]
    size = block_refs[0].shape[0]
    pieces = len(block_refs) // 2
    for i, ref in enumerate(block_refs):
        piece = lax.rem(place_ref[1] + pieces - i % pieces, pieces)
        at = pl.ds(pl.multiple_of((i // pieces * pieces + piece) * size, size), size)
        sums_ref[at, :] = ref[...]
    grad = jnp.dot(cols_ref[...], sums_ref[...], preferred_element_type=F32)
    grad_ref[...] = grad
    sent_ref[...] = grad.astype(BF16)
    token_ref[...] = jnp.zeros_like(token_ref)


def merged_grads(place, cols, blocks):
    size, width = blocks[0].shape
    return pl.pallas_call(
        merged_grad_kernel,
        out_shape=[jax.ShapeDtypeStruct((cols.shape[0], width), kind) for kind in (F32, BF16)]
        + [jax.ShapeDtypeStruct((8, 128), F32)],
        in_specs=[whole_smem()] + [whole_vmem()] * (1 + len(blocks)),
        out_specs=[whole_vmem()] * 3,
        scratch_shapes=[pltpu.VMEM((size * len(blocks), width), BF16)],
        compiler_params=params(SMALL),
        name="merged_grads",
    )(place, cols, *blocks)


def atom_grad_kernel(chips, place_ref, sums_ref, weight_hbm, first_ref, second_ref, weight_ref, sem):
    half = place_ref[1] // (chips // 2)
    rows, own = weight_ref.shape[0], first_ref.shape[0]
    at = pl.ds(pl.multiple_of(half * rows, rows), rows)
    load = pltpu.make_async_copy(weight_hbm.at[at], weight_ref, sem)
    load.start()
    load.wait()
    for side, ref in ((half, first_ref), (1 - half, second_ref)):
        block = sums_ref[pl.ds(pl.multiple_of(side * own, own), own), :]
        ref[...] = lax.dot_general(
            block, weight_ref[...], (((1,), (1,)), ((), ())), preferred_element_type=F32
        ).astype(BF16)


def atom_grads(chips, place, sums, weight):
    own, width = sums.shape[0] // 2, sums.shape[1]
    rows = weight.shape[0] // 2
    return pl.pallas_call(
        functools.partial(atom_grad_kernel, chips),
        out_shape=[jax.ShapeDtypeStruct((own, rows), BF16)] * 2,
        in_specs=[whole_smem(), whole_vmem(), in_hbm()],
        out_specs=[whole_vmem()] * 2,
        scratch_shapes=[pltpu.VMEM((rows, width), BF16), pltpu.SemaphoreType.DMA],
        compiler_params=params(SMALL),
        cost_estimate=pl.CostEstimate(
            flops=4 * own * rows * width, bytes_accessed=2 * rows * width, transcendentals=0
        ),
        name="atom_grads",
    )(place, sums, weight)


def expert_kernel(parts, place_ref, coef_ref, *refs):
    grad_refs, out_ref, held_ref, sems = refs[:-3], refs[-3], refs[-2], refs[-1]
    me = place_ref[0]
    count, _, width = out_ref.shape
    systems = coef_ref.shape[0]
    copies = []
    scales = [[coef_ref[me ^ k, me * count + e] for e in range(count)] for k in range(systems)]
    for h, (lo, size) in enumerate(parts):

        @pl.loop(0, size // STEP)
        def _(i):
            at = pl.ds(pl.multiple_of(lo + i * STEP, STEP), STEP)
            for col in range(0, width, 128):
                cols = slice(col, min(col + 128, width))
                grads = [ref[at, cols].astype(F32) for ref in grad_refs]
                for e in range(count):
                    total = scales[0][e] * grads[0]
                    for k in range(1, systems):
                        total = total + scales[k][e] * grads[k]
                    held_ref[e, at, cols] = total

        at = pl.ds(lo, size)
        copies.append(pltpu.make_async_copy(held_ref.at[:, at, :], out_ref.at[:, at, :], sems.at[h]))
        copies[-1].start()
    for copy in copies:
        copy.wait()


def expert_grads(place, coef, grads, shape, parts):
    return pl.pallas_call(
        functools.partial(expert_kernel, parts),
        out_shape=jax.ShapeDtypeStruct(shape, F32),
        in_specs=[whole_smem(), whole_smem()] + [whole_vmem()] * len(grads),
        out_specs=in_hbm(),
        scratch_shapes=[pltpu.VMEM(shape, F32), pltpu.SemaphoreType.DMA((len(parts),))],
        compiler_params=params(SMALL),
        name="expert_grads",
    )(place, coef, *grads)


def hot_kernel(cols_ref, rows_ref, across_ref, down_ref, _, gather_ref, sum_ref, token_ref):
    atoms = down_ref.shape[0]

    def hot(same):
        return jnp.where(same, 1.0, 0.0).astype(BF16)

    for i in range(2):
        at = slice(i * atoms, (i + 1) * atoms)
        gather_ref[:, at] = hot(cols_ref[:, i : i + 1] == across_ref[...])
        sum_ref[at, :] = hot(down_ref[...] == rows_ref[i : i + 1, :])
    token_ref[...] = jnp.zeros_like(token_ref)


def hot_ends(cols, rows, order, earlier, tile):
    edges, atoms = cols.shape[0], order.shape[0]
    fixed = lambda *shape: pl.BlockSpec(shape, lambda i: (0, 0))
    return pl.pallas_call(
        hot_kernel,
        grid=(edges // tile,),
        out_shape=[
            jax.ShapeDtypeStruct((edges, 2 * atoms), BF16),
            jax.ShapeDtypeStruct((2 * atoms, edges), BF16),
            jax.ShapeDtypeStruct((8, 128), F32),
        ],
        in_specs=[
            pl.BlockSpec((tile, 2), lambda i: (i, 0)),
            pl.BlockSpec((2, tile), lambda i: (0, i)),
            fixed(1, atoms),
            fixed(atoms, 1),
            in_hbm(),
        ],
        out_specs=[
            pl.BlockSpec((tile, 2 * atoms), lambda i: (i, 0)),
            pl.BlockSpec((2 * atoms, tile), lambda i: (0, i)),
            fixed(8, 128),
        ],
        compiler_params=params(),
        cost_estimate=pl.CostEstimate(
            flops=16 * edges * atoms, bytes_accessed=8 * edges * atoms, transcendentals=0
        ),
        name="hot_ends",
    )(cols, rows, order[None, :], order[:, None], earlier)


def scale_kernel(slots, place_ref, gather_ref, radial_ref, *refs):
    block_refs = refs[:slots]
    atoms_out, scaled_ref, token_ref, atoms_ref, cot_ref, sems = refs[slots:]
    step = pl.program_id(0)
    own = block_refs[0].shape[1]
    store = pltpu.make_async_copy(atoms_ref, atoms_out, sems.at[2 * slots])

    @pl.when(step == 0)
    def _():
        loads = []
        chips = slots // 2
        for k, ref in enumerate(block_refs):
            back = lax.rem(place_ref[1] - k % chips + chips, chips)
            at = pl.ds(pl.multiple_of((k // chips * chips + back) * own, own), own)
            for i, to in enumerate((atoms_ref, cot_ref)):
                loads.append(pltpu.make_async_copy(ref.at[i], to.at[at], sems.at[2 * k + i]))
                loads[-1].start()
        for load in loads:
            load.wait()
        store.start()

    cot = jnp.dot(gather_ref[...], cot_ref[...], preferred_element_type=F32)
    scaled_ref[...] = (cot * radial_ref[...].astype(F32)).astype(BF16)
    token_ref[...] = jnp.zeros_like(token_ref)

    @pl.when(step == pl.num_programs(0) - 1)
    def _():
        store.wait()


def scaled_edges(place, hot_gather, radial, blocks, tile):
    edges, width = radial.shape
    atoms = hot_gather.shape[1] // 2
    slots = len(blocks)
    return pl.pallas_call(
        functools.partial(scale_kernel, slots),
        grid=(edges // tile,),
        out_shape=[
            jax.ShapeDtypeStruct((atoms, width), BF16),
            jax.ShapeDtypeStruct((edges, width), BF16),
            jax.ShapeDtypeStruct((8, 128), F32),
        ],
        in_specs=[
            whole_smem(),
            pl.BlockSpec((tile, atoms), lambda i: (i, 1)),
            pl.BlockSpec((tile, width), lambda i: (i, 0)),
        ]
        + [in_hbm()] * slots,
        out_specs=[
            in_hbm(),
            pl.BlockSpec((tile, width), lambda i: (i, 0)),
            pl.BlockSpec((8, 128), lambda i: (0, 0)),
        ],
        scratch_shapes=[
            pltpu.VMEM((atoms, width), BF16),
            pltpu.VMEM((atoms, width), BF16),
            pltpu.SemaphoreType.DMA((2 * slots + 1,)),
        ],
        compiler_params=params(),
        cost_estimate=pl.CostEstimate(
            flops=2 * atoms * width * edges, bytes_accessed=6 * edges * width, transcendentals=0
        ),
        name="scaled_edges",
    )(place, hot_gather, radial, *blocks)


def edge_kernel(
    chips, place_ref, gather_ref, sum_ref, radial_ref, scaled_ref, atoms_hbm, _, *refs
):
    blocks = 2 * chips
    block_refs = refs[:blocks]
    kept_ref, sent_ref, node_kept_ref, node_sent_ref, weight_out = refs[blocks : blocks + 5]
    atoms_ref, weight_ref, proj_ref, value_ref, acc_ref, sem, sems = refs[blocks + 5 :]
    step, last = pl.program_id(0), pl.num_programs(0) - 1
    atoms, width_in = atoms_ref.shape
    width = radial_ref.shape[1]
    store = pltpu.make_async_copy(weight_ref, weight_out, sem)

    def messages():
        pre = jnp.dot(gather_ref[...], proj_ref[...], preferred_element_type=F32)
        sigma = 0.5 + 0.5 * jnp.tanh(0.5 * pre)
        silu = pre * sigma
        slope = sigma + silu * (1.0 - sigma)
        to = lax.rem(step, 2)
        value_ref[to, :, :width] = (scaled_ref[...].astype(F32) * slope).astype(BF16)
        value_ref[to, :, width:] = (silu * radial_ref[...].astype(F32)).astype(BF16)

    def add_up():
        at = lax.rem(step + 1, 2)
        acc_ref[:, :width] += jnp.dot(
            sum_ref[:atoms, :], value_ref[at, :, :width], preferred_element_type=F32
        )
        acc_ref[:, width:] += jnp.dot(
            sum_ref[atoms:, :], value_ref[at], preferred_element_type=F32
        )

    @pl.when(step == 0)
    def _():
        chip, core = place_ref[1], place_ref[2]
        depth = block_refs[0].shape[0]
        loads = [pltpu.make_async_copy(atoms_hbm, atoms_ref, sems.at[blocks])]
        for i, ref in enumerate(block_refs):
            source = lax.rem(chip - i // 2 + chips, chips)
            device = 2 * source + (1 - core if i % 2 else core)
            at = pl.ds(pl.multiple_of(device * depth, STEP), depth)
            loads.append(pltpu.make_async_copy(ref, weight_ref.at[at], sems.at[i]))
        for load in loads:
            load.start()
        acc_ref[...] = jnp.zeros_like(acc_ref)
        for load in loads:
            load.wait()
        store.start()
        for half in range(2):
            proj_ref[half * atoms : (half + 1) * atoms, :] = jnp.dot(
                atoms_ref[...],
                weight_ref[half * width_in : (half + 1) * width_in, :],
                preferred_element_type=F32,
            ).astype(BF16)
        messages()

    @pl.when(jnp.logical_and(step > 0, step < last))
    def _():
        add_up()
        messages()

    @pl.when(step == last)
    def _():
        add_up()
        side = atoms // 2
        for k in range(chips):
            chip = lax.rem(place_ref[1] + k, chips)
            cols = pl.ds(pl.multiple_of(chip // (chips // 2) * width, width), width)
            size = kept_ref.shape[1]
            row = lax.rem(chip, chips // 2) * size
            kept_ref[k] = acc_ref[pl.ds(pl.multiple_of(row, size), size), cols]
            sent_ref[k] = acc_ref[pl.ds(pl.multiple_of(side + row, size), size), cols].astype(BF16)
            cols = slice(2 * width, 3 * width)
            size = node_kept_ref.shape[1]
            row = chip * size
            node_kept_ref[k] = acc_ref[pl.ds(pl.multiple_of(row, size), size), cols]
            node_sent_ref[k] = acc_ref[pl.ds(pl.multiple_of(side + row, size), size), cols].astype(
                BF16
            )
        store.wait()


def edge_sums(chips, place, gather, sums, radial, scaled, atoms, earlier, blocks, tile):
    edges, width = radial.shape
    count, width_in = atoms.shape
    flops = 2 * count * width * (2 * width_in + 5 * edges)
    fixed = lambda *shape: pl.BlockSpec(shape, lambda i: (0,) * len(shape))
    sums_shape = (chips, count // chips, width)
    node_shape = (chips, count // 2 // chips, width)
    halves = [(sums_shape, F32), (sums_shape, BF16), (node_shape, F32), (node_shape, BF16)]
    outs = halves + [((2 * width_in, width), BF16)]
    steps = edges // tile
    return pl.pallas_call(
        functools.partial(edge_kernel, chips),
        grid=(steps + 1,),
        out_shape=[jax.ShapeDtypeStruct(shape, kind) for shape, kind in outs],
        in_specs=[
            whole_smem(),
            pl.BlockSpec((tile, 2 * count), lambda i: (jnp.minimum(i, steps - 1), 0)),
            pl.BlockSpec((2 * count, tile), lambda i: (0, jnp.maximum(i - 1, 0))),
            pl.BlockSpec((tile, width), lambda i: (jnp.minimum(i, steps - 1), 0)),
            pl.BlockSpec((tile, width), lambda i: (jnp.minimum(i, steps - 1), 0)),
        ]
        + [in_hbm()] * (2 + len(blocks)),
        out_specs=[fixed(*shape) for shape, _ in halves] + [in_hbm()],
        scratch_shapes=[
            pltpu.VMEM((count, width_in), BF16),
            pltpu.VMEM((2 * width_in, width), BF16),
            pltpu.VMEM((2 * count, width), BF16),
            pltpu.VMEM((2, tile, 2 * width), BF16),
            pltpu.VMEM((count, 3 * width), F32),
            pltpu.SemaphoreType.DMA,
            pltpu.SemaphoreType.DMA((len(blocks) + 1,)),
        ],
        compiler_params=params(),
        cost_estimate=pl.CostEstimate(
            flops=flops,
            bytes_accessed=4 * edges * width + 8 * edges * count,
            transcendentals=edges * width,
        ),
        name="edge_sums",
    )(place, gather, sums, radial, scaled, atoms, earlier, *blocks)


def shards(systems, ways, atoms, cotangent, experts, radial, coef, source, target):
    chips = ways // 2
    me_sys = lax.axis_index("sys")
    me_edge = lax.axis_index("edge")
    chip, core = me_edge // 2, me_edge % 2
    place = jnp.stack([me_sys, chip, core]).astype(jnp.int32)
    _, depth, width = experts.shape
    own = atoms.shape[1]
    tile = min(512, radial.shape[1])
    parts = row_parts(depth)

    def across(x, k):
        return lax.ppermute(x, "sys", [(s, s ^ k) for s in range(systems)])

    def swap(x):
        return lax.ppermute(x, "edge", [(e, e ^ 1) for e in range(ways)])

    def shift(x, k):
        return lax.ppermute(x, "edge", [(e, (e + 2 * k) % ways) for e in range(ways)])

    def both_cores(blocks):
        return blocks + [swap(block) for block in blocks]

    merged = merge_parts(place, coef, experts, parts)
    pair = jnp.concatenate([atoms, cotangent], axis=0)
    features = both_cores([pair] + [shift(pair, k) for k in range(1, chips)])

    at = jnp.arange(ways * own, dtype=jnp.int32)
    side, z, offset = at // (chips * own), at // own % chips, at % own
    order = (2 * z + (core ^ side)) * own + offset
    ends = jnp.concatenate([source, target])
    hot_gather, hot_sum, hot_token = hot_ends(ends.T, ends, order, pair, tile)
    all_atoms, scaled, scaled_token = scaled_edges(place, hot_gather, radial[0], features, tile)
    own_cols = lax.dynamic_slice_in_dim(all_atoms, (me_edge % chips) * depth, depth, 1).T

    total = merged[0] + hot_token[0, 0]
    for k in range(1, systems):
        total = total + across(merged[k], k).astype(F32)
    held = total.astype(BF16)
    blocks = []
    for k in range(chips):
        if k == chips - 1:
            held = held + scaled_token[0, 0].astype(BF16)
        if k:
            held = shift(held, 1)
        blocks += [held, swap(held)]

    kept, sent, node_kept, node_sent, weight = edge_sums(
        chips, place, hot_gather, hot_sum, radial[0], scaled, all_atoms, own_cols, blocks, tile
    )

    def reduce(kept, other, zero):
        terms = [kept[k] + other[k].astype(F32) + zero for k in range(chips)]
        total = terms[0]
        for k in range(1, chips):
            total = total + shift(terms[k].astype(BF16), k).astype(F32)
        return total.astype(BF16)

    shares = chips // 2
    sums = reduce(kept, swap(sent), 0.0)

    def share(x, j):
        to = [z // shares * shares + (z + j) % shares for z in range(chips)]
        return lax.ppermute(x, "edge", [(2 * z + c, 2 * to[z] + c) for z in range(chips) for c in range(2)])

    picked = both_cores([sums] + [share(sums, j) for j in range(1, shares)])
    grad, send, grad_token = merged_grads(place, own_cols, picked)
    grads = [grad] + [across(send, k) for k in range(1, systems)]
    expert_grad = expert_grads(place, coef, grads, experts.shape, parts)

    atom_grad = 0.0
    for flip, term in enumerate(atom_grads(chips, place, sums, weight)):
        to = [2 * (z % shares) + (z // shares ^ flip) for z in range(chips)]
        pairs = [(2 * z + c, 2 * to[z] + c) for z in range(chips) for c in range(2)]
        atom_grad = atom_grad + lax.ppermute(term, "edge", pairs).astype(F32)

    node = reduce(node_kept, swap(node_sent), grad_token[0, 0])
    return node[None], atom_grad[None], expert_grad


def solution(mesh):
    placed = P("sys", "edge", None)
    return jax.shard_map(
        functools.partial(shards, mesh.shape["sys"], mesh.shape["edge"]),
        mesh=mesh,
        in_specs=(placed, placed, placed, placed, P(), P("sys", "edge"), P("sys", "edge")),
        out_specs=(placed, placed, placed),
        check_vma=False,
    )
```

```python
import functools

import jax
import jax.numpy as jnp
from jax import lax
from jax.experimental import pallas as pl
from jax.experimental.pallas import tpu as pltpu
from jax.sharding import PartitionSpec as P

F32 = jnp.float32
BF16 = jnp.bfloat16
LARGE = 60 << 20
SMALL = 24 << 20
STEP = 16


def whole_vmem():
    return pl.BlockSpec(memory_space=pltpu.VMEM)


def in_hbm():
    return pl.BlockSpec(memory_space=pltpu.HBM)


def whole_smem():
    return pl.BlockSpec(memory_space=pltpu.SMEM)


def params(limit=LARGE):
    return pltpu.CompilerParams(vmem_limit_bytes=limit)


def row_parts(depth):
    first = -(-depth // (2 * STEP)) * STEP
    return [(0, first), (first, depth - first)]


def merge_kernel(parts, place_ref, coef_ref, experts_ref, *refs):
    part_refs, held_ref, sems = refs[:-2], refs[-2], refs[-1]
    systems, count = coef_ref.shape[0], experts_ref.shape[0]
    width = experts_ref.shape[2]
    me = place_ref[0]
    loads = []
    for h, (lo, size) in enumerate(parts):
        at = pl.ds(lo, size)
        loads.append(
            pltpu.make_async_copy(experts_ref.at[:, at, :], held_ref.at[:, at, :], sems.at[h])
        )
        loads[-1].start()
    scales = [[coef_ref[me ^ k, me * count + e] for e in range(count)] for k in range(systems)]
    for h, (lo, size) in enumerate(parts):
        loads[h].wait()

        @pl.loop(0, size // STEP)
        def _(i):
            at = pl.ds(pl.multiple_of(lo + i * STEP, STEP), STEP)
            for col in range(0, width, 128):
                cols = slice(col, min(col + 128, width))
                loaded = [held_ref[e, at, cols].astype(F32) for e in range(count)]
                for k in range(systems):
                    total = scales[k][0] * loaded[0]
                    for e in range(1, count):
                        total = total + scales[k][e] * loaded[e]
                    part_refs[k][at, cols] = total.astype(part_refs[k].dtype)


def merge_parts(place, coef, experts, parts):
    _, depth, width = experts.shape
    systems = coef.shape[0]
    return pl.pallas_call(
        functools.partial(merge_kernel, parts),
        out_shape=[
            jax.ShapeDtypeStruct((depth, width), BF16 if k else F32) for k in range(systems)
        ],
        in_specs=[whole_smem(), whole_smem(), in_hbm()],
        out_specs=[whole_vmem()] * systems,
        scratch_shapes=[
            pltpu.VMEM(experts.shape, BF16),
            pltpu.SemaphoreType.DMA((len(parts),)),
        ],
        compiler_params=params(),
        name="merge_parts",
    )(place, coef, experts)


def join_kernel(atoms_ref, cot_ref, _, both_ref):
    both_ref[0] = atoms_ref[0]
    both_ref[1] = cot_ref[0]


def join(atoms, cotangent, earlier):
    return pl.pallas_call(
        join_kernel,
        out_shape=jax.ShapeDtypeStruct((2, *atoms.shape[1:]), BF16),
        in_specs=[whole_vmem(), whole_vmem(), in_hbm()],
        out_specs=whole_vmem(),
        compiler_params=params(SMALL),
        name="join",
    )(atoms, cotangent, earlier)


def rows_kernel(count, *refs):
    out_ref = refs[-1]
    total = refs[0][...]
    for ref in refs[1:count]:
        total = total + ref[...].astype(F32)
    out_ref[...] = total.astype(BF16)


def weight_rows(parts, earlier):
    return pl.pallas_call(
        functools.partial(rows_kernel, len(parts)),
        out_shape=jax.ShapeDtypeStruct(parts[0].shape, BF16),
        in_specs=[whole_vmem()] * len(parts) + [in_hbm()] * len(earlier),
        out_specs=whole_vmem(),
        compiler_params=params(SMALL),
        name="weight_rows",
    )(*parts, *earlier)


def merged_grad_kernel(place_ref, cols_ref, *refs):
    block_refs, grad_ref, sent_ref, token_ref, sums_ref = refs[:-4], *refs[-4:]
    size = block_refs[0].shape[0]
    pieces = len(block_refs) // 2
    for i, ref in enumerate(block_refs):
        piece = lax.rem(place_ref[1] + pieces - i % pieces, pieces)
        at = pl.ds(pl.multiple_of((i // pieces * pieces + piece) * size, size), size)
        sums_ref[at, :] = ref[...]
    grad = jnp.dot(cols_ref[...], sums_ref[...], preferred_element_type=F32)
    grad_ref[...] = grad
    sent_ref[...] = grad.astype(BF16)
    token_ref[...] = jnp.zeros_like(token_ref)


def merged_grads(place, cols, blocks):
    size, width = blocks[0].shape
    return pl.pallas_call(
        merged_grad_kernel,
        out_shape=[jax.ShapeDtypeStruct((cols.shape[0], width), kind) for kind in (F32, BF16)]
        + [jax.ShapeDtypeStruct((1, width), F32)],
        in_specs=[whole_smem()] + [whole_vmem()] * (1 + len(blocks)),
        out_specs=[whole_vmem()] * 3,
        scratch_shapes=[pltpu.VMEM((size * len(blocks), width), BF16)],
        compiler_params=params(SMALL),
        name="merged_grads",
    )(place, cols, *blocks)


def atom_grad_kernel(
    chips, place_ref, sums_ref, weight_hbm, first_ref, second_ref, token_ref, weight_ref, sem
):
    half = place_ref[1] // (chips // 2)
    rows, own = weight_ref.shape[0], first_ref.shape[0]
    at = pl.ds(pl.multiple_of(half * rows, rows), rows)
    load = pltpu.make_async_copy(weight_hbm.at[at], weight_ref, sem)
    load.start()
    load.wait()
    for side, ref in ((half, first_ref), (1 - half, second_ref)):
        block = sums_ref[pl.ds(pl.multiple_of(side * own, own), own), :]
        ref[...] = lax.dot_general(
            block, weight_ref[...], (((1,), (1,)), ((), ())), preferred_element_type=F32
        ).astype(BF16)
    token_ref[...] = jnp.zeros_like(token_ref)


def atom_grads(chips, place, sums, weight):
    own, width = sums.shape[0] // 2, sums.shape[1]
    rows = weight.shape[0] // 2
    return pl.pallas_call(
        functools.partial(atom_grad_kernel, chips),
        out_shape=[jax.ShapeDtypeStruct((own, rows), BF16)] * 2
        + [jax.ShapeDtypeStruct((1, width), BF16)],
        in_specs=[whole_smem(), whole_vmem(), in_hbm()],
        out_specs=[whole_vmem()] * 3,
        scratch_shapes=[pltpu.VMEM((rows, width), BF16), pltpu.SemaphoreType.DMA],
        compiler_params=params(SMALL),
        cost_estimate=pl.CostEstimate(
            flops=4 * own * rows * width, bytes_accessed=2 * rows * width, transcendentals=0
        ),
        name="atom_grads",
    )(place, sums, weight)


def expert_kernel(parts, place_ref, coef_ref, *refs):
    grad_refs, out_ref, held_ref, sems = refs[:-3], refs[-3], refs[-2], refs[-1]
    me = place_ref[0]
    count, _, width = out_ref.shape
    systems = coef_ref.shape[0]
    copies = []
    scales = [[coef_ref[me ^ k, me * count + e] for e in range(count)] for k in range(systems)]
    for h, (lo, size) in enumerate(parts):

        @pl.loop(0, size // STEP)
        def _(i):
            at = pl.ds(pl.multiple_of(lo + i * STEP, STEP), STEP)
            for col in range(0, width, 128):
                cols = slice(col, min(col + 128, width))
                grads = [ref[at, cols].astype(F32) for ref in grad_refs]
                for e in range(count):
                    total = scales[0][e] * grads[0]
                    for k in range(1, systems):
                        total = total + scales[k][e] * grads[k]
                    held_ref[e, at, cols] = total

        at = pl.ds(lo, size)
        copies.append(pltpu.make_async_copy(held_ref.at[:, at, :], out_ref.at[:, at, :], sems.at[h]))
        copies[-1].start()
    for copy in copies:
        copy.wait()


def expert_grads(place, coef, grads, shape, parts):
    return pl.pallas_call(
        functools.partial(expert_kernel, parts),
        out_shape=jax.ShapeDtypeStruct(shape, F32),
        in_specs=[whole_smem(), whole_smem()] + [whole_vmem()] * len(grads),
        out_specs=in_hbm(),
        scratch_shapes=[pltpu.VMEM(shape, F32), pltpu.SemaphoreType.DMA((len(parts),))],
        compiler_params=params(SMALL),
        name="expert_grads",
    )(place, coef, *grads)


def hot_kernel(cols_ref, rows_ref, across_ref, down_ref, _, gather_ref, sum_ref, token_ref):
    atoms = down_ref.shape[0]

    def hot(same):
        return jnp.where(same, 1.0, 0.0).astype(BF16)

    for i in range(2):
        at = slice(i * atoms, (i + 1) * atoms)
        gather_ref[:, at] = hot(cols_ref[:, i : i + 1] == across_ref[...])
        sum_ref[at, :] = hot(down_ref[...] == rows_ref[i : i + 1, :])
    token_ref[...] = jnp.zeros_like(token_ref)


def hot_ends(cols, rows, order, earlier, width, tile):
    edges, atoms = cols.shape[0], order.shape[0]
    fixed = lambda *shape: pl.BlockSpec(shape, lambda i: (0, 0))
    return pl.pallas_call(
        hot_kernel,
        grid=(edges // tile,),
        out_shape=[
            jax.ShapeDtypeStruct((edges, 2 * atoms), BF16),
            jax.ShapeDtypeStruct((2 * atoms, edges), BF16),
            jax.ShapeDtypeStruct((1, width), F32),
        ],
        in_specs=[
            pl.BlockSpec((tile, 2), lambda i: (i, 0)),
            pl.BlockSpec((2, tile), lambda i: (0, i)),
            fixed(1, atoms),
            fixed(atoms, 1),
            in_hbm(),
        ],
        out_specs=[
            pl.BlockSpec((tile, 2 * atoms), lambda i: (i, 0)),
            pl.BlockSpec((2 * atoms, tile), lambda i: (0, i)),
            fixed(1, width),
        ],
        compiler_params=params(),
        cost_estimate=pl.CostEstimate(
            flops=16 * edges * atoms, bytes_accessed=8 * edges * atoms, transcendentals=0
        ),
        name="hot_ends",
    )(cols, rows, order[None, :], order[:, None], earlier)


def scale_kernel(slots, place_ref, gather_ref, radial_ref, *refs):
    block_refs = refs[:slots]
    atoms_out, scaled_ref, token_ref, atoms_ref, cot_ref, sems = refs[slots:]
    step = pl.program_id(0)
    own = block_refs[0].shape[1]
    store = pltpu.make_async_copy(atoms_ref, atoms_out, sems.at[2 * slots])

    @pl.when(step == 0)
    def _():
        loads = []
        chips = slots // 2
        for k, ref in enumerate(block_refs):
            back = lax.rem(place_ref[1] - k % chips + chips, chips)
            at = pl.ds(pl.multiple_of((k // chips * chips + back) * own, own), own)
            for i, to in enumerate((atoms_ref, cot_ref)):
                loads.append(pltpu.make_async_copy(ref.at[i], to.at[at], sems.at[2 * k + i]))
                loads[-1].start()
        for load in loads:
            load.wait()
        store.start()

    cot = jnp.dot(gather_ref[...], cot_ref[...], preferred_element_type=F32)
    scaled_ref[...] = (cot * radial_ref[...].astype(F32)).astype(BF16)
    token_ref[...] = jnp.zeros_like(token_ref)

    @pl.when(step == pl.num_programs(0) - 1)
    def _():
        store.wait()


def scaled_edges(place, hot_gather, radial, blocks, tile):
    edges, width = radial.shape
    atoms = hot_gather.shape[1] // 2
    slots = len(blocks)
    return pl.pallas_call(
        functools.partial(scale_kernel, slots),
        grid=(edges // tile,),
        out_shape=[
            jax.ShapeDtypeStruct((atoms, width), BF16),
            jax.ShapeDtypeStruct((edges, width), BF16),
            jax.ShapeDtypeStruct((1, width), BF16),
        ],
        in_specs=[
            whole_smem(),
            pl.BlockSpec((tile, atoms), lambda i: (i, 1)),
            pl.BlockSpec((tile, width), lambda i: (i, 0)),
        ]
        + [in_hbm()] * slots,
        out_specs=[
            in_hbm(),
            pl.BlockSpec((tile, width), lambda i: (i, 0)),
            pl.BlockSpec((1, width), lambda i: (0, 0)),
        ],
        scratch_shapes=[
            pltpu.VMEM((atoms, width), BF16),
            pltpu.VMEM((atoms, width), BF16),
            pltpu.SemaphoreType.DMA((2 * slots + 1,)),
        ],
        compiler_params=params(),
        cost_estimate=pl.CostEstimate(
            flops=2 * atoms * width * edges, bytes_accessed=6 * edges * width, transcendentals=0
        ),
        name="scaled_edges",
    )(place, hot_gather, radial, *blocks)


def edge_kernel(
    chips, place_ref, gather_ref, sum_ref, radial_ref, scaled_ref, atoms_hbm, *refs
):
    blocks = 2 * chips
    block_refs = refs[:blocks]
    kept_ref, sent_ref, node_kept_ref, node_sent_ref, weight_out = refs[blocks : blocks + 5]
    atoms_ref, weight_ref, proj_ref, value_ref, acc_ref, sem, sems = refs[blocks + 5 :]
    step, last = pl.program_id(0), pl.num_programs(0) - 1
    atoms, width_in = atoms_ref.shape
    width = radial_ref.shape[1]
    store = pltpu.make_async_copy(weight_ref, weight_out, sem)

    def messages():
        pre = jnp.dot(gather_ref[...], proj_ref[...], preferred_element_type=F32)
        sigma = 0.5 + 0.5 * jnp.tanh(0.5 * pre)
        silu = pre * sigma
        slope = sigma + silu * (1.0 - sigma)
        to = lax.rem(step, 2)
        value_ref[to, :, :width] = (scaled_ref[...].astype(F32) * slope).astype(BF16)
        value_ref[to, :, width:] = (silu * radial_ref[...].astype(F32)).astype(BF16)

    def add_up():
        at = lax.rem(step + 1, 2)
        acc_ref[:, :width] += jnp.dot(
            sum_ref[:atoms, :], value_ref[at, :, :width], preferred_element_type=F32
        )
        acc_ref[:, width:] += jnp.dot(
            sum_ref[atoms:, :], value_ref[at], preferred_element_type=F32
        )

    @pl.when(step == 0)
    def _():
        chip, core = place_ref[1], place_ref[2]
        depth = block_refs[0].shape[0]
        loads = [pltpu.make_async_copy(atoms_hbm, atoms_ref, sems.at[blocks])]
        for i, ref in enumerate(block_refs):
            source = lax.rem(chip - i // 2 + chips, chips)
            device = 2 * source + (1 - core if i % 2 else core)
            at = pl.ds(pl.multiple_of(device * depth, STEP), depth)
            loads.append(pltpu.make_async_copy(ref, weight_ref.at[at], sems.at[i]))
        for load in loads:
            load.start()
        acc_ref[...] = jnp.zeros_like(acc_ref)
        for load in loads:
            load.wait()
        store.start()
        for half in range(2):
            proj_ref[half * atoms : (half + 1) * atoms, :] = jnp.dot(
                atoms_ref[...],
                weight_ref[half * width_in : (half + 1) * width_in, :],
                preferred_element_type=F32,
            ).astype(BF16)
        messages()

    @pl.when(jnp.logical_and(step > 0, step < last))
    def _():
        add_up()
        messages()

    @pl.when(step == last)
    def _():
        add_up()
        side = atoms // 2
        for k in range(chips):
            chip = lax.rem(place_ref[1] + k, chips)
            cols = pl.ds(pl.multiple_of(chip // (chips // 2) * width, width), width)
            size = kept_ref.shape[1]
            row = lax.rem(chip, chips // 2) * size
            kept_ref[k] = acc_ref[pl.ds(pl.multiple_of(row, size), size), cols]
            sent_ref[k] = acc_ref[pl.ds(pl.multiple_of(side + row, size), size), cols].astype(BF16)
            cols = slice(2 * width, 3 * width)
            size = node_kept_ref.shape[1]
            row = chip * size
            node_kept_ref[k] = acc_ref[pl.ds(pl.multiple_of(row, size), size), cols]
            node_sent_ref[k] = acc_ref[pl.ds(pl.multiple_of(side + row, size), size), cols].astype(
                BF16
            )
        store.wait()


def edge_sums(chips, place, gather, sums, radial, scaled, atoms, blocks, tile):
    edges, width = radial.shape
    count, width_in = atoms.shape
    flops = 2 * count * width * (2 * width_in + 5 * edges)
    fixed = lambda *shape: pl.BlockSpec(shape, lambda i: (0,) * len(shape))
    sums_shape = (chips, count // chips, width)
    node_shape = (chips, count // 2 // chips, width)
    halves = [(sums_shape, F32), (sums_shape, BF16), (node_shape, F32), (node_shape, BF16)]
    outs = halves + [((2 * width_in, width), BF16)]
    steps = edges // tile
    return pl.pallas_call(
        functools.partial(edge_kernel, chips),
        grid=(steps + 1,),
        out_shape=[jax.ShapeDtypeStruct(shape, kind) for shape, kind in outs],
        in_specs=[
            whole_smem(),
            pl.BlockSpec((tile, 2 * count), lambda i: (jnp.minimum(i, steps - 1), 0)),
            pl.BlockSpec((2 * count, tile), lambda i: (0, jnp.maximum(i - 1, 0))),
            pl.BlockSpec((tile, width), lambda i: (jnp.minimum(i, steps - 1), 0)),
            pl.BlockSpec((tile, width), lambda i: (jnp.minimum(i, steps - 1), 0)),
        ]
        + [in_hbm()] * (1 + len(blocks)),
        out_specs=[fixed(*shape) for shape, _ in halves] + [in_hbm()],
        scratch_shapes=[
            pltpu.VMEM((count, width_in), BF16),
            pltpu.VMEM((2 * width_in, width), BF16),
            pltpu.VMEM((2 * count, width), BF16),
            pltpu.VMEM((2, tile, 2 * width), BF16),
            pltpu.VMEM((count, 3 * width), F32),
            pltpu.SemaphoreType.DMA,
            pltpu.SemaphoreType.DMA((len(blocks) + 1,)),
        ],
        compiler_params=params(),
        cost_estimate=pl.CostEstimate(
            flops=flops,
            bytes_accessed=4 * edges * width + 8 * edges * count,
            transcendentals=edges * width,
        ),
        name="edge_sums",
    )(place, gather, sums, radial, scaled, atoms, *blocks)


def shards(systems, ways, atoms, cotangent, experts, radial, coef, source, target):
    chips = ways // 2
    me_sys = lax.axis_index("sys")
    me_edge = lax.axis_index("edge")
    chip, core = me_edge // 2, me_edge % 2
    place = jnp.stack([me_sys, chip, core]).astype(jnp.int32)
    _, depth, width = experts.shape
    own = atoms.shape[1]
    tile = min(512, radial.shape[1])
    parts = row_parts(depth)

    def across(x, k):
        return lax.ppermute(x, "sys", [(s, s ^ k) for s in range(systems)])

    def swap(x):
        return lax.ppermute(x, "edge", [(e, e ^ 1) for e in range(ways)])

    def shift(x, k):
        return lax.ppermute(x, "edge", [(e, (e + 2 * k) % ways) for e in range(ways)])

    def both_cores(blocks):
        return blocks + [swap(block) for block in blocks]

    merged = merge_parts(place, coef, experts, parts)
    pair = join(atoms, cotangent, merged[-1])
    features = both_cores([pair] + [shift(pair, k) for k in range(1, chips)])

    at = jnp.arange(ways * own, dtype=jnp.int32)
    side, z, offset = at // (chips * own), at // own % chips, at % own
    order = (2 * z + (core ^ side)) * own + offset
    ends = jnp.concatenate([source, target])
    hot_gather, hot_sum, hot_token = hot_ends(ends.T, ends, order, pair, width, tile)
    all_atoms, scaled, scaled_token = scaled_edges(place, hot_gather, radial[0], features, tile)
    own_cols = lax.dynamic_slice_in_dim(all_atoms, (me_edge % chips) * depth, depth, 1).T

    got = [merged[0]] + [across(merged[k], k) for k in range(1, systems)]
    held = weight_rows(got, features[1:chips] + [hot_token])
    blocks = []
    for k in range(chips):
        if k == chips - 1:
            held = held + scaled_token
        if k:
            held = shift(held, 1)
        blocks += [held, swap(held)]

    kept, sent, node_kept, node_sent, weight = edge_sums(
        chips, place, hot_gather, hot_sum, radial[0], scaled, all_atoms, blocks, tile
    )

    def reduce(kept, other, zero):
        terms = [kept[k] + other[k].astype(F32) + zero for k in range(chips)]
        total = terms[0]
        for k in range(1, chips):
            total = total + shift(terms[k].astype(BF16), k).astype(F32)
        return total.astype(BF16)

    shares = chips // 2
    sums = reduce(kept, swap(sent), 0.0)

    def share(x, j):
        to = [z // shares * shares + (z + j) % shares for z in range(chips)]
        return lax.ppermute(x, "edge", [(2 * z + c, 2 * to[z] + c) for z in range(chips) for c in range(2)])

    *terms, term_token = atom_grads(chips, place, sums, weight)
    picked = both_cores([sums] + [share(sums, j) + term_token for j in range(1, shares)])
    grad, send, grad_token = merged_grads(place, own_cols, picked)
    grads = [grad] + [across(send, k) for k in range(1, systems)]
    expert_grad = expert_grads(place, coef, grads, experts.shape, parts)

    atom_grad = 0.0
    for flip, term in enumerate(terms):
        to = [2 * (z % shares) + (z // shares ^ flip) for z in range(chips)]
        pairs = [(2 * z + c, 2 * to[z] + c) for z in range(chips) for c in range(2)]
        atom_grad = atom_grad + lax.ppermute(term, "edge", pairs).astype(F32)

    node = reduce(node_kept, swap(node_sent), grad_token)
    return node[None], atom_grad[None], expert_grad


def solution(mesh):
    placed = P("sys", "edge", None)
    return jax.shard_map(
        functools.partial(shards, mesh.shape["sys"], mesh.shape["edge"]),
        mesh=mesh,
        in_specs=(placed, placed, placed, placed, P(), P("sys", "edge"), P("sys", "edge")),
        out_specs=(placed, placed, placed),
        check_vma=False,
    )
```

```python
import functools

import jax
import jax.numpy as jnp
from jax import lax
from jax.experimental import pallas as pl
from jax.experimental.pallas import tpu as pltpu
from jax.sharding import PartitionSpec as P

F32 = jnp.float32
BF16 = jnp.bfloat16
LARGE = 60 << 20
SMALL = 24 << 20
STEP = 16


def whole_vmem():
    return pl.BlockSpec(memory_space=pltpu.VMEM)


def in_hbm():
    return pl.BlockSpec(memory_space=pltpu.HBM)


def whole_smem():
    return pl.BlockSpec(memory_space=pltpu.SMEM)


def params(limit=LARGE):
    return pltpu.CompilerParams(vmem_limit_bytes=limit)


def row_parts(depth):
    first = -(-depth // (2 * STEP)) * STEP
    return [(0, first), (first, depth - first)]


def merge_kernel(parts, place_ref, coef_ref, experts_ref, _, *refs):
    part_refs, held_ref, sems = refs[:-2], refs[-2], refs[-1]
    systems, count = coef_ref.shape[0], experts_ref.shape[0]
    width = experts_ref.shape[2]
    me = place_ref[0]
    loads = []
    for h, (lo, size) in enumerate(parts):
        at = pl.ds(lo, size)
        loads.append(
            pltpu.make_async_copy(experts_ref.at[:, at, :], held_ref.at[:, at, :], sems.at[h])
        )
        loads[-1].start()
    scales = [[coef_ref[me ^ k, me * count + e] for e in range(count)] for k in range(systems)]
    for h, (lo, size) in enumerate(parts):
        loads[h].wait()

        @pl.loop(0, size // STEP)
        def _(i):
            at = pl.ds(pl.multiple_of(lo + i * STEP, STEP), STEP)
            for col in range(0, width, 128):
                cols = slice(col, min(col + 128, width))
                loaded = [held_ref[e, at, cols].astype(F32) for e in range(count)]
                for k in range(systems):
                    total = scales[k][0] * loaded[0]
                    for e in range(1, count):
                        total = total + scales[k][e] * loaded[e]
                    part_refs[k][at, cols] = total.astype(part_refs[k].dtype)


def merge_parts(place, coef, experts, earlier, parts):
    _, depth, width = experts.shape
    systems = coef.shape[0]
    return pl.pallas_call(
        functools.partial(merge_kernel, parts),
        out_shape=[
            jax.ShapeDtypeStruct((depth, width), BF16 if k else F32) for k in range(systems)
        ],
        in_specs=[whole_smem(), whole_smem(), in_hbm(), in_hbm()],
        out_specs=[whole_vmem()] * systems,
        scratch_shapes=[
            pltpu.VMEM(experts.shape, BF16),
            pltpu.SemaphoreType.DMA((len(parts),)),
        ],
        compiler_params=params(),
        name="merge_parts",
    )(place, coef, experts, earlier)


def join_kernel(atoms_ref, cot_ref, both_ref, sems):
    loads = [
        pltpu.make_async_copy(ref.at[0], both_ref.at[i], sems.at[i])
        for i, ref in enumerate((atoms_ref, cot_ref))
    ]
    for load in loads:
        load.start()
    for load in loads:
        load.wait()


def join(atoms, cotangent):
    return pl.pallas_call(
        join_kernel,
        out_shape=jax.ShapeDtypeStruct((2, *atoms.shape[1:]), BF16),
        in_specs=[in_hbm(), in_hbm()],
        out_specs=whole_vmem(),
        scratch_shapes=[pltpu.SemaphoreType.DMA((2,))],
        compiler_params=params(),
        name="join",
    )(atoms, cotangent)


def rows_kernel(count, *refs):
    out_ref = refs[-1]
    total = refs[0][...]
    for ref in refs[1:count]:
        total = total + ref[...].astype(F32)
    out_ref[...] = total.astype(BF16)


def weight_rows(parts, earlier):
    return pl.pallas_call(
        functools.partial(rows_kernel, len(parts)),
        out_shape=jax.ShapeDtypeStruct(parts[0].shape, BF16),
        in_specs=[whole_vmem()] * len(parts) + [in_hbm()] * len(earlier),
        out_specs=whole_vmem(),
        compiler_params=params(SMALL),
        name="weight_rows",
    )(*parts, *earlier)


def merged_grad_kernel(through, place_ref, cols_ref, *refs):
    grad_ref, sent_ref, sums_ref = refs[-through - 3], refs[-through - 2], refs[-1]
    block_refs = refs[: -2 * through - 3]
    size = block_refs[0].shape[0]
    pieces = len(block_refs) // 2
    for i, ref in enumerate(block_refs):
        piece = lax.rem(place_ref[1] + pieces - i % pieces, pieces)
        at = pl.ds(pl.multiple_of((i // pieces * pieces + piece) * size, size), size)
        sums_ref[at, :] = ref[...]
    grad = jnp.dot(cols_ref[...], sums_ref[...], preferred_element_type=F32)
    grad_ref[...] = grad
    sent_ref[...] = grad.astype(BF16)
    for i in range(through):
        refs[len(block_refs) + through + 2 + i][...] = refs[len(block_refs) + i][...]


def merged_grads(place, cols, blocks, others):
    size, width = blocks[0].shape
    return pl.pallas_call(
        functools.partial(merged_grad_kernel, len(others)),
        out_shape=[jax.ShapeDtypeStruct((cols.shape[0], width), kind) for kind in (F32, BF16)]
        + [jax.ShapeDtypeStruct(other.shape, other.dtype) for other in others],
        in_specs=[whole_smem()] + [whole_vmem()] * (1 + len(blocks) + len(others)),
        out_specs=[whole_vmem()] * (2 + len(others)),
        scratch_shapes=[pltpu.VMEM((size * len(blocks), width), BF16)],
        compiler_params=params(SMALL),
        name="merged_grads",
    )(place, cols, *blocks, *others)


def atom_grad_kernel(
    chips, place_ref, sums_ref, weight_hbm, first_ref, second_ref, token_ref, weight_ref, sem
):
    half = place_ref[1] // (chips // 2)
    rows, own = weight_ref.shape[0], first_ref.shape[0]
    at = pl.ds(pl.multiple_of(half * rows, rows), rows)
    load = pltpu.make_async_copy(weight_hbm.at[at], weight_ref, sem)
    load.start()
    load.wait()
    for side, ref in ((half, first_ref), (1 - half, second_ref)):
        block = sums_ref[pl.ds(pl.multiple_of(side * own, own), own), :]
        ref[...] = lax.dot_general(
            block, weight_ref[...], (((1,), (1,)), ((), ())), preferred_element_type=F32
        ).astype(BF16)
    token_ref[...] = jnp.zeros_like(token_ref)


def atom_grads(chips, place, sums, weight):
    own, width = sums.shape[0] // 2, sums.shape[1]
    rows = weight.shape[0] // 2
    return pl.pallas_call(
        functools.partial(atom_grad_kernel, chips),
        out_shape=[jax.ShapeDtypeStruct((own, rows), BF16)] * 2
        + [jax.ShapeDtypeStruct((1, width), BF16)],
        in_specs=[whole_smem(), whole_vmem(), in_hbm()],
        out_specs=[whole_vmem()] * 3,
        scratch_shapes=[pltpu.VMEM((rows, width), BF16), pltpu.SemaphoreType.DMA],
        compiler_params=params(SMALL),
        cost_estimate=pl.CostEstimate(
            flops=4 * own * rows * width, bytes_accessed=2 * rows * width, transcendentals=0
        ),
        name="atom_grads",
    )(place, sums, weight)


def expert_kernel(parts, place_ref, coef_ref, *refs):
    grad_refs, out_ref, held_ref, sems = refs[:-3], refs[-3], refs[-2], refs[-1]
    me = place_ref[0]
    count, _, width = out_ref.shape
    systems = coef_ref.shape[0]
    copies = []
    scales = [[coef_ref[me ^ k, me * count + e] for e in range(count)] for k in range(systems)]
    for h, (lo, size) in enumerate(parts):

        @pl.loop(0, size // STEP)
        def _(i):
            at = pl.ds(pl.multiple_of(lo + i * STEP, STEP), STEP)
            for col in range(0, width, 128):
                cols = slice(col, min(col + 128, width))
                grads = [ref[at, cols].astype(F32) for ref in grad_refs]
                for e in range(count):
                    total = scales[0][e] * grads[0]
                    for k in range(1, systems):
                        total = total + scales[k][e] * grads[k]
                    held_ref[e, at, cols] = total

        at = pl.ds(lo, size)
        copies.append(pltpu.make_async_copy(held_ref.at[:, at, :], out_ref.at[:, at, :], sems.at[h]))
        copies[-1].start()
    for copy in copies:
        copy.wait()


def expert_grads(place, coef, grads, shape, parts):
    return pl.pallas_call(
        functools.partial(expert_kernel, parts),
        out_shape=jax.ShapeDtypeStruct(shape, F32),
        in_specs=[whole_smem(), whole_smem()] + [whole_vmem()] * len(grads),
        out_specs=in_hbm(),
        scratch_shapes=[pltpu.VMEM(shape, F32), pltpu.SemaphoreType.DMA((len(parts),))],
        compiler_params=params(SMALL),
        name="expert_grads",
    )(place, coef, *grads)


def hot_kernel(cols_ref, rows_ref, across_ref, down_ref, _, gather_ref, sum_ref, token_ref):
    atoms = down_ref.shape[0]

    def hot(same):
        return jnp.where(same, 1.0, 0.0).astype(BF16)

    for i in range(2):
        at = slice(i * atoms, (i + 1) * atoms)
        gather_ref[:, at] = hot(cols_ref[:, i : i + 1] == across_ref[...])
        sum_ref[at, :] = hot(down_ref[...] == rows_ref[i : i + 1, :])
    token_ref[...] = jnp.zeros_like(token_ref)


def hot_ends(cols, rows, order, earlier, width, tile):
    edges, atoms = cols.shape[0], order.shape[0]
    fixed = lambda *shape: pl.BlockSpec(shape, lambda i: (0, 0))
    return pl.pallas_call(
        hot_kernel,
        grid=(edges // tile,),
        out_shape=[
            jax.ShapeDtypeStruct((edges, 2 * atoms), BF16),
            jax.ShapeDtypeStruct((2 * atoms, edges), BF16),
            jax.ShapeDtypeStruct((1, width), F32),
        ],
        in_specs=[
            pl.BlockSpec((tile, 2), lambda i: (i, 0)),
            pl.BlockSpec((2, tile), lambda i: (0, i)),
            fixed(1, atoms),
            fixed(atoms, 1),
            in_hbm(),
        ],
        out_specs=[
            pl.BlockSpec((tile, 2 * atoms), lambda i: (i, 0)),
            pl.BlockSpec((2 * atoms, tile), lambda i: (0, i)),
            fixed(1, width),
        ],
        compiler_params=params(),
        cost_estimate=pl.CostEstimate(
            flops=16 * edges * atoms, bytes_accessed=8 * edges * atoms, transcendentals=0
        ),
        name="hot_ends",
    )(cols, rows, order[None, :], order[:, None], earlier)


def scale_kernel(slots, place_ref, gather_ref, radial_ref, *refs):
    block_refs = refs[:slots]
    atoms_out, scaled_ref, token_ref, atoms_ref, cot_ref, sems = refs[slots:]
    step = pl.program_id(0)
    own = block_refs[0].shape[1]
    store = pltpu.make_async_copy(atoms_ref, atoms_out, sems.at[2 * slots])

    @pl.when(step == 0)
    def _():
        loads = []
        chips = slots // 2
        for k, ref in enumerate(block_refs):
            back = lax.rem(place_ref[1] - k % chips + chips, chips)
            at = pl.ds(pl.multiple_of((k // chips * chips + back) * own, own), own)
            for i, to in enumerate((atoms_ref, cot_ref)):
                loads.append(pltpu.make_async_copy(ref.at[i], to.at[at], sems.at[2 * k + i]))
                loads[-1].start()
        for load in loads:
            load.wait()
        store.start()

    cot = jnp.dot(gather_ref[...], cot_ref[...], preferred_element_type=F32)
    scaled_ref[...] = (cot * radial_ref[...].astype(F32)).astype(BF16)
    token_ref[...] = jnp.zeros_like(token_ref)

    @pl.when(step == pl.num_programs(0) - 1)
    def _():
        store.wait()


def scaled_edges(place, hot_gather, radial, blocks, tile):
    edges, width = radial.shape
    atoms = hot_gather.shape[1] // 2
    slots = len(blocks)
    return pl.pallas_call(
        functools.partial(scale_kernel, slots),
        grid=(edges // tile,),
        out_shape=[
            jax.ShapeDtypeStruct((atoms, width), BF16),
            jax.ShapeDtypeStruct((edges, width), BF16),
            jax.ShapeDtypeStruct((1, width), BF16),
        ],
        in_specs=[
            whole_smem(),
            pl.BlockSpec((tile, atoms), lambda i: (i, 1)),
            pl.BlockSpec((tile, width), lambda i: (i, 0)),
        ]
        + [in_hbm()] * slots,
        out_specs=[
            in_hbm(),
            pl.BlockSpec((tile, width), lambda i: (i, 0)),
            pl.BlockSpec((1, width), lambda i: (0, 0)),
        ],
        scratch_shapes=[
            pltpu.VMEM((atoms, width), BF16),
            pltpu.VMEM((atoms, width), BF16),
            pltpu.SemaphoreType.DMA((2 * slots + 1,)),
        ],
        compiler_params=params(),
        cost_estimate=pl.CostEstimate(
            flops=2 * atoms * width * edges, bytes_accessed=6 * edges * width, transcendentals=0
        ),
        name="scaled_edges",
    )(place, hot_gather, radial, *blocks)


def edge_kernel(
    chips, place_ref, gather_ref, sum_ref, radial_ref, scaled_ref, atoms_hbm, *refs
):
    blocks = 2 * chips
    block_refs = refs[:blocks]
    kept_ref, sent_ref, node_kept_ref, node_sent_ref, weight_out = refs[blocks : blocks + 5]
    atoms_ref, weight_ref, proj_ref, value_ref, acc_ref, sem, sems = refs[blocks + 5 :]
    step, last = pl.program_id(0), pl.num_programs(0) - 1
    atoms, width_in = atoms_ref.shape
    width = radial_ref.shape[1]
    store = pltpu.make_async_copy(weight_ref, weight_out, sem)

    def messages():
        pre = jnp.dot(gather_ref[...], proj_ref[...], preferred_element_type=F32)
        sigma = 0.5 + 0.5 * jnp.tanh(0.5 * pre)
        silu = pre * sigma
        slope = sigma + silu * (1.0 - sigma)
        to = lax.rem(step, 2)
        value_ref[to, :, :width] = (scaled_ref[...].astype(F32) * slope).astype(BF16)
        value_ref[to, :, width:] = (silu * radial_ref[...].astype(F32)).astype(BF16)

    def add_up():
        at = lax.rem(step + 1, 2)
        acc_ref[:, :width] += jnp.dot(
            sum_ref[:atoms, :], value_ref[at, :, :width], preferred_element_type=F32
        )
        acc_ref[:, width:] += jnp.dot(
            sum_ref[atoms:, :], value_ref[at], preferred_element_type=F32
        )

    @pl.when(step == 0)
    def _():
        chip, core = place_ref[1], place_ref[2]
        depth = block_refs[0].shape[0]
        loads = [pltpu.make_async_copy(atoms_hbm, atoms_ref, sems.at[blocks])]
        for i, ref in enumerate(block_refs):
            source = lax.rem(chip - i // 2 + chips, chips)
            device = 2 * source + (1 - core if i % 2 else core)
            at = pl.ds(pl.multiple_of(device * depth, STEP), depth)
            loads.append(pltpu.make_async_copy(ref, weight_ref.at[at], sems.at[i]))
        for load in loads:
            load.start()
        acc_ref[...] = jnp.zeros_like(acc_ref)
        for load in loads:
            load.wait()
        store.start()
        for half in range(2):
            proj_ref[half * atoms : (half + 1) * atoms, :] = jnp.dot(
                atoms_ref[...],
                weight_ref[half * width_in : (half + 1) * width_in, :],
                preferred_element_type=F32,
            ).astype(BF16)
        messages()

    @pl.when(jnp.logical_and(step > 0, step < last))
    def _():
        add_up()
        messages()

    @pl.when(step == last)
    def _():
        add_up()
        side = atoms // 2
        for k in range(chips):
            chip = lax.rem(place_ref[1] + k, chips)
            cols = pl.ds(pl.multiple_of(chip // (chips // 2) * width, width), width)
            size = kept_ref.shape[1]
            row = lax.rem(chip, chips // 2) * size
            kept_ref[k] = acc_ref[pl.ds(pl.multiple_of(row, size), size), cols]
            sent_ref[k] = acc_ref[pl.ds(pl.multiple_of(side + row, size), size), cols].astype(BF16)
            cols = slice(2 * width, 3 * width)
            size = node_kept_ref.shape[1]
            row = chip * size
            node_kept_ref[k] = acc_ref[pl.ds(pl.multiple_of(row, size), size), cols]
            node_sent_ref[k] = acc_ref[pl.ds(pl.multiple_of(side + row, size), size), cols].astype(
                BF16
            )
        store.wait()


def edge_sums(chips, place, gather, sums, radial, scaled, atoms, blocks, tile):
    edges, width = radial.shape
    count, width_in = atoms.shape
    flops = 2 * count * width * (2 * width_in + 5 * edges)
    fixed = lambda *shape: pl.BlockSpec(shape, lambda i: (0,) * len(shape))
    sums_shape = (chips, count // chips, width)
    node_shape = (chips, count // 2 // chips, width)
    halves = [(sums_shape, F32), (sums_shape, BF16), (node_shape, F32), (node_shape, BF16)]
    outs = halves + [((2 * width_in, width), BF16)]
    steps = edges // tile
    return pl.pallas_call(
        functools.partial(edge_kernel, chips),
        grid=(steps + 1,),
        out_shape=[jax.ShapeDtypeStruct(shape, kind) for shape, kind in outs],
        in_specs=[
            whole_smem(),
            pl.BlockSpec((tile, 2 * count), lambda i: (jnp.minimum(i, steps - 1), 0)),
            pl.BlockSpec((2 * count, tile), lambda i: (0, jnp.maximum(i - 1, 0))),
            pl.BlockSpec((tile, width), lambda i: (jnp.minimum(i, steps - 1), 0)),
            pl.BlockSpec((tile, width), lambda i: (jnp.minimum(i, steps - 1), 0)),
        ]
        + [in_hbm()] * (1 + len(blocks)),
        out_specs=[fixed(*shape) for shape, _ in halves] + [in_hbm()],
        scratch_shapes=[
            pltpu.VMEM((count, width_in), BF16),
            pltpu.VMEM((2 * width_in, width), BF16),
            pltpu.VMEM((2 * count, width), BF16),
            pltpu.VMEM((2, tile, 2 * width), BF16),
            pltpu.VMEM((count, 3 * width), F32),
            pltpu.SemaphoreType.DMA,
            pltpu.SemaphoreType.DMA((len(blocks) + 1,)),
        ],
        compiler_params=params(),
        cost_estimate=pl.CostEstimate(
            flops=flops,
            bytes_accessed=4 * edges * width + 8 * edges * count,
            transcendentals=edges * width,
        ),
        name="edge_sums",
    )(place, gather, sums, radial, scaled, atoms, *blocks)


def shards(systems, ways, atoms, cotangent, experts, radial, coef, source, target):
    chips = ways // 2
    me_sys = lax.axis_index("sys")
    me_edge = lax.axis_index("edge")
    chip, core = me_edge // 2, me_edge % 2
    place = jnp.stack([me_sys, chip, core]).astype(jnp.int32)
    _, depth, width = experts.shape
    own = atoms.shape[1]
    tile = min(512, radial.shape[1])
    parts = row_parts(depth)

    def across(x, k):
        return lax.ppermute(x, "sys", [(s, s ^ k) for s in range(systems)])

    def swap(x):
        return lax.ppermute(x, "edge", [(e, e ^ 1) for e in range(ways)])

    def shift(x, k):
        return lax.ppermute(x, "edge", [(e, (e + 2 * k) % ways) for e in range(ways)])

    def both_cores(blocks):
        return blocks + [swap(block) for block in blocks]

    pair = join(atoms, cotangent)
    merged = merge_parts(place, coef, experts, pair, parts)
    features = both_cores([pair] + [shift(pair, k) for k in range(1, chips)])

    at = jnp.arange(ways * own, dtype=jnp.int32)
    side, z, offset = at // (chips * own), at // own % chips, at % own
    order = (2 * z + (core ^ side)) * own + offset
    ends = jnp.concatenate([source, target])
    hot_gather, hot_sum, hot_token = hot_ends(ends.T, ends, order, pair, width, tile)
    all_atoms, scaled, scaled_token = scaled_edges(place, hot_gather, radial[0], features, tile)
    own_cols = lax.dynamic_slice_in_dim(all_atoms, (me_edge % chips) * depth, depth, 1).T

    got = [merged[0]] + [across(merged[k], k) for k in range(1, systems)]
    held = weight_rows(got, features[1:chips] + [hot_token])
    blocks = []
    for k in range(chips):
        if k == chips - 1:
            held = held + scaled_token
        if k:
            held = shift(held, 1)
        blocks += [held, swap(held)]

    kept, sent, node_kept, node_sent, weight = edge_sums(
        chips, place, hot_gather, hot_sum, radial[0], scaled, all_atoms, blocks, tile
    )

    def terms_of(kept, other):
        terms = [kept[k] + other[k].astype(F32) for k in range(chips)]
        return terms[0], [term.astype(BF16) for term in terms[1:]]

    def reduce(total, terms):
        for k, term in enumerate(terms, 1):
            total = total + shift(term, k).astype(F32)
        return total.astype(BF16)

    shares = chips // 2
    sums = reduce(*terms_of(kept, swap(sent)))
    node, node_terms = terms_of(node_kept, swap(node_sent))

    def share(x, j):
        to = [z // shares * shares + (z + j) % shares for z in range(chips)]
        return lax.ppermute(x, "edge", [(2 * z + c, 2 * to[z] + c) for z in range(chips) for c in range(2)])

    *terms, term_token = atom_grads(chips, place, sums, weight)
    picked = both_cores([sums] + [share(sums, j) + term_token for j in range(1, shares)])
    grad, send, *node_terms = merged_grads(place, own_cols, picked, node_terms)
    grads = [grad] + [across(send, k) for k in range(1, systems)]
    expert_grad = expert_grads(place, coef, grads, experts.shape, parts)

    atom_grad = 0.0
    for flip, term in enumerate(terms):
        to = [2 * (z % shares) + (z // shares ^ flip) for z in range(chips)]
        pairs = [(2 * z + c, 2 * to[z] + c) for z in range(chips) for c in range(2)]
        atom_grad = atom_grad + lax.ppermute(term, "edge", pairs).astype(F32)

    return reduce(node, node_terms)[None], atom_grad[None], expert_grad


def solution(mesh):
    placed = P("sys", "edge", None)
    return jax.shard_map(
        functools.partial(shards, mesh.shape["sys"], mesh.shape["edge"]),
        mesh=mesh,
        in_specs=(placed, placed, placed, placed, P(), P("sys", "edge"), P("sys", "edge")),
        out_specs=(placed, placed, placed),
        check_vma=False,
    )
```

```python
import functools

import jax
import jax.numpy as jnp
from jax import lax
from jax.experimental import pallas as pl
from jax.experimental.pallas import tpu as pltpu
from jax.sharding import PartitionSpec as P

F32 = jnp.float32
BF16 = jnp.bfloat16
LARGE = 60 << 20
SMALL = 24 << 20
STEP = 16


def whole_vmem():
    return pl.BlockSpec(memory_space=pltpu.VMEM)


def in_hbm():
    return pl.BlockSpec(memory_space=pltpu.HBM)


def whole_smem():
    return pl.BlockSpec(memory_space=pltpu.SMEM)


def params(limit=LARGE):
    return pltpu.CompilerParams(vmem_limit_bytes=limit)


def row_parts(depth):
    first = -(-depth // (2 * STEP)) * STEP
    return [(0, first), (first, depth - first)]


def merge_kernel(parts, place_ref, coef_ref, experts_ref, _, *refs):
    part_refs, held_ref, sems = refs[:-2], refs[-2], refs[-1]
    systems, count = coef_ref.shape[0], experts_ref.shape[0]
    width = experts_ref.shape[2]
    me = place_ref[0]
    loads = []
    for h, (lo, size) in enumerate(parts):
        at = pl.ds(lo, size)
        loads.append(
            pltpu.make_async_copy(experts_ref.at[:, at, :], held_ref.at[:, at, :], sems.at[h])
        )
        loads[-1].start()
    scales = [[coef_ref[me ^ k, me * count + e] for e in range(count)] for k in range(systems)]
    for h, (lo, size) in enumerate(parts):
        loads[h].wait()

        @pl.loop(0, size // STEP)
        def _(i):
            at = pl.ds(pl.multiple_of(lo + i * STEP, STEP), STEP)
            for col in range(0, width, 128):
                cols = slice(col, min(col + 128, width))
                loaded = [held_ref[e, at, cols].astype(F32) for e in range(count)]
                for k in range(systems):
                    total = scales[k][0] * loaded[0]
                    for e in range(1, count):
                        total = total + scales[k][e] * loaded[e]
                    part_refs[k][at, cols] = total.astype(part_refs[k].dtype)


def merge_parts(place, coef, experts, earlier, parts):
    _, depth, width = experts.shape
    systems = coef.shape[0]
    return pl.pallas_call(
        functools.partial(merge_kernel, parts),
        out_shape=[
            jax.ShapeDtypeStruct((depth, width), BF16 if k else F32) for k in range(systems)
        ],
        in_specs=[whole_smem(), whole_smem(), in_hbm(), in_hbm()],
        out_specs=[whole_vmem()] * systems,
        scratch_shapes=[
            pltpu.VMEM(experts.shape, BF16),
            pltpu.SemaphoreType.DMA((len(parts),)),
        ],
        compiler_params=params(),
        name="merge_parts",
    )(place, coef, experts, earlier)


def join_kernel(atoms_ref, cot_ref, both_ref, sems):
    loads = [
        pltpu.make_async_copy(ref.at[0], both_ref.at[i], sems.at[i])
        for i, ref in enumerate((atoms_ref, cot_ref))
    ]
    for load in loads:
        load.start()
    for load in loads:
        load.wait()


def join(atoms, cotangent):
    return pl.pallas_call(
        join_kernel,
        out_shape=jax.ShapeDtypeStruct((2, *atoms.shape[1:]), BF16),
        in_specs=[in_hbm(), in_hbm()],
        out_specs=whole_vmem(),
        scratch_shapes=[pltpu.SemaphoreType.DMA((2,))],
        compiler_params=params(),
        name="join",
    )(atoms, cotangent)


def rows_kernel(count, *refs):
    out_ref = refs[-1]
    total = refs[0][...]
    for ref in refs[1:count]:
        total = total + ref[...].astype(F32)
    out_ref[...] = total.astype(BF16)


def weight_rows(parts, earlier):
    return pl.pallas_call(
        functools.partial(rows_kernel, len(parts)),
        out_shape=jax.ShapeDtypeStruct(parts[0].shape, BF16),
        in_specs=[whole_vmem()] * len(parts) + [in_hbm()] * len(earlier),
        out_specs=whole_vmem(),
        compiler_params=params(SMALL),
        name="weight_rows",
    )(*parts, *earlier)


def merged_grad_kernel(through, place_ref, cols_ref, *refs):
    grad_ref, sent_ref, sums_ref = refs[-through - 3], refs[-through - 2], refs[-1]
    block_refs = refs[: -2 * through - 3]
    size = block_refs[0].shape[0]
    pieces = len(block_refs) // 2
    for i, ref in enumerate(block_refs):
        piece = lax.rem(place_ref[1] + pieces - i % pieces, pieces)
        chips, own = 2 * pieces, size // 2
        for b in range(2):
            back = lax.rem(place_ref[1] - (2 * piece + b) + chips, chips)
            at = pl.ds(pl.multiple_of((i // pieces * chips + back) * own, own), own)
            sums_ref[at, :] = ref[b * own : (b + 1) * own, :]
    grad = jnp.dot(cols_ref[...], sums_ref[...], preferred_element_type=F32)
    grad_ref[...] = grad
    sent_ref[...] = grad.astype(BF16)
    for i in range(through):
        refs[len(block_refs) + through + 2 + i][...] = refs[len(block_refs) + i][...]


def merged_grads(place, cols, blocks, others):
    size, width = blocks[0].shape
    return pl.pallas_call(
        functools.partial(merged_grad_kernel, len(others)),
        out_shape=[jax.ShapeDtypeStruct((cols.shape[0], width), kind) for kind in (F32, BF16)]
        + [jax.ShapeDtypeStruct(other.shape, other.dtype) for other in others],
        in_specs=[whole_smem()] + [whole_vmem()] * (1 + len(blocks) + len(others)),
        out_specs=[whole_vmem()] * (2 + len(others)),
        scratch_shapes=[pltpu.VMEM((size * len(blocks), width), BF16)],
        compiler_params=params(SMALL),
        name="merged_grads",
    )(place, cols, *blocks, *others)


def atom_grad_kernel(
    chips, place_ref, sums_ref, weight_hbm, first_ref, second_ref, token_ref, weight_ref, sem
):
    half = place_ref[1] // (chips // 2)
    rows, own = weight_ref.shape[0], first_ref.shape[0]
    at = pl.ds(pl.multiple_of(half * rows, rows), rows)
    load = pltpu.make_async_copy(weight_hbm.at[at], weight_ref, sem)
    load.start()
    load.wait()
    for side, ref in ((half, first_ref), (1 - half, second_ref)):
        block = sums_ref[pl.ds(pl.multiple_of(side * own, own), own), :]
        ref[...] = lax.dot_general(
            block, weight_ref[...], (((1,), (1,)), ((), ())), preferred_element_type=F32
        ).astype(BF16)
    token_ref[...] = jnp.zeros_like(token_ref)


def atom_grads(chips, place, sums, weight):
    own, width = sums.shape[0] // 2, sums.shape[1]
    rows = weight.shape[0] // 2
    return pl.pallas_call(
        functools.partial(atom_grad_kernel, chips),
        out_shape=[jax.ShapeDtypeStruct((own, rows), BF16)] * 2
        + [jax.ShapeDtypeStruct((1, width), BF16)],
        in_specs=[whole_smem(), whole_vmem(), in_hbm()],
        out_specs=[whole_vmem()] * 3,
        scratch_shapes=[pltpu.VMEM((rows, width), BF16), pltpu.SemaphoreType.DMA],
        compiler_params=params(SMALL),
        cost_estimate=pl.CostEstimate(
            flops=4 * own * rows * width, bytes_accessed=2 * rows * width, transcendentals=0
        ),
        name="atom_grads",
    )(place, sums, weight)


def expert_kernel(parts, place_ref, coef_ref, *refs):
    grad_refs, out_ref, held_ref, sems = refs[:-3], refs[-3], refs[-2], refs[-1]
    me = place_ref[0]
    count, _, width = out_ref.shape
    systems = coef_ref.shape[0]
    copies = []
    scales = [[coef_ref[me ^ k, me * count + e] for e in range(count)] for k in range(systems)]
    for h, (lo, size) in enumerate(parts):

        @pl.loop(0, size // STEP)
        def _(i):
            at = pl.ds(pl.multiple_of(lo + i * STEP, STEP), STEP)
            for col in range(0, width, 128):
                cols = slice(col, min(col + 128, width))
                grads = [ref[at, cols].astype(F32) for ref in grad_refs]
                for e in range(count):
                    total = scales[0][e] * grads[0]
                    for k in range(1, systems):
                        total = total + scales[k][e] * grads[k]
                    held_ref[e, at, cols] = total

        at = pl.ds(lo, size)
        copies.append(pltpu.make_async_copy(held_ref.at[:, at, :], out_ref.at[:, at, :], sems.at[h]))
        copies[-1].start()
    for copy in copies:
        copy.wait()


def expert_grads(place, coef, grads, shape, parts):
    return pl.pallas_call(
        functools.partial(expert_kernel, parts),
        out_shape=jax.ShapeDtypeStruct(shape, F32),
        in_specs=[whole_smem(), whole_smem()] + [whole_vmem()] * len(grads),
        out_specs=in_hbm(),
        scratch_shapes=[pltpu.VMEM(shape, F32), pltpu.SemaphoreType.DMA((len(parts),))],
        compiler_params=params(SMALL),
        name="expert_grads",
    )(place, coef, *grads)


def hot_kernel(cols_ref, rows_ref, across_ref, down_ref, _, gather_ref, sum_ref, token_ref):
    atoms = down_ref.shape[0]

    def hot(same):
        return jnp.where(same, 1.0, 0.0).astype(BF16)

    for i in range(2):
        at = slice(i * atoms, (i + 1) * atoms)
        gather_ref[:, at] = hot(cols_ref[:, i : i + 1] == across_ref[...])
        sum_ref[at, :] = hot(down_ref[...] == rows_ref[i : i + 1, :])
    token_ref[...] = jnp.zeros_like(token_ref)


def hot_ends(cols, rows, order, earlier, width, tile):
    edges, atoms = cols.shape[0], order.shape[0]
    fixed = lambda *shape: pl.BlockSpec(shape, lambda i: (0, 0))
    return pl.pallas_call(
        hot_kernel,
        grid=(edges // tile,),
        out_shape=[
            jax.ShapeDtypeStruct((edges, 2 * atoms), BF16),
            jax.ShapeDtypeStruct((2 * atoms, edges), BF16),
            jax.ShapeDtypeStruct((1, width), F32),
        ],
        in_specs=[
            pl.BlockSpec((tile, 2), lambda i: (i, 0)),
            pl.BlockSpec((2, tile), lambda i: (0, i)),
            fixed(1, atoms),
            fixed(atoms, 1),
            in_hbm(),
        ],
        out_specs=[
            pl.BlockSpec((tile, 2 * atoms), lambda i: (i, 0)),
            pl.BlockSpec((2 * atoms, tile), lambda i: (0, i)),
            fixed(1, width),
        ],
        compiler_params=params(),
        cost_estimate=pl.CostEstimate(
            flops=16 * edges * atoms, bytes_accessed=8 * edges * atoms, transcendentals=0
        ),
        name="hot_ends",
    )(cols, rows, order[None, :], order[:, None], earlier)


def scale_kernel(slots, place_ref, gather_ref, radial_ref, _, *refs):
    block_refs = refs[:slots]
    atoms_out, scaled_ref, token_ref, atoms_ref, cot_ref, sems = refs[slots:]
    step = pl.program_id(0)
    own = block_refs[0].shape[1]
    store = pltpu.make_async_copy(atoms_ref, atoms_out, sems.at[2 * slots])

    @pl.when(step == 0)
    def _():
        loads = []
        chips = slots // 2
        for k, ref in enumerate(block_refs):
            back = lax.rem(place_ref[1] - k % chips + chips, chips)
            at = pl.ds(pl.multiple_of((k // chips * chips + back) * own, own), own)
            for i, to in enumerate((atoms_ref, cot_ref)):
                loads.append(pltpu.make_async_copy(ref.at[i], to.at[at], sems.at[2 * k + i]))
                loads[-1].start()
        for load in loads:
            load.wait()
        store.start()

    cot = jnp.dot(gather_ref[...], cot_ref[...], preferred_element_type=F32)
    scaled_ref[...] = (cot * radial_ref[...].astype(F32)).astype(BF16)
    token_ref[...] = jnp.zeros_like(token_ref)

    @pl.when(step == pl.num_programs(0) - 1)
    def _():
        store.wait()


def scaled_edges(place, hot_gather, radial, earlier, blocks, tile):
    edges, width = radial.shape
    atoms = hot_gather.shape[1] // 2
    slots = len(blocks)
    return pl.pallas_call(
        functools.partial(scale_kernel, slots),
        grid=(edges // tile,),
        out_shape=[
            jax.ShapeDtypeStruct((atoms, width), BF16),
            jax.ShapeDtypeStruct((edges, width), BF16),
            jax.ShapeDtypeStruct((1, width), BF16),
        ],
        in_specs=[
            whole_smem(),
            pl.BlockSpec((tile, atoms), lambda i: (i, 1)),
            pl.BlockSpec((tile, width), lambda i: (i, 0)),
        ]
        + [in_hbm()] * (1 + slots),
        out_specs=[
            in_hbm(),
            pl.BlockSpec((tile, width), lambda i: (i, 0)),
            pl.BlockSpec((1, width), lambda i: (0, 0)),
        ],
        scratch_shapes=[
            pltpu.VMEM((atoms, width), BF16),
            pltpu.VMEM((atoms, width), BF16),
            pltpu.SemaphoreType.DMA((2 * slots + 1,)),
        ],
        compiler_params=params(),
        cost_estimate=pl.CostEstimate(
            flops=2 * atoms * width * edges, bytes_accessed=6 * edges * width, transcendentals=0
        ),
        name="scaled_edges",
    )(place, hot_gather, radial, earlier, *blocks)


def edge_kernel(
    chips, place_ref, gather_ref, sum_ref, radial_ref, scaled_ref, atoms_hbm, *refs
):
    blocks = 2 * chips
    block_refs = refs[:blocks]
    kept_ref, sent_ref, node_kept_ref, node_sent_ref, weight_out = refs[blocks : blocks + 5]
    atoms_ref, weight_ref, proj_ref, value_ref, acc_ref, sem, sems = refs[blocks + 5 :]
    step, last = pl.program_id(0), pl.num_programs(0) - 1
    atoms, width_in = atoms_ref.shape
    width = radial_ref.shape[1]
    store = pltpu.make_async_copy(weight_ref, weight_out, sem)

    def messages():
        pre = jnp.dot(gather_ref[...], proj_ref[...], preferred_element_type=F32)
        sigma = 0.5 + 0.5 * jnp.tanh(0.5 * pre)
        silu = pre * sigma
        slope = sigma + silu * (1.0 - sigma)
        to = lax.rem(step, 2)
        value_ref[to, :, :width] = (scaled_ref[...].astype(F32) * slope).astype(BF16)
        value_ref[to, :, width:] = (silu * radial_ref[...].astype(F32)).astype(BF16)

    def add_up():
        at = lax.rem(step + 1, 2)
        acc_ref[:, :width] += jnp.dot(
            sum_ref[:atoms, :], value_ref[at, :, :width], preferred_element_type=F32
        )
        acc_ref[:, width:] += jnp.dot(
            sum_ref[atoms:, :], value_ref[at], preferred_element_type=F32
        )

    @pl.when(step == 0)
    def _():
        chip, core = place_ref[1], place_ref[2]
        depth = block_refs[0].shape[0]
        loads = [pltpu.make_async_copy(atoms_hbm, atoms_ref, sems.at[blocks])]
        for i, ref in enumerate(block_refs):
            source = lax.rem(chip - i // 2 + chips, chips)
            device = 2 * source + (1 - core if i % 2 else core)
            at = pl.ds(pl.multiple_of(device * depth, STEP), depth)
            loads.append(pltpu.make_async_copy(ref, weight_ref.at[at], sems.at[i]))
        for load in loads:
            load.start()
        acc_ref[...] = jnp.zeros_like(acc_ref)
        for load in loads:
            load.wait()
        store.start()
        for half in range(2):
            proj_ref[half * atoms : (half + 1) * atoms, :] = jnp.dot(
                atoms_ref[...],
                weight_ref[half * width_in : (half + 1) * width_in, :],
                preferred_element_type=F32,
            ).astype(BF16)
        messages()

    @pl.when(jnp.logical_and(step > 0, step < last))
    def _():
        add_up()
        messages()

    @pl.when(step == last)
    def _():
        add_up()
        side = atoms // 2
        for k in range(chips):
            chip = lax.rem(place_ref[1] + k, chips)
            cols = pl.ds(pl.multiple_of(chip // (chips // 2) * width, width), width)
            size = kept_ref.shape[1]
            row = lax.rem(chip, chips // 2) * size
            kept_ref[k] = acc_ref[pl.ds(pl.multiple_of(row, size), size), cols]
            sent_ref[k] = acc_ref[pl.ds(pl.multiple_of(side + row, size), size), cols].astype(BF16)
            cols = slice(2 * width, 3 * width)
            size = node_kept_ref.shape[1]
            row = chip * size
            node_kept_ref[k] = acc_ref[pl.ds(pl.multiple_of(row, size), size), cols]
            node_sent_ref[k] = acc_ref[pl.ds(pl.multiple_of(side + row, size), size), cols].astype(
                BF16
            )
        store.wait()


def edge_sums(chips, place, gather, sums, radial, scaled, atoms, blocks, tile):
    edges, width = radial.shape
    count, width_in = atoms.shape
    flops = 2 * count * width * (2 * width_in + 5 * edges)
    fixed = lambda *shape: pl.BlockSpec(shape, lambda i: (0,) * len(shape))
    sums_shape = (chips, count // chips, width)
    node_shape = (chips, count // 2 // chips, width)
    halves = [(sums_shape, F32), (sums_shape, BF16), (node_shape, F32), (node_shape, BF16)]
    outs = halves + [((2 * width_in, width), BF16)]
    steps = edges // tile
    return pl.pallas_call(
        functools.partial(edge_kernel, chips),
        grid=(steps + 1,),
        out_shape=[jax.ShapeDtypeStruct(shape, kind) for shape, kind in outs],
        in_specs=[
            whole_smem(),
            pl.BlockSpec((tile, 2 * count), lambda i: (jnp.minimum(i, steps - 1), 0)),
            pl.BlockSpec((2 * count, tile), lambda i: (0, jnp.maximum(i - 1, 0))),
            pl.BlockSpec((tile, width), lambda i: (jnp.minimum(i, steps - 1), 0)),
            pl.BlockSpec((tile, width), lambda i: (jnp.minimum(i, steps - 1), 0)),
        ]
        + [in_hbm()] * (1 + len(blocks)),
        out_specs=[fixed(*shape) for shape, _ in halves] + [in_hbm()],
        scratch_shapes=[
            pltpu.VMEM((count, width_in), BF16),
            pltpu.VMEM((2 * width_in, width), BF16),
            pltpu.VMEM((2 * count, width), BF16),
            pltpu.VMEM((2, tile, 2 * width), BF16),
            pltpu.VMEM((count, 3 * width), F32),
            pltpu.SemaphoreType.DMA,
            pltpu.SemaphoreType.DMA((len(blocks) + 1,)),
        ],
        compiler_params=params(),
        cost_estimate=pl.CostEstimate(
            flops=flops,
            bytes_accessed=4 * edges * width + 8 * edges * count,
            transcendentals=edges * width,
        ),
        name="edge_sums",
    )(place, gather, sums, radial, scaled, atoms, *blocks)


def shards(systems, ways, atoms, cotangent, experts, radial, coef, source, target):
    chips = ways // 2
    me_sys = lax.axis_index("sys")
    me_edge = lax.axis_index("edge")
    chip, core = me_edge // 2, me_edge % 2
    place = jnp.stack([me_sys, chip, core]).astype(jnp.int32)
    _, depth, width = experts.shape
    own = atoms.shape[1]
    tile = min(512, radial.shape[1])
    parts = row_parts(depth)

    def across(x, k):
        return lax.ppermute(x, "sys", [(s, s ^ k) for s in range(systems)])

    def swap(x):
        return lax.ppermute(x, "edge", [(e, e ^ 1) for e in range(ways)])

    def shift(x, k):
        return lax.ppermute(x, "edge", [(e, (e + 2 * k) % ways) for e in range(ways)])

    def both_cores(blocks):
        return blocks + [swap(block) for block in blocks]

    pair = join(atoms, cotangent)
    merged = merge_parts(place, coef, experts, pair, parts)
    features = both_cores([pair] + [shift(pair, k) for k in range(1, chips)])

    at = jnp.arange(ways * own, dtype=jnp.int32)
    side, z, offset = at // (chips * own), at // own % chips, at % own
    order = (2 * z + (core ^ side)) * own + offset
    ends = jnp.concatenate([source, target])
    hot_gather, hot_sum, hot_token = hot_ends(ends.T, ends, order, pair, width, tile)
    own_cols = jnp.concatenate([block[0] for block in features], axis=0)
    own_cols = lax.dynamic_slice_in_dim(own_cols, (me_edge % chips) * depth, depth, 1).T
    all_atoms, scaled, scaled_token = scaled_edges(
        place, hot_gather, radial[0], own_cols, features, tile
    )

    got = [merged[0]] + [across(merged[k], k) for k in range(1, systems)]
    held = weight_rows(got, features[1:chips] + [hot_token])
    blocks = []
    for k in range(chips):
        if k == chips - 1:
            held = held + scaled_token
        if k:
            held = shift(held, 1)
        blocks += [held, swap(held)]

    kept, sent, node_kept, node_sent, weight = edge_sums(
        chips, place, hot_gather, hot_sum, radial[0], scaled, all_atoms, blocks, tile
    )

    def terms_of(kept, other):
        terms = [kept[k] + other[k].astype(F32) for k in range(chips)]
        return terms[0], [term.astype(BF16) for term in terms[1:]]

    def reduce(total, terms):
        for k, term in enumerate(terms, 1):
            total = total + shift(term, k).astype(F32)
        return total.astype(BF16)

    shares = chips // 2
    sums = reduce(*terms_of(kept, swap(sent)))
    node, node_terms = terms_of(node_kept, swap(node_sent))

    def share(x, j):
        to = [z // shares * shares + (z + j) % shares for z in range(chips)]
        return lax.ppermute(x, "edge", [(2 * z + c, 2 * to[z] + c) for z in range(chips) for c in range(2)])

    *terms, term_token = atom_grads(chips, place, sums, weight)
    picked = both_cores([sums] + [share(sums, j) + term_token for j in range(1, shares)])
    grad, send, *passed = merged_grads(place, own_cols, picked, terms + node_terms)
    terms, node_terms = passed[: len(terms)], passed[len(terms) :]
    grads = [grad] + [across(send, k) for k in range(1, systems)]
    expert_grad = expert_grads(place, coef, grads, experts.shape, parts)

    atom_grad = 0.0
    for flip, term in enumerate(terms):
        to = [2 * (z % shares) + (z // shares ^ flip) for z in range(chips)]
        pairs = [(2 * z + c, 2 * to[z] + c) for z in range(chips) for c in range(2)]
        atom_grad = atom_grad + lax.ppermute(term, "edge", pairs).astype(F32)

    return reduce(node, node_terms)[None], atom_grad[None], expert_grad


def solution(mesh):
    placed = P("sys", "edge", None)
    return jax.shard_map(
        functools.partial(shards, mesh.shape["sys"], mesh.shape["edge"]),
        mesh=mesh,
        in_specs=(placed, placed, placed, placed, P(), P("sys", "edge"), P("sys", "edge")),
        out_specs=(placed, placed, placed),
        check_vma=False,
    )
```

```python
import functools

import jax
import jax.numpy as jnp
from jax import lax
from jax.experimental import pallas as pl
from jax.experimental.pallas import tpu as pltpu
from jax.sharding import PartitionSpec as P

F32 = jnp.float32
BF16 = jnp.bfloat16
LARGE = 60 << 20
SMALL = 24 << 20
STEP = 16


def whole_vmem():
    return pl.BlockSpec(memory_space=pltpu.VMEM)


def in_hbm():
    return pl.BlockSpec(memory_space=pltpu.HBM)


def whole_smem():
    return pl.BlockSpec(memory_space=pltpu.SMEM)


def params(limit=LARGE):
    return pltpu.CompilerParams(vmem_limit_bytes=limit)


def row_parts(depth):
    first = -(-depth // (2 * STEP)) * STEP
    return [(0, first), (first, depth - first)]


def merge_kernel(parts, place_ref, coef_ref, experts_ref, _, *refs):
    part_refs, held_ref, sems = refs[:-2], refs[-2], refs[-1]
    systems, count = coef_ref.shape[0], experts_ref.shape[0]
    width = experts_ref.shape[2]
    me = place_ref[0]
    loads = []
    for h, (lo, size) in enumerate(parts):
        at = pl.ds(lo, size)
        loads.append(
            pltpu.make_async_copy(experts_ref.at[:, at, :], held_ref.at[:, at, :], sems.at[h])
        )
        loads[-1].start()
    scales = [[coef_ref[me ^ k, me * count + e] for e in range(count)] for k in range(systems)]
    for h, (lo, size) in enumerate(parts):
        loads[h].wait()

        @pl.loop(0, size // STEP)
        def _(i):
            at = pl.ds(pl.multiple_of(lo + i * STEP, STEP), STEP)
            for col in range(0, width, 128):
                cols = slice(col, min(col + 128, width))
                loaded = [held_ref[e, at, cols].astype(F32) for e in range(count)]
                for k in range(systems):
                    total = scales[k][0] * loaded[0]
                    for e in range(1, count):
                        total = total + scales[k][e] * loaded[e]
                    part_refs[k][at, cols] = total.astype(part_refs[k].dtype)


def merge_parts(place, coef, experts, earlier, parts):
    _, depth, width = experts.shape
    systems = coef.shape[0]
    return pl.pallas_call(
        functools.partial(merge_kernel, parts),
        out_shape=[
            jax.ShapeDtypeStruct((depth, width), BF16 if k else F32) for k in range(systems)
        ],
        in_specs=[whole_smem(), whole_smem(), in_hbm(), in_hbm()],
        out_specs=[whole_vmem()] * systems,
        scratch_shapes=[
            pltpu.VMEM(experts.shape, BF16),
            pltpu.SemaphoreType.DMA((len(parts),)),
        ],
        compiler_params=params(),
        name="merge_parts",
    )(place, coef, experts, earlier)


def join_kernel(atoms_ref, cot_ref, both_ref, sems):
    loads = [
        pltpu.make_async_copy(ref.at[0], both_ref.at[i], sems.at[i])
        for i, ref in enumerate((atoms_ref, cot_ref))
    ]
    for load in loads:
        load.start()
    for load in loads:
        load.wait()


def join(atoms, cotangent):
    return pl.pallas_call(
        join_kernel,
        out_shape=jax.ShapeDtypeStruct((2, *atoms.shape[1:]), BF16),
        in_specs=[in_hbm(), in_hbm()],
        out_specs=whole_vmem(),
        scratch_shapes=[pltpu.SemaphoreType.DMA((2,))],
        compiler_params=params(),
        name="join",
    )(atoms, cotangent)


def rows_kernel(count, *refs):
    out_ref = refs[-1]
    total = refs[0][...]
    for ref in refs[1:count]:
        total = total + ref[...].astype(F32)
    out_ref[...] = total.astype(BF16)


def weight_rows(parts, earlier):
    return pl.pallas_call(
        functools.partial(rows_kernel, len(parts)),
        out_shape=jax.ShapeDtypeStruct(parts[0].shape, BF16),
        in_specs=[whole_vmem()] * len(parts) + [in_hbm()] * len(earlier),
        out_specs=whole_vmem(),
        compiler_params=params(SMALL),
        name="weight_rows",
    )(*parts, *earlier)


def merged_grad_kernel(through, place_ref, cols_ref, *refs):
    grad_ref, sent_ref, sums_ref = refs[-through - 3], refs[-through - 2], refs[-1]
    block_refs = refs[: -2 * through - 3]
    size = block_refs[0].shape[0]
    pieces = len(block_refs) // 2
    for i, ref in enumerate(block_refs):
        piece = lax.rem(place_ref[1] + pieces - i % pieces, pieces)
        at = pl.ds(pl.multiple_of((i // pieces * pieces + piece) * size, size), size)
        sums_ref[at, :] = ref[...]
    grad = jnp.dot(cols_ref[...], sums_ref[...], preferred_element_type=F32)
    grad_ref[...] = grad
    sent_ref[...] = grad.astype(BF16)
    for i in range(through):
        refs[len(block_refs) + through + 2 + i][...] = refs[len(block_refs) + i][...]


def merged_grads(place, cols, blocks, others):
    size, width = blocks[0].shape
    return pl.pallas_call(
        functools.partial(merged_grad_kernel, len(others)),
        out_shape=[jax.ShapeDtypeStruct((cols.shape[0], width), kind) for kind in (F32, BF16)]
        + [jax.ShapeDtypeStruct(other.shape, other.dtype) for other in others],
        in_specs=[whole_smem()] + [whole_vmem()] * (1 + len(blocks) + len(others)),
        out_specs=[whole_vmem()] * (2 + len(others)),
        scratch_shapes=[pltpu.VMEM((size * len(blocks), width), BF16)],
        compiler_params=params(SMALL),
        name="merged_grads",
    )(place, cols, *blocks, *others)


def atom_grad_kernel(
    chips, place_ref, sums_ref, weight_hbm, first_ref, second_ref, token_ref, weight_ref, sem
):
    half = place_ref[1] // (chips // 2)
    rows, own = weight_ref.shape[0], first_ref.shape[0]
    at = pl.ds(pl.multiple_of(half * rows, rows), rows)
    load = pltpu.make_async_copy(weight_hbm.at[at], weight_ref, sem)
    load.start()
    load.wait()
    for side, ref in ((half, first_ref), (1 - half, second_ref)):
        block = sums_ref[pl.ds(pl.multiple_of(side * own, own), own), :]
        ref[...] = lax.dot_general(
            block, weight_ref[...], (((1,), (1,)), ((), ())), preferred_element_type=F32
        ).astype(BF16)
    token_ref[...] = jnp.zeros_like(token_ref)


def atom_grads(chips, place, sums, weight):
    own, width = sums.shape[0] // 2, sums.shape[1]
    rows = weight.shape[0] // 2
    return pl.pallas_call(
        functools.partial(atom_grad_kernel, chips),
        out_shape=[jax.ShapeDtypeStruct((own, rows), BF16)] * 2
        + [jax.ShapeDtypeStruct((1, width), BF16)],
        in_specs=[whole_smem(), whole_vmem(), in_hbm()],
        out_specs=[whole_vmem()] * 3,
        scratch_shapes=[pltpu.VMEM((rows, width), BF16), pltpu.SemaphoreType.DMA],
        compiler_params=params(SMALL),
        cost_estimate=pl.CostEstimate(
            flops=4 * own * rows * width, bytes_accessed=2 * rows * width, transcendentals=0
        ),
        name="atom_grads",
    )(place, sums, weight)


def expert_kernel(parts, place_ref, coef_ref, *refs):
    grad_refs, out_ref, held_ref, sems = refs[:-3], refs[-3], refs[-2], refs[-1]
    me = place_ref[0]
    count, _, width = out_ref.shape
    systems = coef_ref.shape[0]
    copies = []
    scales = [[coef_ref[me ^ k, me * count + e] for e in range(count)] for k in range(systems)]
    for h, (lo, size) in enumerate(parts):

        @pl.loop(0, size // STEP)
        def _(i):
            at = pl.ds(pl.multiple_of(lo + i * STEP, STEP), STEP)
            for col in range(0, width, 128):
                cols = slice(col, min(col + 128, width))
                grads = [ref[at, cols].astype(F32) for ref in grad_refs]
                for e in range(count):
                    total = scales[0][e] * grads[0]
                    for k in range(1, systems):
                        total = total + scales[k][e] * grads[k]
                    held_ref[e, at, cols] = total

        at = pl.ds(lo, size)
        copies.append(pltpu.make_async_copy(held_ref.at[:, at, :], out_ref.at[:, at, :], sems.at[h]))
        copies[-1].start()
    for copy in copies:
        copy.wait()


def expert_grads(place, coef, grads, shape, parts):
    return pl.pallas_call(
        functools.partial(expert_kernel, parts),
        out_shape=jax.ShapeDtypeStruct(shape, F32),
        in_specs=[whole_smem(), whole_smem()] + [whole_vmem()] * len(grads),
        out_specs=in_hbm(),
        scratch_shapes=[pltpu.VMEM(shape, F32), pltpu.SemaphoreType.DMA((len(parts),))],
        compiler_params=params(SMALL),
        name="expert_grads",
    )(place, coef, *grads)


def hot_kernel(cols_ref, rows_ref, across_ref, down_ref, _, gather_ref, sum_ref, token_ref):
    atoms = down_ref.shape[0]

    def hot(same):
        return jnp.where(same, 1.0, 0.0).astype(BF16)

    for i in range(2):
        at = slice(i * atoms, (i + 1) * atoms)
        gather_ref[:, at] = hot(cols_ref[:, i : i + 1] == across_ref[...])
        sum_ref[at, :] = hot(down_ref[...] == rows_ref[i : i + 1, :])
    token_ref[...] = jnp.zeros_like(token_ref)


def hot_ends(cols, rows, order, earlier, width, tile):
    edges, atoms = cols.shape[0], order.shape[0]
    fixed = lambda *shape: pl.BlockSpec(shape, lambda i: (0, 0))
    return pl.pallas_call(
        hot_kernel,
        grid=(edges // tile,),
        out_shape=[
            jax.ShapeDtypeStruct((edges, 2 * atoms), BF16),
            jax.ShapeDtypeStruct((2 * atoms, edges), BF16),
            jax.ShapeDtypeStruct((1, width), F32),
        ],
        in_specs=[
            pl.BlockSpec((tile, 2), lambda i: (i, 0)),
            pl.BlockSpec((2, tile), lambda i: (0, i)),
            fixed(1, atoms),
            fixed(atoms, 1),
            in_hbm(),
        ],
        out_specs=[
            pl.BlockSpec((tile, 2 * atoms), lambda i: (i, 0)),
            pl.BlockSpec((2 * atoms, tile), lambda i: (0, i)),
            fixed(1, width),
        ],
        compiler_params=params(),
        cost_estimate=pl.CostEstimate(
            flops=16 * edges * atoms, bytes_accessed=8 * edges * atoms, transcendentals=0
        ),
        name="hot_ends",
    )(cols, rows, order[None, :], order[:, None], earlier)


def scale_kernel(slots, place_ref, gather_ref, radial_ref, *refs):
    block_refs = refs[:slots]
    atoms_out, scaled_ref, token_ref, cols_ref, atoms_ref, cot_ref, sems = refs[slots:]
    step = pl.program_id(0)
    own = block_refs[0].shape[1]
    store = pltpu.make_async_copy(atoms_ref, atoms_out, sems.at[2 * slots])

    @pl.when(step == 0)
    def _():
        loads = []
        chips = slots // 2
        for k, ref in enumerate(block_refs):
            back = lax.rem(place_ref[1] - k % chips + chips, chips)
            at = pl.ds(pl.multiple_of((k // chips * chips + back) * own, own), own)
            for i, to in enumerate((atoms_ref, cot_ref)):
                loads.append(pltpu.make_async_copy(ref.at[i], to.at[at], sems.at[2 * k + i]))
                loads[-1].start()
        for load in loads:
            load.wait()
        store.start()
        depth = cols_ref.shape[0]
        device = lax.rem(2 * place_ref[1] + place_ref[2], chips)
        for i in range(chips):

            @pl.when(device == i)
            def _():
                own_cols = atoms_ref[:, i * depth : (i + 1) * depth].astype(F32)
                cols_ref[...] = own_cols.T.astype(BF16)

    cot = jnp.dot(gather_ref[...], cot_ref[...], preferred_element_type=F32)
    scaled_ref[...] = (cot * radial_ref[...].astype(F32)).astype(BF16)
    token_ref[...] = jnp.zeros_like(token_ref)

    @pl.when(step == pl.num_programs(0) - 1)
    def _():
        store.wait()


def scaled_edges(place, hot_gather, radial, depth, blocks, tile):
    edges, width = radial.shape
    atoms = hot_gather.shape[1] // 2
    slots = len(blocks)
    return pl.pallas_call(
        functools.partial(scale_kernel, slots),
        grid=(edges // tile,),
        out_shape=[
            jax.ShapeDtypeStruct((atoms, width), BF16),
            jax.ShapeDtypeStruct((edges, width), BF16),
            jax.ShapeDtypeStruct((1, width), BF16),
            jax.ShapeDtypeStruct((depth, atoms), BF16),
        ],
        in_specs=[
            whole_smem(),
            pl.BlockSpec((tile, atoms), lambda i: (i, 1)),
            pl.BlockSpec((tile, width), lambda i: (i, 0)),
        ]
        + [in_hbm()] * slots,
        out_specs=[
            in_hbm(),
            pl.BlockSpec((tile, width), lambda i: (i, 0)),
            pl.BlockSpec((1, width), lambda i: (0, 0)),
            pl.BlockSpec((depth, atoms), lambda i: (0, 0)),
        ],
        scratch_shapes=[
            pltpu.VMEM((atoms, width), BF16),
            pltpu.VMEM((atoms, width), BF16),
            pltpu.SemaphoreType.DMA((2 * slots + 1,)),
        ],
        compiler_params=params(),
        cost_estimate=pl.CostEstimate(
            flops=2 * atoms * width * edges, bytes_accessed=6 * edges * width, transcendentals=0
        ),
        name="scaled_edges",
    )(place, hot_gather, radial, *blocks)


def edge_kernel(
    chips, place_ref, gather_ref, sum_ref, radial_ref, scaled_ref, atoms_hbm, *refs
):
    blocks = 2 * chips
    block_refs = refs[:blocks]
    kept_ref, sent_ref, node_kept_ref, node_sent_ref, weight_out = refs[blocks : blocks + 5]
    atoms_ref, weight_ref, proj_ref, value_ref, acc_ref, sem, sems = refs[blocks + 5 :]
    step, last = pl.program_id(0), pl.num_programs(0) - 1
    atoms, width_in = atoms_ref.shape
    width = radial_ref.shape[1]
    store = pltpu.make_async_copy(weight_ref, weight_out, sem)

    def messages():
        pre = jnp.dot(gather_ref[...], proj_ref[...], preferred_element_type=F32)
        sigma = 0.5 + 0.5 * jnp.tanh(0.5 * pre)
        silu = pre * sigma
        slope = sigma + silu * (1.0 - sigma)
        to = lax.rem(step, 2)
        value_ref[to, :, :width] = (scaled_ref[...].astype(F32) * slope).astype(BF16)
        value_ref[to, :, width:] = (silu * radial_ref[...].astype(F32)).astype(BF16)

    def add_up():
        at = lax.rem(step + 1, 2)
        acc_ref[:, :width] += jnp.dot(
            sum_ref[:atoms, :], value_ref[at, :, :width], preferred_element_type=F32
        )
        acc_ref[:, width:] += jnp.dot(
            sum_ref[atoms:, :], value_ref[at], preferred_element_type=F32
        )

    @pl.when(step == 0)
    def _():
        chip, core = place_ref[1], place_ref[2]
        depth = block_refs[0].shape[0]
        loads = [pltpu.make_async_copy(atoms_hbm, atoms_ref, sems.at[blocks])]
        for i, ref in enumerate(block_refs):
            source = lax.rem(chip - i // 2 + chips, chips)
            device = 2 * source + (1 - core if i % 2 else core)
            at = pl.ds(pl.multiple_of(device * depth, STEP), depth)
            loads.append(pltpu.make_async_copy(ref, weight_ref.at[at], sems.at[i]))
        for load in loads:
            load.start()
        acc_ref[...] = jnp.zeros_like(acc_ref)
        for load in loads:
            load.wait()
        store.start()
        for half in range(2):
            proj_ref[half * atoms : (half + 1) * atoms, :] = jnp.dot(
                atoms_ref[...],
                weight_ref[half * width_in : (half + 1) * width_in, :],
                preferred_element_type=F32,
            ).astype(BF16)
        messages()

    @pl.when(jnp.logical_and(step > 0, step < last))
    def _():
        add_up()
        messages()

    @pl.when(step == last)
    def _():
        add_up()
        side = atoms // 2
        for k in range(chips):
            chip = lax.rem(place_ref[1] + k, chips)
            cols = pl.ds(pl.multiple_of(chip // (chips // 2) * width, width), width)
            size = kept_ref.shape[1]
            row = lax.rem(chip, chips // 2) * size
            kept_ref[k] = acc_ref[pl.ds(pl.multiple_of(row, size), size), cols]
            sent_ref[k] = acc_ref[pl.ds(pl.multiple_of(side + row, size), size), cols].astype(BF16)
            cols = slice(2 * width, 3 * width)
            size = node_kept_ref.shape[1]
            row = chip * size
            node_kept_ref[k] = acc_ref[pl.ds(pl.multiple_of(row, size), size), cols]
            node_sent_ref[k] = acc_ref[pl.ds(pl.multiple_of(side + row, size), size), cols].astype(
                BF16
            )
        store.wait()


def edge_sums(chips, place, gather, sums, radial, scaled, atoms, blocks, tile):
    edges, width = radial.shape
    count, width_in = atoms.shape
    flops = 2 * count * width * (2 * width_in + 5 * edges)
    fixed = lambda *shape: pl.BlockSpec(shape, lambda i: (0,) * len(shape))
    sums_shape = (chips, count // chips, width)
    node_shape = (chips, count // 2 // chips, width)
    halves = [(sums_shape, F32), (sums_shape, BF16), (node_shape, F32), (node_shape, BF16)]
    outs = halves + [((2 * width_in, width), BF16)]
    steps = edges // tile
    return pl.pallas_call(
        functools.partial(edge_kernel, chips),
        grid=(steps + 1,),
        out_shape=[jax.ShapeDtypeStruct(shape, kind) for shape, kind in outs],
        in_specs=[
            whole_smem(),
            pl.BlockSpec((tile, 2 * count), lambda i: (jnp.minimum(i, steps - 1), 0)),
            pl.BlockSpec((2 * count, tile), lambda i: (0, jnp.maximum(i - 1, 0))),
            pl.BlockSpec((tile, width), lambda i: (jnp.minimum(i, steps - 1), 0)),
            pl.BlockSpec((tile, width), lambda i: (jnp.minimum(i, steps - 1), 0)),
        ]
        + [in_hbm()] * (1 + len(blocks)),
        out_specs=[fixed(*shape) for shape, _ in halves] + [in_hbm()],
        scratch_shapes=[
            pltpu.VMEM((count, width_in), BF16),
            pltpu.VMEM((2 * width_in, width), BF16),
            pltpu.VMEM((2 * count, width), BF16),
            pltpu.VMEM((2, tile, 2 * width), BF16),
            pltpu.VMEM((count, 3 * width), F32),
            pltpu.SemaphoreType.DMA,
            pltpu.SemaphoreType.DMA((len(blocks) + 1,)),
        ],
        compiler_params=params(),
        cost_estimate=pl.CostEstimate(
            flops=flops,
            bytes_accessed=4 * edges * width + 8 * edges * count,
            transcendentals=edges * width,
        ),
        name="edge_sums",
    )(place, gather, sums, radial, scaled, atoms, *blocks)


def shards(systems, ways, atoms, cotangent, experts, radial, coef, source, target):
    chips = ways // 2
    me_sys = lax.axis_index("sys")
    me_edge = lax.axis_index("edge")
    chip, core = me_edge // 2, me_edge % 2
    place = jnp.stack([me_sys, chip, core]).astype(jnp.int32)
    _, depth, width = experts.shape
    own = atoms.shape[1]
    tile = min(512, radial.shape[1])
    parts = row_parts(depth)

    def across(x, k):
        return lax.ppermute(x, "sys", [(s, s ^ k) for s in range(systems)])

    def swap(x):
        return lax.ppermute(x, "edge", [(e, e ^ 1) for e in range(ways)])

    def shift(x, k):
        return lax.ppermute(x, "edge", [(e, (e + 2 * k) % ways) for e in range(ways)])

    def both_cores(blocks):
        return blocks + [swap(block) for block in blocks]

    pair = join(atoms, cotangent)
    merged = merge_parts(place, coef, experts, pair, parts)
    features = both_cores([pair] + [shift(pair, k) for k in range(1, chips)])

    at = jnp.arange(ways * own, dtype=jnp.int32)
    side, z, offset = at // (chips * own), at // own % chips, at % own
    order = (2 * z + (core ^ side)) * own + offset
    ends = jnp.concatenate([source, target])
    hot_gather, hot_sum, hot_token = hot_ends(ends.T, ends, order, pair, width, tile)
    all_atoms, scaled, scaled_token, own_cols = scaled_edges(
        place, hot_gather, radial[0], depth, features, tile
    )

    got = [merged[0]] + [across(merged[k], k) for k in range(1, systems)]
    held = weight_rows(got, features[1:chips] + [hot_token])
    blocks = []
    for k in range(chips):
        if k == chips - 1:
            held = held + scaled_token
        if k:
            held = shift(held, 1)
        blocks += [held, swap(held)]

    kept, sent, node_kept, node_sent, weight = edge_sums(
        chips, place, hot_gather, hot_sum, radial[0], scaled, all_atoms, blocks, tile
    )

    def terms_of(kept, other):
        terms = [kept[k] + other[k].astype(F32) for k in range(chips)]
        return terms[0], [term.astype(BF16) for term in terms[1:]]

    def reduce(total, terms):
        for k, term in enumerate(terms, 1):
            total = total + shift(term, k).astype(F32)
        return total.astype(BF16)

    shares = chips // 2
    sums = reduce(*terms_of(kept, swap(sent)))
    node, node_terms = terms_of(node_kept, swap(node_sent))

    def share(x, j):
        to = [z // shares * shares + (z + j) % shares for z in range(chips)]
        return lax.ppermute(x, "edge", [(2 * z + c, 2 * to[z] + c) for z in range(chips) for c in range(2)])

    *terms, term_token = atom_grads(chips, place, sums, weight)
    picked = both_cores([sums] + [share(sums, j) + term_token for j in range(1, shares)])
    grad, send, *node_terms = merged_grads(place, own_cols, picked, node_terms)
    grads = [grad] + [across(send, k) for k in range(1, systems)]
    expert_grad = expert_grads(place, coef, grads, experts.shape, parts)

    atom_grad = 0.0
    for flip, term in enumerate(terms):
        to = [2 * (z % shares) + (z // shares ^ flip) for z in range(chips)]
        pairs = [(2 * z + c, 2 * to[z] + c) for z in range(chips) for c in range(2)]
        atom_grad = atom_grad + lax.ppermute(term, "edge", pairs).astype(F32)

    return reduce(node, node_terms)[None], atom_grad[None], expert_grad


def solution(mesh):
    placed = P("sys", "edge", None)
    return jax.shard_map(
        functools.partial(shards, mesh.shape["sys"], mesh.shape["edge"]),
        mesh=mesh,
        in_specs=(placed, placed, placed, placed, P(), P("sys", "edge"), P("sys", "edge")),
        out_specs=(placed, placed, placed),
        check_vma=False,
    )
```
